32 devices in a mesh: rep: 4 (over z), shard: 8 (over y, x, core).
Axes of the slice: x: 2, y: 2, z: 4, core: 2. Of those that a mesh axis runs over, the one named last changes fastest.
Arguments:
- inputs: bfloat16 [8192, 1024], P(('rep', 'shard')), may hold values from -6 to 6
- cotangent: bfloat16 [8192, 1024], P(('rep', 'shard')), may hold values from -6 to 6
- segments: int32 [32, 256], P(('rep', 'shard')), may hold values from 0 to 7, never falling along the last dimension, each value on 1 to 128 neighbouring positions
- w_qkv: bfloat16 [2, 1024, 3072], P(None, 'shard'), may hold values from -0.1875 to 0.1875
- w_out: bfloat16 [2, 1024, 1024], P(None, 'shard'), may hold values from -1 to 1
- w_up: bfloat16 [2, 1024, 4096], P(None, 'shard'), may hold values from -0.1875 to 0.1875
- w_down: bfloat16 [2, 4096, 1024], P(None, 'shard'), may hold values from -0.09375 to 0.09375
- bias_query: bfloat16 [2, 1024], P(None, 'shard'), may hold values from -3 to 3
- bias_value: bfloat16 [2, 1024], P(None, 'shard'), may hold values from -3 to 3
- bias_out: bfloat16 [2, 1024], P(None, 'shard'), may hold values from -2 to 2
- bias_up: bfloat16 [2, 4096], P(None, 'shard'), may hold values from -3 to 3
- bias_down: bfloat16 [2, 1024], P(None, 'shard'), may hold values from -2 to 2
- norm1_gain: bfloat16 [2, 1024], P(None, 'shard'), may hold values from 0.5 to 1.5
- norm1_bias: bfloat16 [2, 1024], P(None, 'shard'), may hold values from -2 to 2
- norm2_gain: bfloat16 [2, 1024], P(None, 'shard'), may hold values from 0.5 to 1.5
- norm2_bias: bfloat16 [2, 1024], P(None, 'shard'), may hold values from -2 to 2
- tau: float32 [2, 16], replicated, may hold values from 3 to 12
Outputs:
- output: bfloat16 [8192, 1024], P(('rep', 'shard'))
- input_grad: float32 [8192, 1024], P(('rep', 'shard'))
- grad_w_qkv: float32 [2, 1024, 3072], P(None, 'shard')
- grad_w_out: float32 [2, 1024, 1024], P(None, 'shard')
- grad_w_up: float32 [2, 1024, 4096], P(None, 'shard')
- grad_w_down: float32 [2, 4096, 1024], P(None, 'shard')
- grad_bias_query: float32 [2, 1024], P(None, 'shard')
- grad_bias_value: float32 [2, 1024], P(None, 'shard')
- grad_bias_out: float32 [2, 1024], P(None, 'shard')
- grad_bias_up: float32 [2, 4096], P(None, 'shard')
- grad_bias_down: float32 [2, 1024], P(None, 'shard')
- grad_norm1_gain: float32 [2, 1024], P(None, 'shard')
- grad_norm1_bias: float32 [2, 1024], P(None, 'shard')
- grad_norm2_gain: float32 [2, 1024], P(None, 'shard')
- grad_norm2_bias: float32 [2, 1024], P(None, 'shard')
- clipped_qk: float32 [2, 1024, 2048], P(None, 'shard')
- clipped_bias_query: float32 [2, 1024], P(None, 'shard')
The draws below stay inside these ranges and needn't reach their ends.
Inputs may be any that keep to these rules, and one draw needn't show every extreme that they name: `segments`: segment numbers never fall along a sequence, so each document's tokens are consecutive.
All inputs are finite; a program needn't handle non-finite values.
Results may differ from the reference program's by a relative error of at most 0.019.
Values may be sent and summed in bfloat16 or wider, within the bound.
A program may use at most 256 MiB of HBM per device.

```python
import math
import jax
import jax.numpy as jnp
import numpy as np
from jax import lax

D = 1024
HEADS = 16
FF = 4096
LAYERS = 2
TOK_DEV = 256
SEQS = 32
TOKENS = 8192


def steps_of(key, shape, cuts, least, high):
    def one(axis_at, blocks):
        heights = jax.random.uniform(jax.random.fold_in(jax.random.fold_in(key, 6), axis_at), (blocks,), jnp.float32, least / len(cuts), high / len(cuts))
        return jnp.repeat(jnp.exp(heights), shape[axis_at] // blocks).reshape((-1,) + (1,) * (len(shape) - axis_at - 1))

    gain = one(*cuts[0])
    for cut in cuts[1:]:
        gain = gain * one(*cut)
    return gain


def split_up(amount, total, reach, lean):
    portions = [(1 << 20) // math.isqrt(standing ** lean) + 1 for standing in range(2, amount + 1)]
    rest, counts = total - reach - (amount - 1), [1] * (amount - 1)
    while rest > 0:
        free = [i for i in range(amount - 1) if counts[i] < reach]
        whole, left = sum([portions[i] for i in free]), rest
        for i in free:
            more = min(reach - counts[i], max(1, left * portions[i] // whole), rest)
            counts[i] = counts[i] + more
            rest = rest - more
    return np.array([reach] + counts)


def ragged_sizes(key, count, total, limit, skew):
    if count == 2:
        one = jax.random.randint(key, (), max(1, total - limit), min(limit, total - 1) + 1)
        return jnp.stack([one, total - one])
    sizes = jnp.asarray(split_up(count, total, limit, skew), jnp.int32)
    twos = (count - 1) // 2
    source_of, sink = sizes[1:1 + 2 * twos:2], sizes[2:2 + 2 * twos:2]
    slack = jnp.minimum(source_of - 1, limit - sink)
    shifted = jax.random.randint(jax.random.fold_in(key, 1), (twos,), 0, 1 << 20) % (slack + 1)
    sizes = sizes.at[1:1 + 2 * twos:2].set(source_of - shifted).at[2:2 + 2 * twos:2].set(sink + shifted)
    return sizes[jax.random.permutation(jax.random.fold_in(key, 2), count)]


def gaussian(rng, dims, deviation, most, split=(), dtype=jnp.bfloat16):
    entries = deviation * jax.random.normal(rng, dims, jnp.float32)
    if split:
        entries = entries * steps_of(rng, dims, split, -0.22, 0.18)
    return jnp.clip(entries, -most, most).astype(dtype)


def setup_inputs(seed: int = 0) -> dict:
    seeds = jax.random.split(jax.random.key(seed), 18)
    inputs = gaussian(seeds[0], (TOKENS, D), 1.0, 6.0, ((0, 32),))
    cotangent = gaussian(seeds[1], (TOKENS, D), 1.0, 6.0, ((0, 32),))
    segments = jax.vmap(lambda own: jnp.searchsorted(jnp.cumsum(ragged_sizes(own, max(4, TOK_DEV // 32), TOK_DEV, TOK_DEV // 2, 2)), jnp.arange(TOK_DEV), side="right"))(jax.random.split(seeds[2], SEQS)).reshape((SEQS, TOK_DEV)).astype(jnp.int32)
    w_qkv = gaussian(seeds[3], (LAYERS, D, 3 * D), D ** -0.5, 0.1875, ((1, 8),))
    w_out = gaussian(seeds[4], (LAYERS, D, D), 32 ** -0.5, 1.0, ((1, 8),))
    w_up = gaussian(seeds[5], (LAYERS, D, FF), D ** -0.5, 0.1875, ((1, 8),))
    w_down = gaussian(seeds[6], (LAYERS, FF, D), FF ** -0.5, 0.09375, ((1, 8),))
    bias_query = gaussian(seeds[7], (LAYERS, D), 0.5, 3.0, ((1, 8),))
    bias_value = gaussian(seeds[8], (LAYERS, D), 0.5, 3.0, ((1, 8),))
    bias_out = gaussian(seeds[9], (LAYERS, D), 0.3, 2.0, ((1, 8),))
    bias_up = gaussian(seeds[10], (LAYERS, FF), 0.5, 3.0, ((1, 8),))
    bias_down = gaussian(seeds[11], (LAYERS, D), 0.3, 2.0, ((1, 8),))
    norm1_gain = jnp.clip(1.0 + 0.1 * jax.random.normal(seeds[12], (LAYERS, D), jnp.float32), 0.5, 1.5).astype(jnp.bfloat16)
    norm1_bias = gaussian(seeds[13], (LAYERS, D), 0.3, 2.0, ((1, 8),))
    norm2_gain = jnp.clip(1.0 + 0.1 * jax.random.normal(seeds[14], (LAYERS, D), jnp.float32), 0.5, 1.5).astype(jnp.bfloat16)
    norm2_bias = gaussian(seeds[15], (LAYERS, D), 0.3, 2.0, ((1, 8),))
    tau = jnp.clip(jnp.exp(jax.random.uniform(seeds[16], (LAYERS, HEADS), jnp.float32, math.log(3.0), math.log(12.0))), 3.0, 12.0)
    return dict(inputs=inputs, cotangent=cotangent, segments=segments, w_qkv=w_qkv, w_out=w_out, w_up=w_up, w_down=w_down, bias_query=bias_query, bias_value=bias_value, bias_out=bias_out, bias_up=bias_up, bias_down=bias_down, norm1_gain=norm1_gain, norm1_bias=norm1_bias, norm2_gain=norm2_gain, norm2_bias=norm2_bias, tau=tau)


@jax.custom_vjp
def low(v):
    return lax.optimization_barrier(v.astype(jnp.bfloat16)).astype(jnp.float32)

@jax.custom_vjp
def low_back(v):
    return v

def low_keep(v):
    return (low(v), None)

def low_pass(kept, grad):
    return (grad,)

def back_keep(v):
    return (v, None)

def back_low(kept, grad):
    return (low(grad),)
low.defvjp(low_keep, low_pass)
low_back.defvjp(back_keep, back_low)
epsilon = 1e-05
neg_large = -1e+30
highest = lax.Precision.HIGHEST

def normalize(values):
    centred = values - lax.optimization_barrier(jnp.mean(values, axis=-1, keepdims=True))
    rstd = lax.rsqrt(lax.optimization_barrier(jnp.mean(centred * centred, axis=-1, keepdims=True)) + epsilon)
    return centred * rstd

def one_layer(hidden, seg_rows, params):
    w_qkv, w_out, w_up, w_down, bias_query, bias_value, bias_out, bias_up, bias_down, gain_first, shift_first, gain_second, shift_second = params
    seq_count, length = seg_rows.shape
    width = hidden.shape[1]
    head_dim = width // HEADS
    hidden_low = low(hidden)
    bias_row = jnp.concatenate([bias_query, jnp.zeros_like(bias_query), bias_value])
    qkv = low(low_back(jnp.dot(hidden_low, w_qkv, precision=highest) + bias_row))
    pieces = qkv.reshape(seq_count, length, 3, HEADS, head_dim)
    query = pieces[:, :, 0]
    key_rows = pieces[:, :, 1]
    value_rows = pieces[:, :, 2]
    scores = jnp.einsum('sqhd,skhd->shqk', query, key_rows, precision=highest) * (1.0 / math.sqrt(head_dim))
    scores = low_back(scores)
    same = seg_rows[:, :, None] == seg_rows[:, None, :]
    masked = jnp.where(same[:, None], scores, neg_large)
    top = lax.optimization_barrier(jnp.max(masked, axis=-1, keepdims=True))
    expo = jnp.exp(masked - top)
    probs = low(expo / lax.optimization_barrier(jnp.sum(expo, axis=-1, keepdims=True)))
    attended = jnp.einsum('shqk,skhd->sqhd', probs, value_rows, precision=highest)
    attended = low(low_back(attended.reshape(seq_count * length, width)))
    summed_one = hidden + low_back(jnp.dot(attended, w_out, precision=highest) + bias_out)
    first = normalize(summed_one) * gain_first + shift_first
    pre = low_back(jnp.dot(low(first), w_up, precision=highest) + bias_up)
    activation = low(jax.nn.gelu(pre, approximate=False))
    summed_two = first + low_back(jnp.dot(activation, w_down, precision=highest) + bias_down)
    result = normalize(summed_two) * gain_second + shift_second
    head_top = lax.optimization_barrier(jnp.max(top[..., 0], axis=(0, 2)))
    return (result, head_top)

def forward(hidden, seg_rows, weights):
    tops = []
    for layer_index in range(LAYERS):
        params = tuple((weight[layer_index] for weight in weights))
        hidden, head_top = one_layer(hidden, seg_rows, params)
        tops.append(head_top)
    return (hidden, jnp.stack(tops))

def reference(inputs, cotangent, segments, w_qkv, w_out, w_up, w_down, bias_query, bias_value, bias_out, bias_up, bias_down, norm1_gain, norm1_bias, norm2_gain, norm2_bias, tau):
    weights = tuple((weight.astype(jnp.float32) for weight in (w_qkv, w_out, w_up, w_down, bias_query, bias_value, bias_out, bias_up, bias_down, norm1_gain, norm1_bias, norm2_gain, norm2_bias)))
    width = inputs.shape[1]
    group = 4
    length = segments.shape[1]
    blocks = segments.shape[0] // group
    inputs_blocks = inputs.astype(jnp.float32).reshape(blocks, group * length, width)
    cot_blocks = cotangent.astype(jnp.float32).reshape(blocks, group * length, width)
    seg_blocks = segments.reshape(blocks, group, length)

    def step(carry, item):
        totals, tops = carry
        block_in, block_cot, block_seg = item
        result, pullback, top_now = jax.vjp(lambda first_arg, second_arg: forward(first_arg, block_seg, second_arg), block_in, weights, has_aux=True)
        grad_in, grad_weights = pullback(block_cot)
        totals = tuple((total + grad for total, grad in zip(totals, grad_weights)))
        return ((totals, jnp.maximum(tops, top_now)), (result, grad_in))
    start = (tuple((jnp.zeros_like(weight) for weight in weights)), jnp.full((LAYERS, HEADS), neg_large, jnp.float32))
    (totals, tops), (results, grads_in) = lax.scan(step, start, (inputs_blocks, cot_blocks, seg_blocks))
    output = results.reshape(-1, width).astype(jnp.bfloat16)
    input_grad = grads_in.reshape(-1, width)
    head_dim = width // HEADS
    factor = jnp.sqrt(tau / jnp.maximum(tops, tau))
    column_scale = jnp.repeat(factor, head_dim, axis=1)
    both_scale = jnp.concatenate([column_scale, column_scale], axis=1)
    clipped_qk = weights[0][:, :, :2 * width] * both_scale[:, None, :]
    clipped_bias_query = weights[4] * column_scale
    return (output, input_grad, totals[0], totals[1], totals[2], totals[3], totals[4], totals[5], totals[6], totals[7], totals[8], totals[9], totals[10], totals[11], totals[12], clipped_qk, clipped_bias_query)
```

```python
import math

import jax
import jax.numpy as jnp
from jax import lax
from jax.sharding import PartitionSpec as P

HEADS = 16


epsilon = 1e-05
neg_large = -1e30
low = jnp.bfloat16
wide = jnp.float32


def normalize(values):
    centred = values - jnp.mean(values, axis=-1, keepdims=True)
    rstd = lax.rsqrt(jnp.mean(centred * centred, axis=-1, keepdims=True) + epsilon)
    return (centred * rstd, rstd)


def norm_back(grad_norm, normed, rstd):
    inner = jnp.mean(grad_norm * normed, axis=-1, keepdims=True)
    return rstd * (grad_norm - jnp.mean(grad_norm, axis=-1, keepdims=True) - normed * inner)


def gelu_slope(pre):
    cdf = 0.5 * (1.0 + lax.erf(pre * (1.0 / math.sqrt(2.0))))
    return cdf + pre * jnp.exp(-0.5 * pre * pre) * (1.0 / math.sqrt(2.0 * math.pi))


def column_sums(values):
    return jnp.sum(values.astype(wide), axis=0)


class Net:
    def __init__(self, shards, reps, step):
        self.shards = shards
        self.reps = reps
        self.step = step
        self.pairs = shards // 2
        self.high = shards // (2 * step)
        self.bits = self.pairs.bit_length() - 1
        self.me = lax.axis_index("shard")
        self.core = (self.me // step) % 2
        self.rep = lax.axis_index("rep")

    def over_core(self, value):
        return lax.ppermute(value, "shard", [(i, i ^ self.step) for i in range(self.shards)])

    def stride(self, bit):
        return (1 << bit) if (1 << bit) < self.step else (2 << bit)

    def over_bit(self, value, bit):
        step = self.stride(bit)
        return lax.ppermute(value, "shard", [(i, i ^ step) for i in range(self.shards)])

    def chip_bit(self, bit):
        return (self.me // self.stride(bit)) % 2

    def rows_in_order(self, value):
        rest = value.shape[2:]
        value = value.reshape((self.high, self.step, 2) + rest)
        return jnp.swapaxes(value, 1, 2).reshape((self.shards,) + rest)

    def rows_by_pair(self, value):
        rest = value.shape[1:]
        value = value.reshape((self.high, 2, self.step) + rest)
        return jnp.swapaxes(value, 1, 2).reshape((self.pairs, 2) + rest)

    def in_order(self, mine, other, place):
        first = place == 0
        return jnp.stack([jnp.where(first, mine, other), jnp.where(first, other, mine)])

    def gather_chips(self, piece, order):
        shape = piece.shape
        for bit in order:
            piece = self.in_order(piece, self.over_bit(piece, bit), self.chip_bit(bit))
        axes = list(reversed(order))
        natural = [axes.index(bit) for bit in reversed(range(self.bits))]
        rest = list(range(self.bits, self.bits + len(shape)))
        return piece.transpose(natural + rest).reshape((self.pairs,) + shape)

    def scatter_chips(self, value, order):
        rest = value.shape[1:]
        value = value.reshape((2,) * self.bits + rest)
        left = list(reversed(range(self.bits)))
        for bit in order:
            axis = left.index(bit)
            place = self.chip_bit(bit)
            theirs = lax.dynamic_index_in_dim(value, 1 - place, axis, keepdims=False)
            ours = lax.dynamic_index_in_dim(value, place, axis, keepdims=False)
            got = self.over_bit(theirs, bit)
            value = (ours.astype(wide) + got.astype(wide)).astype(value.dtype)
            left.remove(bit)
        return value

    def sum_reps(self, value):
        reps, half = self.reps, self.reps // 2

        def add(one, other):
            return (one.astype(wide) + other.astype(wide)).astype(value.dtype)

        total = value
        for i in range(half - 1):
            got = lax.ppermute(total, "rep", [(i, i + 1), (reps - 1 - i, reps - 2 - i)])
            total = add(total, got)
        total = add(total, lax.ppermute(total, "rep", [(half - 1, half), (half, half - 1)]))
        for i in reversed(range(half - 1)):
            got = lax.ppermute(total, "rep", [(i + 1, i), (reps - 2 - i, reps - 1 - i)])
            outer = jnp.logical_or(self.rep == i, self.rep == reps - 1 - i)
            total = jnp.where(outer, got, total)
        return total

    def pair(self, value):
        return jnp.concatenate([value, self.over_core(value)], axis=0)

    def join(self, partial):
        rows = partial.shape[0] // 2
        return partial[:rows] + self.over_core(partial[rows:].astype(low)).astype(wide)


def halves(columns):
    return ((0, columns // 2), (columns // 2, columns))


def gather_weight(net, piece):
    orders = (list(range(net.bits)), list(reversed(range(net.bits))))
    parts = [
        net.gather_chips(piece[:, start:stop], order)
        for order, (start, stop) in zip(orders, halves(piece.shape[1]))
    ]
    return jnp.concatenate(parts, axis=2)


def scatter_weight(net, value):
    orders = (list(range(net.bits)), list(reversed(range(net.bits))))
    parts = [
        net.sum_reps(net.scatter_chips(value[:, :, start:stop], order))
        for order, (start, stop) in zip(orders, halves(value.shape[2]))
    ]
    return jnp.concatenate(parts, axis=1)


def by_core(weight, net, groups):
    rows, columns = weight.shape
    split = weight.reshape(rows, groups * net.high, 2, columns // (2 * groups * net.high))
    mine = lax.dynamic_index_in_dim(split, net.core, 2, keepdims=False)
    other = lax.dynamic_index_in_dim(split, 1 - net.core, 2, keepdims=False)
    return mine.reshape(rows, columns // 2), other.reshape(rows, columns // 2)


def swap_columns(weight, net, groups):
    mine, other = by_core(weight, net, groups)
    return net.in_order(mine, net.over_core(other), net.core).reshape(-1, mine.shape[1])


def swap_back(value, net, groups):
    rows = value.shape[0] // 2
    split = value.reshape(2, rows, value.shape[1])
    mine = lax.dynamic_index_in_dim(split, net.core, 0, keepdims=False)
    other = lax.dynamic_index_in_dim(split, 1 - net.core, 0, keepdims=False)
    got = net.over_core(other)
    block = value.shape[1] // (groups * net.high)
    both = [part.reshape(rows, groups * net.high, block) for part in (mine, got)]
    first = net.core == 0
    stacked = jnp.stack(
        [jnp.where(first, both[0], both[1]), jnp.where(first, both[1], both[0])], axis=2
    )
    return stacked.reshape(rows, 2 * value.shape[1])


def split_heads(rows, heads):
    return rows.reshape(2, rows.shape[0] // 2, heads, rows.shape[1] // heads)


def masked_scores(query, key_rows, same):
    scale = 1.0 / math.sqrt(query.shape[-1])
    scores = jnp.einsum("sqhd,skhd->shqk", query, key_rows, preferred_element_type=wide) * scale
    return jnp.where(same[:, None], scores, neg_large)


def forward_layer(net, hidden, weights, small, same):
    w_qkv, w_out, w_up, w_down = weights
    bias_qkv, bias_out, bias_up, bias_down, gain_first, shift_first, gain_second, shift_second = small
    heads = HEADS // 2
    third = w_qkv.shape[1] // 3
    both_hidden = net.pair(hidden.astype(low))
    qkv = (jnp.dot(both_hidden, w_qkv, preferred_element_type=wide) + bias_qkv).astype(low)
    query = split_heads(qkv[:, :third], heads)
    key_rows = split_heads(qkv[:, third : 2 * third], heads)
    value_rows = split_heads(qkv[:, 2 * third :], heads)
    masked = masked_scores(query, key_rows, same)
    top = jnp.max(masked, axis=3, keepdims=True)
    expo = jnp.exp(masked - top)
    total = jnp.sum(expo, axis=3, keepdims=True)
    probs = (expo / total).astype(low)
    log_total = top + jnp.log(total)
    head_top = jnp.max(top, axis=(0, 2, 3))
    attended = jnp.einsum("shqk,skhd->sqhd", probs, value_rows, preferred_element_type=wide)
    attended = attended.reshape(qkv.shape[0], third).astype(low)
    summed_one = (
        hidden + net.join(jnp.dot(attended, w_out, preferred_element_type=wide)) + bias_out
    )
    normed_one, rstd_one = normalize(summed_one)
    first = normed_one * gain_first + shift_first
    both_first = net.pair(first.astype(low))
    pre = jnp.dot(both_first, w_up, preferred_element_type=wide) + bias_up
    activation = jax.nn.gelu(pre, approximate=False).astype(low)
    summed_two = (
        first + net.join(jnp.dot(activation, w_down, preferred_element_type=wide)) + bias_down
    )
    normed_two, rstd_two = normalize(summed_two)
    result = normed_two * gain_second + shift_second
    saved = (
        both_hidden,
        qkv,
        log_total,
        attended,
        normed_one,
        rstd_one,
        both_first,
        pre,
        activation,
        normed_two,
        rstd_two,
    )
    return (result, head_top, saved)


def matmul_rows(left, right):
    return jnp.einsum("ti,to->io", left, right, preferred_element_type=wide).astype(low)


def matmul_back(left, right):
    return jnp.einsum("to,io->ti", left, right, preferred_element_type=wide)


def backward_layer(net, grad_out, weights, small, same, saved):
    w_qkv, w_out, w_up, w_down = weights
    bias_qkv, bias_out, bias_up, bias_down, gain_first, shift_first, gain_second, shift_second = small
    (
        both_hidden,
        qkv,
        log_total,
        attended,
        normed_one,
        rstd_one,
        both_first,
        pre,
        activation,
        normed_two,
        rstd_two,
    ) = saved
    heads = HEADS // 2
    third = w_qkv.shape[1] // 3
    scale = 1.0 / math.sqrt(third // heads)
    grad_gain_second = jnp.sum(grad_out * normed_two, axis=0)
    grad_shift_second = jnp.sum(grad_out, axis=0)
    grad_sum_two = norm_back(grad_out * gain_second, normed_two, rstd_two)
    branch_two = grad_sum_two.astype(low)
    grad_bias_down = column_sums(branch_two)
    both_two = net.pair(branch_two)
    grad_w_down = matmul_rows(activation, both_two)
    branch_pre = (matmul_back(both_two, w_down) * gelu_slope(pre)).astype(low)
    grad_bias_up = column_sums(branch_pre)
    grad_w_up = matmul_rows(both_first, branch_pre)
    grad_first = grad_sum_two + net.join(matmul_back(branch_pre, w_up))
    grad_gain_first = jnp.sum(grad_first * normed_one, axis=0)
    grad_shift_first = jnp.sum(grad_first, axis=0)
    grad_sum_one = norm_back(grad_first * gain_first, normed_one, rstd_one)
    branch_one = grad_sum_one.astype(low)
    grad_bias_out = column_sums(branch_one)
    both_one = net.pair(branch_one)
    grad_w_out = matmul_rows(attended, both_one)
    grad_attended = split_heads(matmul_back(both_one, w_out).astype(low), heads)
    query = split_heads(qkv[:, :third], heads)
    key_rows = split_heads(qkv[:, third : 2 * third], heads)
    value_rows = split_heads(qkv[:, 2 * third :], heads)
    masked = masked_scores(query, key_rows, same)
    probs = jnp.exp(masked - log_total)
    grad_value = jnp.einsum(
        "shqk,sqhd->skhd", probs.astype(low), grad_attended, preferred_element_type=wide
    )
    grad_probs = jnp.einsum("sqhd,skhd->shqk", grad_attended, value_rows, preferred_element_type=wide)
    row_inner = jnp.sum(probs * grad_probs, axis=3, keepdims=True)
    grad_scores = (probs * (grad_probs - row_inner)).astype(low)
    grad_query = (
        jnp.einsum("shqk,skhd->sqhd", grad_scores, key_rows, preferred_element_type=wide) * scale
    )
    grad_key = (
        jnp.einsum("shqk,sqhd->skhd", grad_scores, query, preferred_element_type=wide) * scale
    )
    grad_qkv = jnp.concatenate(
        [part.astype(low).reshape(qkv.shape[0], third) for part in (grad_query, grad_key, grad_value)],
        axis=1,
    )
    grad_bias_query = column_sums(grad_qkv[:, :third])
    grad_bias_value = column_sums(grad_qkv[:, 2 * third :])
    grad_w_qkv = matmul_rows(both_hidden, grad_qkv)
    grad_hidden = grad_sum_one + net.join(matmul_back(grad_qkv, w_qkv))
    large = []
    for value, paired in ((grad_w_qkv, True), (grad_w_out, False), (grad_w_up, True), (grad_w_down, False)):
        columns = value.shape[1]
        if paired:
            value = net.rows_by_pair(value.reshape(net.shards, -1, columns))
        large.append(scatter_weight(net, value.reshape(net.pairs, -1, columns)))
    owned = (
        swap_back(large[0], net, 3),
        large[1],
        swap_back(large[2], net, 1),
        large[3],
    )
    terms = (
        grad_bias_query,
        grad_bias_value,
        grad_bias_out,
        grad_bias_up,
        grad_bias_down,
        grad_gain_first,
        grad_shift_first,
        grad_gain_second,
        grad_shift_second,
    )
    return (grad_hidden, owned, terms)


def shards(
    inputs,
    cotangent,
    segments,
    w_qkv,
    w_out,
    w_up,
    w_down,
    bias_query,
    bias_value,
    bias_out,
    bias_up,
    bias_down,
    norm1_gain,
    norm1_bias,
    norm2_gain,
    norm2_bias,
    tau,
    *,
    shard_count,
    rep_count,
):
    layer_count = w_qkv.shape[0]
    width = w_qkv.shape[2] // 3
    rows_here = bias_query.shape[1]
    head_dim = width // HEADS
    net = Net(shard_count, rep_count, max(1, head_dim // rows_here))

    vectors = (
        bias_query,
        bias_value,
        bias_out,
        bias_up,
        bias_down,
        norm1_gain,
        norm1_bias,
        norm2_gain,
        norm2_bias,
    )
    lengths = [vector.shape[1] // rows_here for vector in vectors]
    packed = jnp.concatenate(
        [vector.reshape(layer_count, -1, rows_here) for vector in vectors], axis=1
    )
    packed = net.in_order(packed, net.over_core(packed), net.core)
    packed = net.rows_in_order(net.gather_chips(packed, list(range(net.bits))))

    def whole(layer_index, member):
        start = sum(lengths[:member])
        return packed[:, layer_index, start : start + lengths[member]].astype(wide)

    def of_core(layer_index, member):
        split = whole(layer_index, member).reshape(net.high, 2, -1)
        return lax.dynamic_index_in_dim(split, net.core, 1, keepdims=False).reshape(-1)

    def small_of(layer_index):
        bias_q = of_core(layer_index, 0)
        bias_qkv = jnp.concatenate([bias_q, jnp.zeros_like(bias_q), of_core(layer_index, 1)])
        return (
            bias_qkv,
            whole(layer_index, 2).reshape(-1),
            of_core(layer_index, 3),
        ) + tuple(whole(layer_index, member).reshape(-1) for member in (4, 5, 6, 7, 8))

    both_segments = jnp.concatenate([segments, net.over_core(segments)], axis=0)
    same = both_segments[:, :, None] == both_segments[:, None, :]

    hidden = inputs.astype(wide)
    saved_all, weights_all, small_all, tops = [], [], [], []
    for layer_index in range(layer_count):
        pieces = (
            swap_columns(w_qkv[layer_index], net, 3),
            w_out[layer_index],
            swap_columns(w_up[layer_index], net, 1),
            w_down[layer_index],
        )
        weights = []
        for piece, paired in zip(pieces, (True, False, True, False)):
            full = gather_weight(net, piece)
            if paired:
                full = net.rows_in_order(full.reshape(net.pairs, 2, -1, full.shape[2]))
            weights.append(full.reshape(-1, full.shape[2]))
        small = small_of(layer_index)
        hidden, head_top, saved = forward_layer(net, hidden, weights, small, same)
        saved_all.append(saved)
        weights_all.append(weights)
        small_all.append(small)
        tops.append(head_top)
    output = hidden.astype(low)

    local = jnp.stack(tops)
    local = net.in_order(local, net.over_core(local), net.core)
    local = local.reshape(2, layer_count, net.high, -1).transpose(1, 2, 0, 3).reshape(layer_count, HEADS)
    for bit in range(net.bits):
        local = jnp.maximum(local, net.over_bit(local, bit))
    step = 1
    while step < net.reps:
        local = jnp.maximum(
            local, lax.ppermute(local, "rep", [(i, i ^ step) for i in range(net.reps)])
        )
        step *= 2
    peak = local

    grad_flow = cotangent.astype(wide)
    owned_all = [None] * layer_count
    terms_all = [None] * layer_count
    for layer_index in reversed(range(layer_count)):
        grad_flow, owned, terms = backward_layer(
            net,
            grad_flow,
            weights_all[layer_index],
            small_all[layer_index],
            same,
            saved_all[layer_index],
        )
        owned_all[layer_index] = owned
        terms_all[layer_index] = terms
    large = tuple(
        jnp.stack([owned_all[layer_index][member].astype(wide) for layer_index in range(layer_count)])
        for member in range(4)
    )

    def placed(value, member):
        if member in (0, 1, 3):
            value = value.reshape(net.high, 1, net.step, lengths[member], rows_here)
            zero = jnp.zeros_like(value)
            first = net.core == 0
            return jnp.concatenate(
                [jnp.where(first, value, zero), jnp.where(first, zero, value)], axis=1
            )
        return value.reshape(net.high, 2, net.step, lengths[member], rows_here)

    terms = jnp.stack(
        [
            jnp.concatenate(
                [placed(value, member) for member, value in enumerate(terms_all[layer_index])], axis=3
            )
            for layer_index in range(layer_count)
        ],
        axis=3,
    )
    theirs = lax.dynamic_index_in_dim(terms, 1 - net.core, 1, keepdims=False)
    ours = lax.dynamic_index_in_dim(terms, net.core, 1, keepdims=False)
    terms = ours + net.over_core(theirs)
    terms = terms.reshape((net.pairs,) + terms.shape[2:])
    terms = net.sum_reps(net.scatter_chips(terms, list(range(net.bits))))
    vector_grads = []
    start = 0
    for length in lengths:
        vector_grads.append(terms[:, start : start + length].reshape(layer_count, -1))
        start += length

    factor = jnp.sqrt(tau / jnp.maximum(peak, tau))
    column_scale = jnp.repeat(factor, head_dim, axis=1)
    both_scale = jnp.concatenate([column_scale, column_scale], axis=1)
    clipped_qk = w_qkv[:, :, : 2 * width].astype(wide) * both_scale[:, None, :]
    start = lax.axis_index("shard") * rows_here
    scale_here = lax.dynamic_slice_in_dim(column_scale, start, rows_here, 1)
    clipped_bias_query = bias_query.astype(wide) * scale_here
    return (output, grad_flow) + large + tuple(vector_grads) + (clipped_qk, clipped_bias_query)


def solution(mesh):
    tokens = P(("rep", "shard"), None)
    matrix = P(None, "shard", None)
    vector = P(None, "shard")
    in_specs = (tokens, tokens, tokens) + (matrix,) * 4 + (vector,) * 9 + (P(),)
    out_specs = (tokens, tokens) + (matrix,) * 4 + (vector,) * 9 + (matrix, vector)

    def local(*arrays):
        return shards(*arrays, shard_count=mesh.shape["shard"], rep_count=mesh.shape["rep"])

    return jax.shard_map(local, mesh=mesh, in_specs=in_specs, out_specs=out_specs, check_vma=False)
```

```python
import functools
import math

import jax
import jax.numpy as jnp
from jax import lax
from jax.experimental import pallas as pl
from jax.experimental.pallas import tpu as pltpu
from jax.sharding import PartitionSpec as P

HEADS = 16
MESH = pl.DeviceIdType.MESH


epsilon = 1e-05
neg_large = -1e30
low = jnp.bfloat16
wide = jnp.float32


def normalize(values):
    centred = values - jnp.mean(values, axis=-1, keepdims=True)
    rstd = lax.rsqrt(jnp.mean(centred * centred, axis=-1, keepdims=True) + epsilon)
    return (centred * rstd, rstd)


def norm_back(grad_norm, normed, rstd):
    inner = jnp.mean(grad_norm * normed, axis=-1, keepdims=True)
    return rstd * (grad_norm - jnp.mean(grad_norm, axis=-1, keepdims=True) - normed * inner)


def column_sums(values):
    return jnp.sum(values.astype(wide), axis=0)


class Net:
    def __init__(self, shards, reps, step):
        self.shards = shards
        self.reps = reps
        self.step = step
        self.pairs = shards // 2
        self.high = shards // (2 * step)
        self.bits = self.pairs.bit_length() - 1
        self.me = lax.axis_index("shard")
        self.core = (self.me // step) % 2
        self.rep = lax.axis_index("rep")

    def over_core(self, value):
        return lax.ppermute(value, "shard", [(i, i ^ self.step) for i in range(self.shards)])

    def stride(self, bit):
        return (1 << bit) if (1 << bit) < self.step else (2 << bit)

    def over_bit(self, value, bit):
        step = self.stride(bit)
        return lax.ppermute(value, "shard", [(i, i ^ step) for i in range(self.shards)])

    def chip_bit(self, bit):
        return (self.me // self.stride(bit)) % 2

    def rows_in_order(self, value):
        rest = value.shape[2:]
        value = value.reshape((self.high, self.step, 2) + rest)
        return jnp.swapaxes(value, 1, 2).reshape((self.shards,) + rest)

    def rows_by_pair(self, value):
        rest = value.shape[1:]
        value = value.reshape((self.high, 2, self.step) + rest)
        return jnp.swapaxes(value, 1, 2).reshape((self.pairs, 2) + rest)

    def in_order(self, mine, other, place):
        first = place == 0
        return jnp.stack([jnp.where(first, mine, other), jnp.where(first, other, mine)])

    def gather_chips(self, piece, order):
        shape = piece.shape
        for bit in order:
            piece = self.in_order(piece, self.over_bit(piece, bit), self.chip_bit(bit))
        axes = list(reversed(order))
        natural = [axes.index(bit) for bit in reversed(range(self.bits))]
        rest = list(range(self.bits, self.bits + len(shape)))
        return piece.transpose(natural + rest).reshape((self.pairs,) + shape)

    def scatter_chips(self, value, order):
        rest = value.shape[1:]
        value = value.reshape((2,) * self.bits + rest)
        left = list(reversed(range(self.bits)))
        for bit in order:
            axis = left.index(bit)
            place = self.chip_bit(bit)
            theirs = lax.dynamic_index_in_dim(value, 1 - place, axis, keepdims=False)
            ours = lax.dynamic_index_in_dim(value, place, axis, keepdims=False)
            got = self.over_bit(theirs, bit)
            value = (ours.astype(wide) + got.astype(wide)).astype(value.dtype)
            left.remove(bit)
        return value

    def sum_reps(self, value):
        reps, half = self.reps, self.reps // 2

        def add(one, other):
            return (one.astype(wide) + other.astype(wide)).astype(value.dtype)

        total = value
        for i in range(half - 1):
            got = lax.ppermute(total, "rep", [(i, i + 1), (reps - 1 - i, reps - 2 - i)])
            total = add(total, got)
        total = add(total, lax.ppermute(total, "rep", [(half - 1, half), (half, half - 1)]))
        for i in reversed(range(half - 1)):
            got = lax.ppermute(total, "rep", [(i + 1, i), (reps - 2 - i, reps - 1 - i)])
            outer = jnp.logical_or(self.rep == i, self.rep == reps - 1 - i)
            total = jnp.where(outer, got, total)
        return total

    def pair(self, value):
        return jnp.concatenate([value, self.over_core(value)], axis=0)

    def join(self, partial):
        rows = partial.shape[0] // 2
        return partial[:rows] + self.over_core(partial[rows:].astype(low)).astype(wide)


def halves(columns):
    return ((0, columns // 2), (columns // 2, columns))


def scatter_weight(net, value):
    orders = (list(range(net.bits)), list(reversed(range(net.bits))))
    parts = [
        net.sum_reps(net.scatter_chips(value[:, :, start:stop], order))
        for order, (start, stop) in zip(orders, halves(value.shape[2]))
    ]
    return jnp.concatenate(parts, axis=1)


def by_half(weight, net, groups):
    layers, rows, columns = weight.shape
    split = weight.reshape(layers, rows, groups * net.high, 2, columns // (2 * groups * net.high))
    return split.transpose(0, 3, 1, 2, 4).reshape(layers, 2, rows, columns // 2)


def swap_back(value, net, groups):
    rows = value.shape[0] // 2
    split = value.reshape(2, rows, value.shape[1])
    mine = lax.dynamic_index_in_dim(split, net.core, 0, keepdims=False)
    other = lax.dynamic_index_in_dim(split, 1 - net.core, 0, keepdims=False)
    got = net.over_core(other)
    block = value.shape[1] // (groups * net.high)
    both = [part.reshape(rows, groups * net.high, block) for part in (mine, got)]
    first = net.core == 0
    stacked = jnp.stack(
        [jnp.where(first, both[0], both[1]), jnp.where(first, both[1], both[0])], axis=2
    )
    return stacked.reshape(rows, 2 * value.shape[1])


def split_heads(rows, heads):
    return rows.reshape(2, rows.shape[0] // 2, heads, rows.shape[1] // heads)


class Place:
    def __init__(self, dims):
        self.dims = dims
        step = dims.step
        self.rep = lax.axis_index("rep")
        self.me = lax.axis_index("shard")
        self.half = (self.me // step) % 2
        self.pair = (self.me // (2 * step)) * step + self.me % step
        self.plane = self.rep % 2

    def flip(self, value, bit):
        size = 1 << bit
        return value + size * (1 - 2 * ((value // size) % 2))

    def mate(self):
        return (self.rep, self.me + self.dims.step * (1 - 2 * self.half))

    def over_bit(self, bit):
        stride = (1 << bit) if (1 << bit) < self.dims.step else (2 << bit)
        return (self.rep, self.me + stride * (1 - 2 * ((self.me // stride) % 2)))

    def over_plane(self):
        return (self.rep + 1 - 2 * self.plane, self.me)

    def first_shard(self, pair):
        step = self.dims.step
        return (pair // step) * (2 * step) + pair % step


class Dims:
    def __init__(self, shards, reps, step, layers, tokens, width, hidden):
        self.shards, self.reps, self.step = shards, reps, step
        self.pairs = shards // 2
        self.bits = self.pairs.bit_length() - 1
        self.layers, self.tokens, self.width, self.hidden = layers, tokens, width, hidden
        self.head_dim = width // HEADS
        self.third = width // 2
        self.rows = width // shards
        self.kinds = (
            (self.rows, width, 3 * width // 2, True),
            (self.rows, width // 2, width, False),
            (self.rows, width, hidden // 2, True),
            (hidden // shards, hidden // 2, width, False),
        )


def remote(src, dst, send, recv, where):
    return pltpu.make_async_remote_copy(
        src_ref=src, dst_ref=dst, send_sem=send, recv_sem=recv, device_id=where, device_id_type=MESH
    )


class Gather:
    def __init__(self, place, layer, kind, source, whole, sems, in_plane):
        self.place, self.dims = place, place.dims
        self.layer, self.kind = layer, kind
        self.source, self.whole = source, whole
        self.rows, self.held, self.columns, self.paired = self.dims.kinds[kind]
        self.local, self.send, self.recv = sems
        self.at = layer * 4 + kind
        self.in_plane = in_plane
        self.stage = 0
        self.stages = self.dims.bits + (2 if in_plane < self.columns else 1)

    def blocks(self, pair):
        if not self.paired:
            return [pair * self.rows], self.rows
        first = self.place.first_shard(pair) * self.rows
        if self.dims.step == 1:
            return [first], 2 * self.rows
        return [first, first + self.dims.step * self.rows], self.rows

    def window(self, part):
        size = self.in_plane // 2
        if (size % 128) and part < 2:
            low_size = size // 128 * 128
            size = low_size if part == 0 else self.in_plane - low_size
            offset = 0 if part == 0 else low_size
        else:
            offset = part * size
        start = self.place.plane * (self.columns - self.in_plane) + offset
        return pl.ds(pl.multiple_of(start, 128), size), size

    def order(self, part):
        bits = list(range(self.dims.bits))
        return bits if part == 0 else bits[::-1]

    def subset(self, done):
        pairs = [self.place.pair]
        for bit in done:
            pairs = pairs + [self.place.flip(pair, bit) for pair in pairs]
        return pairs

    def begin(self):
        place = self.place
        if self.paired:
            mine = place.me * self.rows
            rows = pl.ds(pl.multiple_of(mine, 16), self.rows)
            pltpu.make_async_copy(
                self.source.at[self.layer, place.half], self.whole.at[self.layer, rows], self.local.at[self.at]
            ).start()
            remote(
                self.source.at[self.layer, 1 - place.half],
                self.whole.at[self.layer, rows],
                self.send.at[self.at, 0],
                self.recv.at[self.at, 0],
                place.mate(),
            ).start()
        else:
            rows = pl.ds(pl.multiple_of(place.pair * self.rows, 16), self.rows)
            pltpu.make_async_copy(
                self.source.at[self.layer], self.whole.at[self.layer, rows], self.local.at[self.at]
            ).start()

    def some(self, rows, columns):
        return self.whole.at[self.layer, pl.ds(0, rows), columns]

    def phase(self, turn):
        place = self.place
        for part in range(2):
            order = self.order(part)
            columns, _ = self.window(part)
            for pair in self.subset(order[:turn]):
                starts, count = self.blocks(pair)
                for start in starts:
                    block = self.whole.at[self.layer, pl.ds(pl.multiple_of(start, 16), count), columns]
                    remote(
                        block,
                        block,
                        self.send.at[self.at, 1 + 2 * turn + part],
                        self.recv.at[self.at, 1 + 2 * turn + part],
                        place.over_bit(order[turn]),
                    ).start()

    def phase_bytes(self, turn, part):
        columns = pl.ds(0, self.window(part)[1])
        per_pair = self.rows * (2 if self.paired else 1)
        block = self.some(per_pair << turn, columns)
        at = 1 + 2 * turn + part
        return remote(block, block, self.send.at[self.at, at], self.recv.at[self.at, at], self.place.mate())

    def across(self):
        place = self.place
        size = self.columns - self.in_plane
        columns = pl.ds(pl.multiple_of(place.plane * self.in_plane, 128), size)
        at = 1 + 2 * self.dims.bits
        for pair in self.subset(range(self.dims.bits))[1:]:
            starts, count = self.blocks(pair)
            for start in starts:
                block = self.whole.at[self.layer, pl.ds(pl.multiple_of(start, 16), count), columns]
                remote(block, block, self.send.at[self.at, at], self.recv.at[self.at, at], place.over_plane()).start()

    def across_bytes(self):
        per_pair = self.rows * (2 if self.paired else 1)
        block = self.some(per_pair * (self.dims.pairs - 1), pl.ds(0, self.columns - self.in_plane))
        at = 1 + 2 * self.dims.bits
        return remote(block, block, self.send.at[self.at, at], self.recv.at[self.at, at], self.place.over_plane())

    def own_bytes(self):
        if not self.paired:
            return None
        block = self.some(self.rows, pl.ds(0, self.columns))
        return remote(block, block, self.send.at[self.at, 0], self.recv.at[self.at, 0], self.place.mate())

    def advance(self):
        if self.stage == 0:
            own = self.some(self.rows, pl.ds(0, self.columns))
            pltpu.make_async_copy(own, own, self.local.at[self.at]).wait()
            if self.paired:
                self.own_bytes().wait_recv()
        elif self.stage <= self.dims.bits:
            for part in range(2):
                self.phase_bytes(self.stage - 1, part).wait_recv()
        else:
            self.across_bytes().wait_recv()
        if self.stage < self.dims.bits:
            self.phase(self.stage)
        elif self.stage + 1 < self.stages:
            self.across()
        self.stage += 1

    def reach(self, stage):
        while self.stage < min(stage, self.stages):
            self.advance()

    def finish_sends(self):
        if self.paired:
            self.own_bytes().wait_send()
        for turn in range(self.dims.bits):
            for part in range(2):
                self.phase_bytes(turn, part).wait_send()
        if self.in_plane < self.columns:
            self.across_bytes().wait_send()


def in_plane_columns(dims, layer, kind):
    columns = dims.kinds[kind][2]
    if dims.reps % 2:
        return columns
    blocks = columns // 128
    return {12: 8, 8: 6, 16: 10}.get(blocks, blocks - blocks // 3) * 128


def gelu_and_slope(pre):
    cdf = 0.5 * (1.0 + lax.erf(pre * (1.0 / math.sqrt(2.0))))
    slope = cdf + pre * jnp.exp(-0.5 * pre * pre) * (1.0 / math.sqrt(2.0 * math.pi))
    return pre * cdf, slope


def dot_last(left, right):
    return lax.dot_general(left, right, (((1,), (1,)), ((), ())), preferred_element_type=wide)


def dot_first(left, right):
    return lax.dot_general(left, right, (((0,), (0,)), ((), ())), preferred_element_type=wide)


def tiles(count, body):
    def step(j, carry):
        body(j)
        return carry

    lax.fori_loop(0, count, step, 0)


def forward_kernel(
    dims,
    x_ref,
    seg_row,
    seg_col,
    small,
    src_qkv,
    src_out,
    src_up,
    src_down,
    output,
    tops,
    out_qkv_w,
    out_out_w,
    out_up_w,
    out_down_w,
    out_hidden,
    out_qkv,
    out_attended,
    out_probs,
    out_norm1,
    out_first,
    out_act,
    out_slope,
    out_norm2,
    out_rstd,
    w_qkv,
    w_out,
    w_up,
    w_down,
    both_hidden,
    qkv,
    attended,
    probs,
    norm1,
    both_first,
    act,
    slope,
    norm2,
    rstd,
    hidden,
    first,
    total,
    away,
    back,
    bias,
    seg_rows,
    seg_cols,
    gather_local,
    gather_send,
    gather_recv,
    mate_send,
    mate_recv,
    save_sem,
):
    place = Place(dims)
    tokens, width = dims.tokens, dims.width
    heads_row = 128 // dims.head_dim
    scale = 1.0 / math.sqrt(dims.head_dim)

    barrier = pltpu.get_barrier_semaphore()
    others = [place.mate()] + [place.over_bit(bit) for bit in range(dims.bits)]
    if dims.reps % 2 == 0:
        others.append(place.over_plane())
    for other in others:
        pl.semaphore_signal(barrier, 1, device_id=other, device_id_type=MESH)
    pl.semaphore_wait(barrier, len(others))

    sources = (src_qkv, src_out, src_up, src_down)
    wholes = (w_qkv, w_out, w_up, w_down)
    gathers = [
        Gather(
            place,
            layer,
            kind,
            sources[kind],
            wholes[kind],
            (gather_local, gather_send, gather_recv),
            in_plane_columns(dims, layer, kind),
        )
        for layer in range(dims.layers)
        for kind in range(4)
    ]

    exchanges = []

    def to_mate(src, dst):
        at = len(exchanges)
        copy = remote(src, dst, mate_send.at[at], mate_recv.at[at], place.mate())
        copy.start()
        exchanges.append(copy)
        return copy

    rows_copy = to_mate(seg_row, seg_rows)
    cols_copy = to_mate(seg_col, seg_cols)
    both_hidden[0, pl.ds(0, tokens)] = x_ref[...]
    hidden_copy = to_mate(both_hidden.at[0, pl.ds(0, tokens)], both_hidden.at[0, pl.ds(tokens, tokens)])
    for gather in gathers:
        gather.begin()
    for gather in gathers[:3]:
        gather.reach(1)

    def prepare(at):
        for ahead in reversed(range(1, dims.bits + 2)):
            if at + ahead < len(gathers):
                gathers[at + ahead].reach(max(1, gathers[at + ahead].stages - ahead))
        gathers[at].reach(gathers[at].stages)

    saves = []

    def save(src, dst):
        copy = pltpu.make_async_copy(src, dst, save_sem.at[len(saves)])
        copy.start()
        saves.append(copy)

    hidden[...] = x_ref[...].astype(wide)
    tops[...] = jnp.full(tops.shape, neg_large, wide)
    rows_copy.wait_recv()
    cols_copy.wait_recv()
    for s, (row_ref, col_ref) in enumerate(((seg_row, seg_col), (seg_rows, seg_cols))):
        same = col_ref[:, 0:1] == row_ref[0:1, :]
        bias[s] = jnp.where(same, 0.0, neg_large)

    chunk = 32 if tokens % 32 == 0 else tokens

    def layer_norm(residual, partial, other, bias_row, gain_row, shift_row, normed, rstd_out, results):
        def body(j):
            rows = pl.ds(pl.multiple_of(j * chunk, chunk), chunk)
            value = residual[rows] + partial[rows] + other[rows].astype(wide) + bias_row
            centred = value - jnp.mean(value, axis=-1, keepdims=True)
            scale_row = lax.rsqrt(jnp.mean(centred * centred, axis=-1, keepdims=True) + epsilon)
            normal = centred * scale_row
            normed[rows] = normal
            rstd_out[rows] = jnp.broadcast_to(scale_row, (chunk, 128))
            results(rows, normal * gain_row + shift_row)

        tiles(tokens // chunk, body)

    def project(left, right, at, tile):
        columns = dims.width

        def far(j):
            cols = pl.ds(pl.multiple_of(j * tile, tile), tile)
            away[at % 2, :, cols] = jnp.dot(
                left[pl.ds(tokens, tokens)], right[:, cols], preferred_element_type=wide
            ).astype(low)

        def near(j):
            cols = pl.ds(pl.multiple_of(j * tile, tile), tile)
            total[:, cols] = jnp.dot(left[pl.ds(0, tokens)], right[:, cols], preferred_element_type=wide)

        tiles(columns // tile, far)
        copy = to_mate(away.at[at % 2], back.at[at])
        tiles(columns // tile, near)
        return copy

    tile = min(512, width)
    waits = []
    for layer in range(dims.layers):
        prepare(4 * layer)
        hidden_copy.wait_recv()

        def qkv_tile(j, layer=layer):
            cols = pl.ds(pl.multiple_of(j * tile, tile), tile)
            value = jnp.dot(both_hidden[layer], w_qkv[layer, :, cols], preferred_element_type=wide)
            qkv[layer, :, cols] = (value + small[layer, 0:1, cols]).astype(low)

        tiles(dims.kinds[0][2] // tile, qkv_tile)
        lane_blocks = dims.third // 128

        def attend(j, layer=layer):
            s, block = j // lane_blocks, j % lane_blocks
            rows = pl.ds(pl.multiple_of(s * tokens, tokens), tokens)

            def lanes(which):
                start = pl.multiple_of(which * dims.third + block * 128, 128)
                return qkv[layer, rows, pl.ds(start, 128)]

            query, key_rows, value_rows = lanes(0), lanes(1), lanes(2)
            mask = bias[s]
            outs = []
            for e in range(heads_row):
                part = slice(e * dims.head_dim, (e + 1) * dims.head_dim)
                scores = dot_last(query[:, part], key_rows[:, part]) * scale + mask
                top = jnp.max(scores, axis=1, keepdims=True)
                expo = jnp.exp(scores - top)
                prob = (expo * (1.0 / jnp.sum(expo, axis=1, keepdims=True))).astype(low)
                head = block * heads_row + e
                probs[layer, s * (lane_blocks * heads_row) + head] = prob
                outs.append(jnp.dot(prob, value_rows[:, part], preferred_element_type=wide))
                peak = jnp.broadcast_to(jnp.max(top, axis=0, keepdims=True), (1, 128))
                tops[layer, pl.ds(head, 1)] = jnp.maximum(tops[layer, pl.ds(head, 1)], peak)
            attended[layer, rows, pl.ds(pl.multiple_of(block * 128, 128), 128)] = jnp.concatenate(
                outs, axis=1
            ).astype(low)

        tiles(2 * lane_blocks, attend)

        prepare(4 * layer + 1)
        if layer > 0:
            waits[2 * layer - 2].wait_send()
        copy = project(attended.at[layer], w_out.at[layer], 2 * layer, tile)
        waits.append(copy)
        copy.wait_recv()

        def first_rows(rows, value, layer=layer):
            first[rows] = value
            both_first[layer, rows] = value.astype(low)

        layer_norm(
            hidden,
            total,
            back.at[2 * layer],
            small[layer, 1:2, :width],
            small[layer, 4:5, :width],
            small[layer, 5:6, :width],
            norm1.at[layer],
            rstd.at[layer, 0],
            first_rows,
        )
        first_copy = to_mate(
            both_first.at[layer, pl.ds(0, tokens)], both_first.at[layer, pl.ds(tokens, tokens)]
        )

        prepare(4 * layer + 2)
        first_copy.wait_recv()
        narrow = 256

        def up_tile(j, layer=layer):
            cols = pl.ds(pl.multiple_of(j * narrow, narrow), narrow)
            pre = jnp.dot(both_first[layer], w_up[layer, :, cols], preferred_element_type=wide)
            value, steep = gelu_and_slope(pre + small[layer, 2:3, cols])
            act[layer, :, cols] = value.astype(low)
            slope[layer, :, cols] = steep.astype(low)

        tiles(dims.kinds[2][2] // narrow, up_tile)

        prepare(4 * layer + 3)
        if layer > 0:
            waits[2 * layer - 1].wait_send()
        copy = project(act.at[layer], w_down.at[layer], 2 * layer + 1, tile)
        waits.append(copy)
        copy.wait_recv()
        last = layer == dims.layers - 1

        def second_rows(rows, value, layer=layer, last=last):
            if last:
                output[rows] = value.astype(low)
            else:
                hidden[rows] = value
                both_hidden[layer + 1, rows] = value.astype(low)

        layer_norm(
            first,
            total,
            back.at[2 * layer + 1],
            small[layer, 3:4, :width],
            small[layer, 6:7, :width],
            small[layer, 7:8, :width],
            norm2.at[layer],
            rstd.at[layer, 1],
            second_rows,
        )
        if not last:
            hidden_copy = to_mate(
                both_hidden.at[layer + 1, pl.ds(0, tokens)],
                both_hidden.at[layer + 1, pl.ds(tokens, tokens)],
            )
        for src, dst in (
            (both_hidden, out_hidden),
            (qkv, out_qkv),
            (attended, out_attended),
            (probs, out_probs),
            (norm1, out_norm1),
            (both_first, out_first),
            (act, out_act),
            (slope, out_slope),
            (norm2, out_norm2),
            (rstd, out_rstd),
            (w_qkv, out_qkv_w),
            (w_out, out_out_w),
            (w_up, out_up_w),
            (w_down, out_down_w),
        ):
            save(src.at[layer], dst.at[layer])

    for copy in exchanges:
        if not any(copy is other for other in waits[: 2 * dims.layers - 2]):
            copy.wait_send()
    for gather in gathers:
        gather.finish_sends()
    for copy in saves:
        copy.wait()


def run_forward(dims, x, segments, small, weights):
    layers, tokens, width = dims.layers, dims.tokens, dims.width
    both = 2 * tokens
    held = [
        jax.ShapeDtypeStruct((layers, rows, columns), low) for _, rows, columns, _ in dims.kinds
    ]
    states = [
        ((layers, both, width), low),
        ((layers, both, 3 * dims.third), low),
        ((layers, both, dims.third), low),
        ((layers, HEADS, tokens, tokens), low),
        ((layers, tokens, width), wide),
        ((layers, both, width), low),
        ((layers, both, dims.hidden // 2), low),
        ((layers, both, dims.hidden // 2), low),
        ((layers, tokens, width), wide),
        ((layers, 2, tokens, 128), wide),
    ]
    saved = held + [jax.ShapeDtypeStruct(shape, dtype) for shape, dtype in states]
    seg = segments.astype(wide)
    seg_row = jnp.broadcast_to(seg, (8, tokens))
    seg_col = jnp.broadcast_to(seg.reshape(tokens, 1), (tokens, 128))
    vmem = pl.BlockSpec(memory_space=pltpu.VMEM)
    anywhere = pl.BlockSpec(memory_space=pl.ANY)
    outs = [
        jax.ShapeDtypeStruct((tokens, width), low),
        jax.ShapeDtypeStruct((layers, HEADS // 2, 128), wide),
    ] + saved
    dma = pltpu.SemaphoreType.DMA
    slots = 2 + 2 * dims.bits
    exchange_count = 3 + 4 * layers
    scratch = (
        [pltpu.VMEM(item.shape, item.dtype) for item in saved]
        + [
            pltpu.VMEM((tokens, width), wide),
            pltpu.VMEM((tokens, width), wide),
            pltpu.VMEM((tokens, width), wide),
            pltpu.VMEM((2, tokens, width), low),
            pltpu.VMEM((2 * layers, tokens, width), low),
            pltpu.VMEM((2, tokens, tokens), wide),
            pltpu.VMEM((8, tokens), wide),
            pltpu.VMEM((tokens, 128), wide),
        ]
        + [
            dma((4 * layers,)),
            dma((4 * layers, slots)),
            dma((4 * layers, slots)),
            dma((exchange_count,)),
            dma((exchange_count,)),
            dma((len(saved) * layers,)),
        ]
    )
    return pl.pallas_call(
        functools.partial(forward_kernel, dims),
        out_shape=outs,
        in_specs=[vmem] * 4 + [anywhere] * 4,
        out_specs=[vmem] * 2 + [anywhere] * len(saved),
        scratch_shapes=scratch,
        compiler_params=pltpu.CompilerParams(
            collective_id=0, has_side_effects=True, vmem_limit_bytes=63 * 2**20
        ),
        name="forward",
    )(x, seg_row, seg_col, small, *weights)


def matmul_rows(left, right):
    return jnp.einsum("ti,to->io", left, right, preferred_element_type=wide).astype(low)


def matmul_back(left, right):
    return jnp.einsum("to,io->ti", left, right, preferred_element_type=wide)


def backward_layer(net, grad_out, weights, small, saved):
    w_qkv, w_out, w_up, w_down = weights
    gain_first, gain_second = small[4, : grad_out.shape[1]], small[6, : grad_out.shape[1]]
    both_hidden, qkv, attended, probs, normed_one, both_first, activation, slope, normed_two, rstd = saved
    rstd_one, rstd_two = rstd[0, :, :1], rstd[1, :, :1]
    heads = HEADS // 2
    third = w_qkv.shape[1] // 3
    scale = 1.0 / math.sqrt(third // heads)
    grad_gain_second = jnp.sum(grad_out * normed_two, axis=0)
    grad_shift_second = jnp.sum(grad_out, axis=0)
    grad_sum_two = norm_back(grad_out * gain_second, normed_two, rstd_two)
    branch_two = grad_sum_two.astype(low)
    grad_bias_down = column_sums(branch_two)
    both_two = net.pair(branch_two)
    grad_w_down = matmul_rows(activation, both_two)
    branch_pre = (matmul_back(both_two, w_down) * slope.astype(wide)).astype(low)
    grad_bias_up = column_sums(branch_pre)
    grad_w_up = matmul_rows(both_first, branch_pre)
    grad_first = grad_sum_two + net.join(matmul_back(branch_pre, w_up))
    grad_gain_first = jnp.sum(grad_first * normed_one, axis=0)
    grad_shift_first = jnp.sum(grad_first, axis=0)
    grad_sum_one = norm_back(grad_first * gain_first, normed_one, rstd_one)
    branch_one = grad_sum_one.astype(low)
    grad_bias_out = column_sums(branch_one)
    both_one = net.pair(branch_one)
    grad_w_out = matmul_rows(attended, both_one)
    grad_attended = split_heads(matmul_back(both_one, w_out).astype(low), heads)
    query = split_heads(qkv[:, :third], heads)
    key_rows = split_heads(qkv[:, third : 2 * third], heads)
    value_rows = split_heads(qkv[:, 2 * third :], heads)
    probs = probs.reshape((2, heads) + probs.shape[1:]).astype(wide)
    grad_value = jnp.einsum(
        "shqk,sqhd->skhd", probs.astype(low), grad_attended, preferred_element_type=wide
    )
    grad_probs = jnp.einsum("sqhd,skhd->shqk", grad_attended, value_rows, preferred_element_type=wide)
    row_inner = jnp.sum(probs * grad_probs, axis=3, keepdims=True)
    grad_scores = (probs * (grad_probs - row_inner)).astype(low)
    grad_query = (
        jnp.einsum("shqk,skhd->sqhd", grad_scores, key_rows, preferred_element_type=wide) * scale
    )
    grad_key = (
        jnp.einsum("shqk,sqhd->skhd", grad_scores, query, preferred_element_type=wide) * scale
    )
    grad_qkv = jnp.concatenate(
        [part.astype(low).reshape(qkv.shape[0], third) for part in (grad_query, grad_key, grad_value)],
        axis=1,
    )
    grad_bias_query = column_sums(grad_qkv[:, :third])
    grad_bias_value = column_sums(grad_qkv[:, 2 * third :])
    grad_w_qkv = matmul_rows(both_hidden, grad_qkv)
    grad_hidden = grad_sum_one + net.join(matmul_back(grad_qkv, w_qkv))
    large = []
    for value, paired in ((grad_w_qkv, True), (grad_w_out, False), (grad_w_up, True), (grad_w_down, False)):
        columns = value.shape[1]
        if paired:
            value = net.rows_by_pair(value.reshape(net.shards, -1, columns))
        large.append(scatter_weight(net, value.reshape(net.pairs, -1, columns)))
    owned = (
        swap_back(large[0], net, 3),
        large[1],
        swap_back(large[2], net, 1),
        large[3],
    )
    terms = (
        grad_bias_query,
        grad_bias_value,
        grad_bias_out,
        grad_bias_up,
        grad_bias_down,
        grad_gain_first,
        grad_shift_first,
        grad_gain_second,
        grad_shift_second,
    )
    return (grad_hidden, owned, terms)


def shards(
    inputs,
    cotangent,
    segments,
    w_qkv,
    w_out,
    w_up,
    w_down,
    bias_query,
    bias_value,
    bias_out,
    bias_up,
    bias_down,
    norm1_gain,
    norm1_bias,
    norm2_gain,
    norm2_bias,
    tau,
    *,
    shard_count,
    rep_count,
):
    layer_count = w_qkv.shape[0]
    width = w_qkv.shape[2] // 3
    rows_here = bias_query.shape[1]
    head_dim = width // HEADS
    net = Net(shard_count, rep_count, max(1, head_dim // rows_here))

    vectors = (
        bias_query,
        bias_value,
        bias_out,
        bias_up,
        bias_down,
        norm1_gain,
        norm1_bias,
        norm2_gain,
        norm2_bias,
    )
    lengths = [vector.shape[1] // rows_here for vector in vectors]
    packed = jnp.concatenate(
        [vector.reshape(layer_count, -1, rows_here) for vector in vectors], axis=1
    )
    packed = net.in_order(packed, net.over_core(packed), net.core)
    packed = net.rows_in_order(net.gather_chips(packed, list(range(net.bits))))

    def whole(layer_index, member):
        start = sum(lengths[:member])
        return packed[:, layer_index, start : start + lengths[member]].astype(wide)

    def of_core(layer_index, member):
        split = whole(layer_index, member).reshape(net.high, 2, -1)
        return lax.dynamic_index_in_dim(split, net.core, 1, keepdims=False).reshape(-1)

    def small_of(layer_index):
        bias_q = of_core(layer_index, 0)
        bias_qkv = jnp.concatenate([bias_q, jnp.zeros_like(bias_q), of_core(layer_index, 1)])
        return (
            bias_qkv,
            whole(layer_index, 2).reshape(-1),
            of_core(layer_index, 3),
        ) + tuple(whole(layer_index, member).reshape(-1) for member in (4, 5, 6, 7, 8))

    tokens = inputs.shape[0]
    dims = Dims(shard_count, rep_count, net.step, layer_count, tokens, width, w_up.shape[2])

    def wide_row(row):
        return jnp.pad(row, (0, dims.hidden // 2 - row.shape[0]))

    small = jnp.stack(
        [jnp.stack([wide_row(row) for row in small_of(layer)]) for layer in range(layer_count)]
    )
    results = run_forward(
        dims,
        inputs,
        segments,
        small,
        (by_half(w_qkv, net, 3), w_out, by_half(w_up, net, 1), w_down),
    )
    output, tops = results[0], results[1]
    weights_all, saved_all = results[2:6], results[6:]

    local = tops[:, :, 0]
    local = net.in_order(local, net.over_core(local), net.core)
    local = local.reshape(2, layer_count, net.high, -1).transpose(1, 2, 0, 3).reshape(layer_count, HEADS)
    for bit in range(net.bits):
        local = jnp.maximum(local, net.over_bit(local, bit))
    step = 1
    while step < net.reps:
        local = jnp.maximum(
            local, lax.ppermute(local, "rep", [(i, i ^ step) for i in range(net.reps)])
        )
        step *= 2
    peak = local

    grad_flow = cotangent.astype(wide)
    owned_all = [None] * layer_count
    terms_all = [None] * layer_count
    for layer_index in reversed(range(layer_count)):
        grad_flow, owned, terms = backward_layer(
            net,
            grad_flow,
            [weight[layer_index] for weight in weights_all],
            small[layer_index],
            [state[layer_index] for state in saved_all],
        )
        owned_all[layer_index] = owned
        terms_all[layer_index] = terms
    large = tuple(
        jnp.stack([owned_all[layer_index][member].astype(wide) for layer_index in range(layer_count)])
        for member in range(4)
    )

    def placed(value, member):
        if member in (0, 1, 3):
            value = value.reshape(net.high, 1, net.step, lengths[member], rows_here)
            zero = jnp.zeros_like(value)
            first = net.core == 0
            return jnp.concatenate(
                [jnp.where(first, value, zero), jnp.where(first, zero, value)], axis=1
            )
        return value.reshape(net.high, 2, net.step, lengths[member], rows_here)

    terms = jnp.stack(
        [
            jnp.concatenate(
                [placed(value, member) for member, value in enumerate(terms_all[layer_index])], axis=3
            )
            for layer_index in range(layer_count)
        ],
        axis=3,
    )
    theirs = lax.dynamic_index_in_dim(terms, 1 - net.core, 1, keepdims=False)
    ours = lax.dynamic_index_in_dim(terms, net.core, 1, keepdims=False)
    terms = ours + net.over_core(theirs)
    terms = terms.reshape((net.pairs,) + terms.shape[2:])
    terms = net.sum_reps(net.scatter_chips(terms, list(range(net.bits))))
    vector_grads = []
    start = 0
    for length in lengths:
        vector_grads.append(terms[:, start : start + length].reshape(layer_count, -1))
        start += length

    factor = jnp.sqrt(tau / jnp.maximum(peak, tau))
    column_scale = jnp.repeat(factor, head_dim, axis=1)
    both_scale = jnp.concatenate([column_scale, column_scale], axis=1)
    clipped_qk = w_qkv[:, :, : 2 * width].astype(wide) * both_scale[:, None, :]
    start = lax.axis_index("shard") * rows_here
    scale_here = lax.dynamic_slice_in_dim(column_scale, start, rows_here, 1)
    clipped_bias_query = bias_query.astype(wide) * scale_here
    return (output, grad_flow) + large + tuple(vector_grads) + (clipped_qk, clipped_bias_query)


def solution(mesh):
    tokens = P(("rep", "shard"), None)
    matrix = P(None, "shard", None)
    vector = P(None, "shard")
    in_specs = (tokens, tokens, tokens) + (matrix,) * 4 + (vector,) * 9 + (P(),)
    out_specs = (tokens, tokens) + (matrix,) * 4 + (vector,) * 9 + (matrix, vector)

    def local(*arrays):
        return shards(*arrays, shard_count=mesh.shape["shard"], rep_count=mesh.shape["rep"])

    return jax.shard_map(local, mesh=mesh, in_specs=in_specs, out_specs=out_specs, check_vma=False)
```

```python
import functools
import math

import jax
import jax.numpy as jnp
from jax import lax
from jax.experimental import pallas as pl
from jax.experimental.pallas import tpu as pltpu
from jax.sharding import PartitionSpec as P

HEADS = 16
MESH = pl.DeviceIdType.MESH


epsilon = 1e-05
neg_large = -1e30
low = jnp.bfloat16
wide = jnp.float32


class Net:
    def __init__(self, shards, reps, step):
        self.shards = shards
        self.reps = reps
        self.step = step
        self.pairs = shards // 2
        self.high = shards // (2 * step)
        self.bits = self.pairs.bit_length() - 1
        self.me = lax.axis_index("shard")
        self.core = (self.me // step) % 2
        self.rep = lax.axis_index("rep")

    def over_core(self, value):
        return lax.ppermute(value, "shard", [(i, i ^ self.step) for i in range(self.shards)])

    def stride(self, bit):
        return (1 << bit) if (1 << bit) < self.step else (2 << bit)

    def over_bit(self, value, bit):
        step = self.stride(bit)
        return lax.ppermute(value, "shard", [(i, i ^ step) for i in range(self.shards)])

    def chip_bit(self, bit):
        return (self.me // self.stride(bit)) % 2

    def rows_in_order(self, value):
        rest = value.shape[2:]
        value = value.reshape((self.high, self.step, 2) + rest)
        return jnp.swapaxes(value, 1, 2).reshape((self.shards,) + rest)

    def rows_by_pair(self, value):
        rest = value.shape[1:]
        value = value.reshape((self.high, 2, self.step) + rest)
        return jnp.swapaxes(value, 1, 2).reshape((self.pairs, 2) + rest)

    def in_order(self, mine, other, place):
        first = place == 0
        return jnp.stack([jnp.where(first, mine, other), jnp.where(first, other, mine)])

    def gather_chips(self, piece, order):
        shape = piece.shape
        for bit in order:
            piece = self.in_order(piece, self.over_bit(piece, bit), self.chip_bit(bit))
        axes = list(reversed(order))
        natural = [axes.index(bit) for bit in reversed(range(self.bits))]
        rest = list(range(self.bits, self.bits + len(shape)))
        return piece.transpose(natural + rest).reshape((self.pairs,) + shape)

    def scatter_chips(self, value, order):
        rest = value.shape[1:]
        value = value.reshape((2,) * self.bits + rest)
        left = list(reversed(range(self.bits)))
        for bit in order:
            axis = left.index(bit)
            place = self.chip_bit(bit)
            theirs = lax.dynamic_index_in_dim(value, 1 - place, axis, keepdims=False)
            ours = lax.dynamic_index_in_dim(value, place, axis, keepdims=False)
            got = self.over_bit(theirs, bit)
            value = (ours.astype(wide) + got.astype(wide)).astype(value.dtype)
            left.remove(bit)
        return value

    def sum_reps(self, value):
        reps, half = self.reps, self.reps // 2

        def add(one, other):
            return (one.astype(wide) + other.astype(wide)).astype(value.dtype)

        total = value
        for i in range(half - 1):
            got = lax.ppermute(total, "rep", [(i, i + 1), (reps - 1 - i, reps - 2 - i)])
            total = add(total, got)
        total = add(total, lax.ppermute(total, "rep", [(half - 1, half), (half, half - 1)]))
        for i in reversed(range(half - 1)):
            got = lax.ppermute(total, "rep", [(i + 1, i), (reps - 2 - i, reps - 1 - i)])
            outer = jnp.logical_or(self.rep == i, self.rep == reps - 1 - i)
            total = jnp.where(outer, got, total)
        return total


def by_half(weight, net, groups):
    layers, rows, columns = weight.shape
    split = weight.reshape(layers, rows, groups * net.high, 2, columns // (2 * groups * net.high))
    return split.transpose(0, 3, 1, 2, 4).reshape(layers, 2, rows, columns // 2)


def whole_columns(mine, other, net, groups):
    layers, rows, columns = mine.shape
    block = columns // (groups * net.high)
    both = [part.reshape(layers, rows, groups * net.high, block) for part in (mine, other)]
    first = net.core == 0
    stacked = jnp.stack(
        [jnp.where(first, both[0], both[1]), jnp.where(first, both[1], both[0])], axis=3
    )
    return stacked.reshape(layers, rows, 2 * columns).astype(wide)


class Place:
    def __init__(self, dims):
        self.dims = dims
        step = dims.step
        self.rep = lax.axis_index("rep")
        self.me = lax.axis_index("shard")
        self.half = (self.me // step) % 2
        self.pair = (self.me // (2 * step)) * step + self.me % step
        self.plane = self.rep % 2

    def flip(self, value, bit):
        size = 1 << bit
        return value + size * (1 - 2 * ((value // size) % 2))

    def mate(self):
        return (self.rep, self.me + self.dims.step * (1 - 2 * self.half))

    def over_bit(self, bit):
        stride = (1 << bit) if (1 << bit) < self.dims.step else (2 << bit)
        return (self.rep, self.me + stride * (1 - 2 * ((self.me // stride) % 2)))

    def over_plane(self):
        return (self.rep + 1 - 2 * self.plane, self.me)

    def first_shard(self, pair):
        step = self.dims.step
        return (pair // step) * (2 * step) + pair % step


class Dims:
    def __init__(self, shards, reps, step, layers, tokens, width, hidden):
        self.shards, self.reps, self.step = shards, reps, step
        self.pairs = shards // 2
        self.bits = self.pairs.bit_length() - 1
        self.layers, self.tokens, self.width, self.hidden = layers, tokens, width, hidden
        self.head_dim = width // HEADS
        self.third = width // 2
        self.rows = width // shards
        self.kinds = (
            (self.rows, width, 3 * width // 2, True),
            (self.rows, width // 2, width, False),
            (self.rows, width, hidden // 2, True),
            (hidden // shards, hidden // 2, width, False),
        )


def remote(src, dst, send, recv, where):
    return pltpu.make_async_remote_copy(
        src_ref=src, dst_ref=dst, send_sem=send, recv_sem=recv, device_id=where, device_id_type=MESH
    )


class Gather:
    def __init__(self, place, layer, kind, source, whole, sems, in_plane):
        self.place, self.dims = place, place.dims
        self.layer, self.kind = layer, kind
        self.source, self.whole = source, whole
        self.rows, self.held, self.columns, self.paired = self.dims.kinds[kind]
        self.local, self.send, self.recv = sems
        self.at = layer * 4 + kind
        self.in_plane = in_plane
        self.stage = 0
        self.stages = self.dims.bits + (2 if in_plane < self.columns else 1)

    def blocks(self, pair):
        if not self.paired:
            return [pair * self.rows], self.rows
        first = self.place.first_shard(pair) * self.rows
        if self.dims.step == 1:
            return [first], 2 * self.rows
        return [first, first + self.dims.step * self.rows], self.rows

    def window(self, part):
        size = self.in_plane // 2
        if (size % 128) and part < 2:
            low_size = size // 128 * 128
            size = low_size if part == 0 else self.in_plane - low_size
            offset = 0 if part == 0 else low_size
        else:
            offset = part * size
        start = self.place.plane * (self.columns - self.in_plane) + offset
        return pl.ds(pl.multiple_of(start, 128), size), size

    def order(self, part):
        bits = list(range(self.dims.bits))
        return bits if part == 0 else bits[::-1]

    def subset(self, done):
        pairs = [self.place.pair]
        for bit in done:
            pairs = pairs + [self.place.flip(pair, bit) for pair in pairs]
        return pairs

    def begin(self):
        place = self.place
        if self.paired:
            mine = place.me * self.rows
            rows = pl.ds(pl.multiple_of(mine, 16), self.rows)
            pltpu.make_async_copy(
                self.source.at[self.layer, place.half], self.whole.at[self.layer, rows], self.local.at[self.at]
            ).start()
            remote(
                self.source.at[self.layer, 1 - place.half],
                self.whole.at[self.layer, rows],
                self.send.at[self.at, 0],
                self.recv.at[self.at, 0],
                place.mate(),
            ).start()
        else:
            rows = pl.ds(pl.multiple_of(place.pair * self.rows, 16), self.rows)
            pltpu.make_async_copy(
                self.source.at[self.layer], self.whole.at[self.layer, rows], self.local.at[self.at]
            ).start()

    def some(self, rows, columns):
        return self.whole.at[self.layer, pl.ds(0, rows), columns]

    def phase(self, turn):
        place = self.place
        for part in range(2):
            order = self.order(part)
            columns, _ = self.window(part)
            for pair in self.subset(order[:turn]):
                starts, count = self.blocks(pair)
                for start in starts:
                    block = self.whole.at[self.layer, pl.ds(pl.multiple_of(start, 16), count), columns]
                    remote(
                        block,
                        block,
                        self.send.at[self.at, 1 + 2 * turn + part],
                        self.recv.at[self.at, 1 + 2 * turn + part],
                        place.over_bit(order[turn]),
                    ).start()

    def phase_bytes(self, turn, part):
        columns = pl.ds(0, self.window(part)[1])
        per_pair = self.rows * (2 if self.paired else 1)
        block = self.some(per_pair << turn, columns)
        at = 1 + 2 * turn + part
        return remote(block, block, self.send.at[self.at, at], self.recv.at[self.at, at], self.place.mate())

    def across(self):
        place = self.place
        size = self.columns - self.in_plane
        columns = pl.ds(pl.multiple_of(place.plane * self.in_plane, 128), size)
        at = 1 + 2 * self.dims.bits
        for pair in self.subset(range(self.dims.bits))[1:]:
            starts, count = self.blocks(pair)
            for start in starts:
                block = self.whole.at[self.layer, pl.ds(pl.multiple_of(start, 16), count), columns]
                remote(block, block, self.send.at[self.at, at], self.recv.at[self.at, at], place.over_plane()).start()

    def across_bytes(self):
        per_pair = self.rows * (2 if self.paired else 1)
        block = self.some(per_pair * (self.dims.pairs - 1), pl.ds(0, self.columns - self.in_plane))
        at = 1 + 2 * self.dims.bits
        return remote(block, block, self.send.at[self.at, at], self.recv.at[self.at, at], self.place.over_plane())

    def own_bytes(self):
        if not self.paired:
            return None
        block = self.some(self.rows, pl.ds(0, self.columns))
        return remote(block, block, self.send.at[self.at, 0], self.recv.at[self.at, 0], self.place.mate())

    def advance(self):
        if self.stage == 0:
            own = self.some(self.rows, pl.ds(0, self.columns))
            pltpu.make_async_copy(own, own, self.local.at[self.at]).wait()
            if self.paired:
                self.own_bytes().wait_recv()
        elif self.stage <= self.dims.bits:
            for part in range(2):
                self.phase_bytes(self.stage - 1, part).wait_recv()
        else:
            self.across_bytes().wait_recv()
        if self.stage < self.dims.bits:
            self.phase(self.stage)
        elif self.stage + 1 < self.stages:
            self.across()
        self.stage += 1

    def reach(self, stage):
        while self.stage < min(stage, self.stages):
            self.advance()

    def finish_sends(self):
        if self.paired:
            self.own_bytes().wait_send()
        for turn in range(self.dims.bits):
            for part in range(2):
                self.phase_bytes(turn, part).wait_send()
        if self.in_plane < self.columns:
            self.across_bytes().wait_send()


class Reduce:
    def __init__(self, place, layer, kind, part, terms, arrived, lines, done, swapped, sems, bufs):
        self.place, self.dims = place, place.dims
        self.layer, self.kind, self.part = layer, kind, part
        self.terms, self.arrived, self.lines, self.done, self.swapped = terms, arrived, lines, done, swapped
        self.send, self.recv = sems
        self.mine, self.other, self.load_sem, self.store_sem = bufs
        self.rows, self.held, self.columns, self.paired = self.dims.kinds[kind]
        self.size = self.columns // 2
        self.columns_here = pl.ds(part * self.size, self.size)
        self.at = (layer * 4 + kind) * 2 + part
        bits = list(range(self.dims.bits))
        self.order = bits if part == 0 else bits[::-1]
        self.moves = self.dims.reps - 1
        self.stage = 0
        self.stages = 1 + self.dims.bits + self.moves + (1 if self.paired else 0)
        self.split = self.paired and self.dims.step > 1
        self.piece = self.rows * (2 if self.paired and not self.split else 1)
        self.pieces = 2 if self.split else 1

    def row_of(self, pair, which):
        if not self.paired:
            return pair * self.rows
        return (self.place.first_shard(pair) + which * self.dims.step) * self.rows

    def sems(self, slot):
        return self.send.at[self.at, slot], self.recv.at[self.at, slot]

    def kept(self, index, turn, away):
        pair = self.place.pair
        for i, bit in enumerate(self.order[turn + 1 :]):
            size = 1 << bit
            wanted = (index // (1 << i)) % 2
            pair = pair + size * (wanted - (self.place.pair // size) % 2)
        if away:
            pair = self.place.flip(pair, self.order[turn])
        return pair

    def count(self, turn):
        return (self.dims.pairs >> (turn + 1)) * self.pieces

    def loop(self, count, body):
        if count <= 4:
            for i in range(count):
                body(i)
        else:
            tiles(count, body)

    def block(self, ref, index, turn, away):
        pair = self.kept(index // self.pieces, turn, away)
        start = self.row_of(pair, index % self.pieces)
        return ref.at[self.layer, pl.ds(pl.multiple_of(start, 16), self.piece), self.columns_here]

    def start_turn(self, turn):
        def one(index):
            remote(
                self.block(self.terms, index, turn, True),
                self.block(self.arrived[turn], index, turn, True),
                *self.sems(turn),
                self.place.over_bit(self.order[turn]),
            ).start()

        self.loop(self.count(turn), one)

    def turn_bytes(self, turn):
        ref = self.terms.at[self.layer, pl.ds(0, self.count(turn) * self.piece), self.columns_here]
        return remote(ref, ref, *self.sems(turn), self.place.over_bit(self.order[turn]))

    def add(self, count, own, other, result):
        step = min(self.piece, self.mine.shape[1])
        per = self.piece // step
        total = count * per

        def part_of(make, index):
            ref = make(index // per)
            return ref.at[pl.ds(pl.multiple_of((index % per) * step, 16), step)]

        def slots(index):
            slot = index % 2
            rows, cols = pl.ds(0, step), pl.ds(0, self.size)
            return self.mine.at[slot, rows, cols], self.other.at[slot, rows, cols], slot

        def load(index):
            one, two, slot = slots(index)
            return (
                pltpu.make_async_copy(part_of(own, index), one, self.load_sem.at[slot, 0]),
                pltpu.make_async_copy(part_of(other, index), two, self.load_sem.at[slot, 1]),
            )

        def store(index):
            one, _, slot = slots(index)
            return pltpu.make_async_copy(one, part_of(result, index), self.store_sem.at[slot])

        def body(index, first, last):
            @when(jnp.logical_not(last) if not isinstance(last, bool) else not last)
            def _():
                @when(jnp.logical_not(first) if not isinstance(first, bool) else not first)
                def _():
                    store(index - 1).wait()

                for copy in load(index + 1):
                    copy.start()

            for copy in load(index):
                copy.wait()
            one, two, _ = slots(index)
            one[...] = (one[...].astype(wide) + two[...].astype(wide)).astype(low)
            store(index).start()

        for copy in load(0):
            copy.start()
        if total <= 4:
            for index in range(total):
                body(index, index == 0, index == total - 1)
        else:
            tiles(total, lambda index: body(index, index == 0, index == total - 1))
        if total > 1:
            store(total - 2).wait()
        store(total - 1).wait()

    def finish_turn(self, turn):
        self.turn_bytes(turn).wait_recv()
        self.add(
            self.count(turn),
            lambda index: self.block(self.terms, index, turn, False),
            lambda index: self.block(self.arrived[turn], index, turn, False),
            lambda index: self.block(self.terms, index, turn, False),
        )

    def own(self, which):
        start = self.row_of(self.place.pair, which)
        return self.terms.at[self.layer, pl.ds(pl.multiple_of(start, 16), self.piece), self.columns_here]

    def line(self, move, which):
        return self.lines.at[self.layer, move, pl.ds(which * self.piece, self.piece), self.columns_here]

    def final(self, which):
        return self.done.at[self.layer, pl.ds(which * self.piece, self.piece), self.columns_here]

    def roles(self, move):
        reps, half = self.dims.reps, self.dims.reps // 2
        if move < half - 1:
            return (move, reps - 1 - move), (move + 1, reps - 2 - move)
        if move == half - 1:
            return (half - 1, half), (half, half - 1)
        back = reps - 2 - move
        return (back + 1, reps - 2 - back), (back, reps - 1 - back)

    def move_copies(self, move, target):
        half = self.dims.reps // 2
        slot = self.dims.bits + move
        for which in range(self.pieces):
            src = self.own(which) if move < half else self.final(which)
            dst = self.line(move, which) if move < half else self.final(which)
            yield remote(src, dst, *self.sems(slot), (target, self.place.me))

    def move_bytes(self, move):
        slot = self.dims.bits + move
        ref = self.done.at[self.layer, pl.ds(0, self.pieces * self.piece), self.columns_here]
        return remote(ref, ref, *self.sems(slot), self.place.mate())

    def start_move(self, move):
        senders, receivers = self.roles(move)
        for sender, receiver in zip(senders, receivers):

            @pl.when(self.place.rep == sender)
            def _(receiver=receiver):
                for copy in self.move_copies(move, receiver):
                    copy.start()

    def finish_move(self, move):
        half = self.dims.reps // 2
        _, receivers = self.roles(move)

        @pl.when(jnp.logical_or(self.place.rep == receivers[0], self.place.rep == receivers[1]))
        def _():
            self.move_bytes(move).wait_recv()
            if move < half:
                self.add(
                    self.pieces,
                    self.own,
                    lambda which: self.line(move, which),
                    self.own if move < half - 1 else self.final,
                )

    def swap_copy(self):
        rows = self.done.at[
            self.layer,
            pl.ds(pl.multiple_of((1 - self.place.half) * self.rows, 16), self.rows),
            self.columns_here,
        ]
        return remote(
            rows,
            self.swapped.at[self.layer, pl.ds(0, self.rows), self.columns_here],
            *self.sems(self.dims.bits + self.moves),
            self.place.mate(),
        )

    def advance(self):
        bits = self.dims.bits
        if self.stage == 0:
            self.start_turn(0)
        elif self.stage < bits:
            self.finish_turn(self.stage - 1)
            self.start_turn(self.stage)
        elif self.stage == bits:
            self.finish_turn(bits - 1)
            self.start_move(0)
        elif self.stage < bits + self.moves:
            self.finish_move(self.stage - bits - 1)
            self.start_move(self.stage - bits)
        elif self.stage == bits + self.moves:
            self.finish_move(self.moves - 1)
            if self.paired:
                self.swap_copy().start()
        else:
            self.swap_copy().wait_recv()
        self.stage += 1

    def reach(self, stage):
        while self.stage < min(stage, self.stages):
            self.advance()

    def finish_sends(self):
        for turn in range(self.dims.bits):
            self.turn_bytes(turn).wait_send()
        for move in range(self.moves):
            senders, _ = self.roles(move)

            @pl.when(jnp.logical_or(self.place.rep == senders[0], self.place.rep == senders[1]))
            def _(move=move):
                self.move_bytes(move).wait_send()

        if self.paired:
            self.swap_copy().wait_send()


def when(condition):
    if isinstance(condition, bool):
        return (lambda body: body()) if condition else (lambda body: None)
    return pl.when(condition)


def in_plane_columns(dims, layer, kind):
    columns = dims.kinds[kind][2]
    if dims.reps % 2:
        return columns
    blocks = columns // 128
    return {12: 8, 8: 6, 16: 10}.get(blocks, blocks - blocks // 3) * 128


def gelu_and_slope(pre):
    cdf = 0.5 * (1.0 + lax.erf(pre * (1.0 / math.sqrt(2.0))))
    slope = cdf + pre * jnp.exp(-0.5 * pre * pre) * (1.0 / math.sqrt(2.0 * math.pi))
    return pre * cdf, slope


def dot_last(left, right):
    return lax.dot_general(left, right, (((1,), (1,)), ((), ())), preferred_element_type=wide)


def dot_first(left, right):
    return lax.dot_general(left, right, (((0,), (0,)), ((), ())), preferred_element_type=wide)


def tiles(count, body):
    def step(j, carry):
        body(j)
        return carry

    lax.fori_loop(0, count, step, 0)


def layers_kernel(dims, *refs):
    refs = iter(refs)

    def take(count):
        return [next(refs) for _ in range(count)]

    x_ref, cotangent, seg_row, seg_col, small = take(5)
    src_qkv, src_out, src_up, src_down = take(4)
    output, tops, vectors, input_grad = take(4)
    terms = take(4)
    arrived = [take(4) for _ in range(dims.bits)]
    lines, done = take(4), take(4)
    swapped = take(2)
    w_qkv, w_out, w_up, w_down = take(4)
    both_hidden, qkv, attended, probs, norm1, both_first, act, slope, norm2, rstd = take(10)
    hidden, first, total, away, back, bias, both_grad, ring, add_mine, add_other = take(10)
    seg_rows, seg_cols = take(2)
    gather_local, gather_send, gather_recv, mate_send, mate_recv = take(5)
    reduce_send, reduce_recv, load_sem, store_sem, ring_sem, io_sem = take(6)
    place = Place(dims)
    tokens, width = dims.tokens, dims.width
    heads_row = 128 // dims.head_dim
    scale = 1.0 / math.sqrt(dims.head_dim)

    barrier = pltpu.get_barrier_semaphore()
    others = [place.mate()] + [place.over_bit(bit) for bit in range(dims.bits)]
    reps = dims.reps
    groups = sorted({1 % reps, (reps - 1) % reps} - {0})
    others += [((place.rep + step) % reps, place.me) for step in groups]
    for other in others:
        pl.semaphore_signal(barrier, 1, device_id=other, device_id_type=MESH)
    pl.semaphore_wait(barrier, len(others))

    sources = (src_qkv, src_out, src_up, src_down)
    wholes = (w_qkv, w_out, w_up, w_down)
    gathers = [
        Gather(
            place,
            layer,
            kind,
            sources[kind],
            wholes[kind],
            (gather_local, gather_send, gather_recv),
            in_plane_columns(dims, layer, kind),
        )
        for layer in range(dims.layers)
        for kind in range(4)
    ]

    exchanges = []

    def to_mate(src, dst):
        at = len(exchanges)
        copy = remote(src, dst, mate_send.at[at], mate_recv.at[at], place.mate())
        copy.start()
        exchanges.append(copy)
        return copy

    rows_copy = to_mate(seg_row, seg_rows)
    cols_copy = to_mate(seg_col, seg_cols)
    x_copy = pltpu.make_async_copy(x_ref, both_hidden.at[0, pl.ds(0, tokens)], io_sem.at[0])
    cotangent_copy = pltpu.make_async_copy(cotangent, both_grad.at[pl.ds(0, tokens)], io_sem.at[1])
    x_copy.start()
    cotangent_copy.start()
    x_copy.wait()
    hidden_copy = to_mate(both_hidden.at[0, pl.ds(0, tokens)], both_hidden.at[0, pl.ds(tokens, tokens)])
    for gather in gathers:
        gather.begin()
    for gather in gathers[:3]:
        gather.reach(1)

    def prepare(at):
        for ahead in reversed(range(1, dims.bits + 2)):
            if at + ahead < len(gathers):
                gathers[at + ahead].reach(max(1, gathers[at + ahead].stages - ahead))
        gathers[at].reach(gathers[at].stages)

    hidden[...] = both_hidden[0, pl.ds(0, tokens)].astype(wide)
    vectors[...] = jnp.zeros(vectors.shape, wide)
    tops[...] = jnp.full(tops.shape, neg_large, wide)
    rows_copy.wait_recv()
    cols_copy.wait_recv()
    for s, (row_ref, col_ref) in enumerate(((seg_row, seg_col), (seg_rows, seg_cols))):
        same = col_ref[:, 0:1] == row_ref[0:1, :]
        bias[s] = jnp.where(same, 0.0, neg_large)

    chunk = 32 if tokens % 32 == 0 else tokens

    def layer_norm(residual, partial, other, bias_row, gain_row, shift_row, normed, rstd_out, results):
        def body(j):
            rows = pl.ds(pl.multiple_of(j * chunk, chunk), chunk)
            value = residual[rows] + partial[rows] + other[rows].astype(wide) + bias_row
            centred = value - jnp.mean(value, axis=-1, keepdims=True)
            scale_row = lax.rsqrt(jnp.mean(centred * centred, axis=-1, keepdims=True) + epsilon)
            normal = centred * scale_row
            normed[rows] = normal
            rstd_out[rows] = jnp.broadcast_to(scale_row, (chunk, 128))
            results(rows, normal * gain_row + shift_row)

        tiles(tokens // chunk, body)

    flying = [None, None]

    def project(left, product, at):
        slot = at % 2
        if flying[slot] is not None:
            flying[slot].wait_send()
            settled.append(flying[slot])

        def far(j):
            cols = pl.ds(pl.multiple_of(j * tile, tile), tile)
            away[slot, :, cols] = product(left[pl.ds(tokens, tokens)], cols).astype(low)

        def near(j):
            cols = pl.ds(pl.multiple_of(j * tile, tile), tile)
            total[:, cols] = product(left[pl.ds(0, tokens)], cols)

        tiles(width // tile, far)
        flying[slot] = to_mate(away.at[slot], back.at[at % (2 * dims.layers)])
        tiles(width // tile, near)
        return flying[slot]

    settled = []
    tile = min(512, width)
    for layer in range(dims.layers):
        prepare(4 * layer)
        hidden_copy.wait_recv()

        def qkv_tile(j, layer=layer):
            cols = pl.ds(pl.multiple_of(j * tile, tile), tile)
            value = jnp.dot(both_hidden[layer], w_qkv[layer, :, cols], preferred_element_type=wide)
            qkv[layer, :, cols] = (value + small[layer, 0:1, cols]).astype(low)

        tiles(dims.kinds[0][2] // tile, qkv_tile)
        lane_blocks = dims.third // 128

        def attend(j, layer=layer):
            s, block = j // lane_blocks, j % lane_blocks
            rows = pl.ds(pl.multiple_of(s * tokens, tokens), tokens)

            def lanes(which):
                start = pl.multiple_of(which * dims.third + block * 128, 128)
                return qkv[layer, rows, pl.ds(start, 128)]

            query, key_rows, value_rows = lanes(0), lanes(1), lanes(2)
            mask = bias[s]
            outs = []
            for e in range(heads_row):
                part = slice(e * dims.head_dim, (e + 1) * dims.head_dim)
                scores = dot_last(query[:, part], key_rows[:, part]) * scale + mask
                top = jnp.max(scores, axis=1, keepdims=True)
                expo = jnp.exp(scores - top)
                prob = (expo * (1.0 / jnp.sum(expo, axis=1, keepdims=True))).astype(low)
                head = block * heads_row + e
                probs[layer, s * (lane_blocks * heads_row) + head] = prob
                outs.append(jnp.dot(prob, value_rows[:, part], preferred_element_type=wide))
                peak = jnp.broadcast_to(jnp.max(top, axis=0, keepdims=True), (1, 128))
                tops[layer, pl.ds(head, 1)] = jnp.maximum(tops[layer, pl.ds(head, 1)], peak)
            attended[layer, rows, pl.ds(pl.multiple_of(block * 128, 128), 128)] = jnp.concatenate(
                outs, axis=1
            ).astype(low)

        tiles(2 * lane_blocks, attend)

        prepare(4 * layer + 1)
        project(
            attended.at[layer],
            lambda left, cols, layer=layer: jnp.dot(
                left, w_out[layer, :, cols], preferred_element_type=wide
            ),
            2 * layer,
        ).wait_recv()

        def first_rows(rows, value, layer=layer):
            first[rows] = value
            both_first[layer, rows] = value.astype(low)

        layer_norm(
            hidden,
            total,
            back.at[2 * layer],
            small[layer, 1:2, :width],
            small[layer, 4:5, :width],
            small[layer, 5:6, :width],
            norm1.at[layer],
            rstd.at[layer, 0],
            first_rows,
        )
        first_copy = to_mate(
            both_first.at[layer, pl.ds(0, tokens)], both_first.at[layer, pl.ds(tokens, tokens)]
        )

        prepare(4 * layer + 2)
        first_copy.wait_recv()
        narrow = 256

        def up_tile(j, layer=layer):
            cols = pl.ds(pl.multiple_of(j * narrow, narrow), narrow)
            pre = jnp.dot(both_first[layer], w_up[layer, :, cols], preferred_element_type=wide)
            value, steep = gelu_and_slope(pre + small[layer, 2:3, cols])
            act[layer, :, cols] = value.astype(low)
            slope[layer, :, cols] = steep.astype(low)

        tiles(dims.kinds[2][2] // narrow, up_tile)

        prepare(4 * layer + 3)
        project(
            act.at[layer],
            lambda left, cols, layer=layer: jnp.dot(
                left, w_down[layer, :, cols], preferred_element_type=wide
            ),
            2 * layer + 1,
        ).wait_recv()
        last = layer == dims.layers - 1

        def second_rows(rows, value, layer=layer, last=last):
            if last:
                output[rows] = value.astype(low)
            else:
                hidden[rows] = value
                both_hidden[layer + 1, rows] = value.astype(low)

        layer_norm(
            first,
            total,
            back.at[2 * layer + 1],
            small[layer, 3:4, :width],
            small[layer, 6:7, :width],
            small[layer, 7:8, :width],
            norm2.at[layer],
            rstd.at[layer, 1],
            second_rows,
        )
        if not last:
            hidden_copy = to_mate(
                both_hidden.at[layer + 1, pl.ds(0, tokens)],
                both_hidden.at[layer + 1, pl.ds(tokens, tokens)],
            )
    reduces = {
        (layer, kind): [
            Reduce(
                place,
                layer,
                kind,
                part,
                terms[kind],
                [arrived[turn][kind] for turn in range(dims.bits)],
                lines[kind],
                done[kind],
                swapped[kind // 2],
                (reduce_send, reduce_recv),
                (add_mine, add_other, load_sem, store_sem),
            )
            for part in range(2)
        ]
        for layer in range(dims.layers)
        for kind in range(4)
    }
    queue = [
        reduces[layer, kind] for layer in reversed(range(dims.layers)) for kind in (3, 2, 1, 0)
    ]
    stages = max(item.stages for pair in queue for item in pair)

    def pump(step, ahead=2):
        if step + ahead < len(queue):
            for item in queue[step + ahead]:
                item.reach(1)
        for behind in reversed(range(stages - 1)):
            at = step - behind
            if 0 <= at < len(queue):
                for item in queue[at]:
                    item.reach(2 + behind)

    def weight_terms(layer, kind, left, right):
        _, held, columns, _ = dims.kinds[kind]
        step = min(256, held)
        wide_cols = columns if columns <= ring.shape[2] else columns // 2
        across = columns // wide_cols
        count = (held // step) * across
        slots = ring.shape[0]

        def store(j):
            rows = pl.ds(pl.multiple_of((j // across) * step, step), step)
            cols = pl.ds(pl.multiple_of((j % across) * wide_cols, 128), wide_cols)
            return pltpu.make_async_copy(
                ring.at[j % slots, pl.ds(0, step), pl.ds(0, wide_cols)],
                terms[kind].at[layer, rows, cols],
                ring_sem.at[j % slots],
            )

        def body(j):
            @pl.when(j >= slots)
            def _():
                store(j - slots).wait()

            rows = pl.ds(pl.multiple_of((j // across) * step, step), step)
            cols = pl.ds(pl.multiple_of((j % across) * wide_cols, 128), wide_cols)
            ring[j % slots, pl.ds(0, step), pl.ds(0, wide_cols)] = dot_first(
                left[:, rows], right[:, cols]
            ).astype(low)
            store(j).start()

        tiles(count, body)
        for j in range(max(0, count - slots), count):
            store(j).wait()

    def count_up(layer, row, value, cols=None):
        cols = pl.ds(0, value.shape[1]) if cols is None else cols
        vectors[layer, pl.ds(row, 1), cols] += jnp.sum(value, axis=0, keepdims=True)

    def norm_grad(value, normed, scale_row, gain_row):
        grad = value * gain_row
        inner = jnp.mean(grad * normed, axis=-1, keepdims=True)
        return scale_row * (grad - jnp.mean(grad, axis=-1, keepdims=True) - normed * inner)

    def back_rows(j):
        return pl.ds(pl.multiple_of(j * chunk, chunk), chunk)

    grad_copy = None
    cotangent_copy.wait()
    pumped = 0
    for layer in reversed(range(dims.layers)):
        newest = layer == dims.layers - 1
        if grad_copy is not None:
            grad_copy.wait_send()
            settled.append(grad_copy)

        def second_back(j, layer=layer, newest=newest):
            rows = back_rows(j)
            value = both_grad[rows].astype(wide) if newest else hidden[rows]
            normed = norm2[layer, rows]
            count_up(layer, 7, value * normed)
            count_up(layer, 8, value)
            grad = norm_grad(value, normed, rstd[layer, 1, rows, 0:1], small[layer, 6:7, :width])
            first[rows] = grad
            rounded = grad.astype(low)
            both_grad[rows] = rounded
            count_up(layer, 4, rounded.astype(wide))

        tiles(tokens // chunk, second_back)
        grad_copy = to_mate(both_grad.at[pl.ds(0, tokens)], both_grad.at[pl.ds(tokens, tokens)])
        grad_copy.wait_recv()

        weight_terms(layer, 3, act.at[layer], both_grad)
        if newest:
            for item in queue[0]:
                item.reach(1)
        else:
            pump(pumped)
            pumped += 1

        def down_back(j, layer=layer):
            cols = pl.ds(pl.multiple_of(j * narrow, narrow), narrow)
            grad = dot_last(both_grad[...], w_down[layer, cols, :])
            rounded = (grad * slope[layer, :, cols].astype(wide)).astype(low)
            slope[layer, :, cols] = rounded
            count_up(layer, 3, rounded.astype(wide), cols)

        tiles(dims.hidden // 2 // narrow, down_back)
        weight_terms(layer, 2, both_first.at[layer], slope.at[layer])
        if newest:
            for item in queue[1]:
                item.reach(1)
        else:
            pump(pumped)
            pumped += 1
        exchange_at = 2 * (dims.layers - 1 - layer)
        project(
            slope.at[layer],
            lambda left, cols, layer=layer: dot_last(left, w_up[layer, cols, :]),
            2 * dims.layers + exchange_at,
        ).wait_recv()
        grad_copy.wait_send()
        settled.append(grad_copy)

        def first_back(j, layer=layer, exchange_at=exchange_at):
            rows = back_rows(j)
            value = first[rows] + total[rows] + back[exchange_at, rows].astype(wide)
            normed = norm1[layer, rows]
            count_up(layer, 5, value * normed)
            count_up(layer, 6, value)
            grad = norm_grad(value, normed, rstd[layer, 0, rows, 0:1], small[layer, 4:5, :width])
            first[rows] = grad
            rounded = grad.astype(low)
            both_grad[rows] = rounded
            count_up(layer, 2, rounded.astype(wide))

        tiles(tokens // chunk, first_back)
        grad_copy = to_mate(both_grad.at[pl.ds(0, tokens)], both_grad.at[pl.ds(tokens, tokens)])
        grad_copy.wait_recv()
        weight_terms(layer, 1, attended.at[layer], both_grad)

        out_tile = min(256, dims.third)

        def out_back(j, layer=layer):
            cols = pl.ds(pl.multiple_of(j * out_tile, out_tile), out_tile)
            attended[layer, :, cols] = dot_last(both_grad[...], w_out[layer, cols, :]).astype(low)

        tiles(dims.third // out_tile, out_back)
        if not newest:
            pump(pumped)
            pumped += 1

        def attend_back(j, layer=layer):
            s, block = j // lane_blocks, j % lane_blocks
            rows = pl.ds(pl.multiple_of(s * tokens, tokens), tokens)
            lanes = pl.ds(pl.multiple_of(block * 128, 128), 128)

            def at(which):
                return pl.ds(pl.multiple_of(which * dims.third + block * 128, 128), 128)

            query, key_rows, value_rows = (qkv[layer, rows, at(which)] for which in range(3))
            grad_out = attended[layer, rows, lanes]
            grads = [[], [], []]
            for e in range(heads_row):
                part = slice(e * dims.head_dim, (e + 1) * dims.head_dim)
                prob = probs[layer, s * (lane_blocks * heads_row) + block * heads_row + e]
                grads[2].append(dot_first(prob, grad_out[:, part]))
                prob = prob.astype(wide)
                grad_prob = dot_last(grad_out[:, part], value_rows[:, part])
                inner = jnp.sum(prob * grad_prob, axis=1, keepdims=True)
                grad_score = (prob * (grad_prob - inner)).astype(low)
                grads[0].append(
                    jnp.dot(grad_score, key_rows[:, part], preferred_element_type=wide) * scale
                )
                grads[1].append(dot_first(grad_score, query[:, part]) * scale)
            for which, row in ((0, 0), (1, None), (2, 1)):
                rounded = jnp.concatenate(grads[which], axis=1).astype(low)
                qkv[layer, rows, at(which)] = rounded
                if row is not None:
                    count_up(layer, row, rounded.astype(wide), lanes)

        tiles(2 * lane_blocks, attend_back)
        weight_terms(layer, 0, both_hidden.at[layer], qkv.at[layer])
        project(
            qkv.at[layer],
            lambda left, cols, layer=layer: dot_last(left, w_qkv[layer, cols, :]),
            2 * dims.layers + exchange_at + 1,
        ).wait_recv()

        def input_rows(j, exchange_at=exchange_at):
            rows = back_rows(j)
            hidden[rows] = first[rows] + total[rows] + back[exchange_at + 1, rows].astype(wide)

        tiles(tokens // chunk, input_rows)
        pump(pumped)
        pumped += 1

    grad_out_copy = pltpu.make_async_copy(hidden, input_grad, io_sem.at[0])
    grad_out_copy.start()
    while pumped < len(queue) + stages:
        pump(pumped)
        pumped += 1

    for copy in exchanges:
        if not any(copy is other for other in settled):
            copy.wait_send()
    for gather in gathers:
        gather.finish_sends()
    for pair in queue:
        for item in pair:
            item.finish_sends()
    grad_out_copy.wait()


def run_layers(dims, x, cotangent, segments, small, weights):
    layers, tokens, width = dims.layers, dims.tokens, dims.width
    both = 2 * tokens

    def shape(dims_of, dtype):
        return jax.ShapeDtypeStruct(dims_of, dtype)

    held = [shape((layers, rows, columns), low) for _, rows, columns, _ in dims.kinds]
    pair_rows = [rows * (2 if paired else 1) for rows, _, _, paired in dims.kinds]
    columns = [kind[2] for kind in dims.kinds]
    outs = (
        [
            shape((tokens, width), low),
            shape((layers, HEADS // 2, 128), wide),
            shape((layers, 16, dims.hidden // 2), wide),
            shape((tokens, width), wide),
        ]
        + held * (1 + dims.bits)
        + [shape((layers, dims.reps // 2, r, c), low) for r, c in zip(pair_rows, columns)]
        + [shape((layers, r, c), low) for r, c in zip(pair_rows, columns)]
        + [shape((layers, dims.rows, columns[kind]), low) for kind in (0, 2)]
    )
    seg = segments.astype(wide)
    seg_row = jnp.broadcast_to(seg, (8, tokens))
    seg_col = jnp.broadcast_to(seg.reshape(tokens, 1), (tokens, 128))
    vmem = pl.BlockSpec(memory_space=pltpu.VMEM)
    anywhere = pl.BlockSpec(memory_space=pl.ANY)
    dma = pltpu.SemaphoreType.DMA
    scratch = [pltpu.VMEM(item.shape, item.dtype) for item in held] + [
        pltpu.VMEM(*item)
        for item in (
            ((layers, both, width), low),
            ((layers, both, 3 * dims.third), low),
            ((layers, both, dims.third), low),
            ((layers, HEADS, tokens, tokens), low),
            ((layers, tokens, width), wide),
            ((layers, both, width), low),
            ((layers, both, dims.hidden // 2), low),
            ((layers, both, dims.hidden // 2), low),
            ((layers, tokens, width), wide),
            ((layers, 2, tokens, 128), wide),
            ((tokens, width), wide),
            ((tokens, width), wide),
            ((tokens, width), wide),
            ((2, tokens, width), low),
            ((2 * layers, tokens, width), low),
            ((2, tokens, tokens), wide),
            ((both, width), low),
            ((3, 256, 1024), low),
            ((2, 256, 1024), low),
            ((2, 256, 1024), low),
            ((8, tokens), wide),
            ((tokens, 128), wide),
        )
    ]
    slots = 2 + 2 * dims.bits
    exchange_count = 3 + 8 * layers
    reduce_slots = dims.bits + dims.reps
    scratch = scratch + [
        dma((4 * layers,)),
        dma((4 * layers, slots)),
        dma((4 * layers, slots)),
        dma((exchange_count,)),
        dma((exchange_count,)),
        dma((8 * layers, reduce_slots)),
        dma((8 * layers, reduce_slots)),
        dma((2, 2)),
        dma((2,)),
        dma((3,)),
        dma((2,)),
    ]
    return pl.pallas_call(
        functools.partial(layers_kernel, dims),
        out_shape=outs,
        in_specs=[anywhere] * 2 + [vmem] * 3 + [anywhere] * 4,
        out_specs=[vmem] * 3 + [anywhere] * (len(outs) - 3),
        scratch_shapes=scratch,
        compiler_params=pltpu.CompilerParams(
            collective_id=0, has_side_effects=True, vmem_limit_bytes=63 * 2**20 + 2**19
        ),
        name="layers",
    )(x, cotangent, seg_row, seg_col, small, *weights)


def shards(
    inputs,
    cotangent,
    segments,
    w_qkv,
    w_out,
    w_up,
    w_down,
    bias_query,
    bias_value,
    bias_out,
    bias_up,
    bias_down,
    norm1_gain,
    norm1_bias,
    norm2_gain,
    norm2_bias,
    tau,
    *,
    shard_count,
    rep_count,
):
    layer_count = w_qkv.shape[0]
    width = w_qkv.shape[2] // 3
    rows_here = bias_query.shape[1]
    head_dim = width // HEADS
    net = Net(shard_count, rep_count, max(1, head_dim // rows_here))

    vectors = (
        bias_query,
        bias_value,
        bias_out,
        bias_up,
        bias_down,
        norm1_gain,
        norm1_bias,
        norm2_gain,
        norm2_bias,
    )
    lengths = [vector.shape[1] // rows_here for vector in vectors]
    packed = jnp.concatenate(
        [vector.reshape(layer_count, -1, rows_here) for vector in vectors], axis=1
    )
    packed = net.in_order(packed, net.over_core(packed), net.core)
    packed = net.rows_in_order(net.gather_chips(packed, list(range(net.bits))))

    def whole(layer_index, member):
        start = sum(lengths[:member])
        return packed[:, layer_index, start : start + lengths[member]].astype(wide)

    def of_core(layer_index, member):
        split = whole(layer_index, member).reshape(net.high, 2, -1)
        return lax.dynamic_index_in_dim(split, net.core, 1, keepdims=False).reshape(-1)

    def small_of(layer_index):
        bias_q = of_core(layer_index, 0)
        bias_qkv = jnp.concatenate([bias_q, jnp.zeros_like(bias_q), of_core(layer_index, 1)])
        return (
            bias_qkv,
            whole(layer_index, 2).reshape(-1),
            of_core(layer_index, 3),
        ) + tuple(whole(layer_index, member).reshape(-1) for member in (4, 5, 6, 7, 8))

    tokens = inputs.shape[0]
    dims = Dims(shard_count, rep_count, net.step, layer_count, tokens, width, w_up.shape[2])

    def wide_row(row):
        return jnp.pad(row, (0, dims.hidden // 2 - row.shape[0]))

    small = jnp.stack(
        [jnp.stack([wide_row(row) for row in small_of(layer)]) for layer in range(layer_count)]
    )
    results = run_layers(
        dims,
        inputs,
        cotangent,
        segments,
        small,
        (by_half(w_qkv, net, 3), w_out, by_half(w_up, net, 1), w_down),
    )
    output, tops, vector_terms, input_grad = results[:4]
    done, swapped = results[-6:-2], results[-2:]

    local = tops[:, :, 0]
    local = net.in_order(local, net.over_core(local), net.core)
    local = local.reshape(2, layer_count, net.high, -1).transpose(1, 2, 0, 3).reshape(layer_count, HEADS)
    for bit in range(net.bits):
        local = jnp.maximum(local, net.over_bit(local, bit))
    step = 1
    while step < net.reps:
        local = jnp.maximum(
            local, lax.ppermute(local, "rep", [(i, i ^ step) for i in range(net.reps)])
        )
        step *= 2
    peak = local

    def own_rows(value):
        split = value.reshape(layer_count, 2, rows_here, value.shape[2])
        return lax.dynamic_index_in_dim(split, net.core, 1, keepdims=False)

    large = (
        whole_columns(own_rows(done[0]), swapped[0], net, 3),
        done[1].astype(wide),
        whole_columns(own_rows(done[2]), swapped[1], net, 1),
        done[3].astype(wide),
    )
    half_width, half_hidden = width // 2, dims.hidden // 2
    lengths_here = (half_width, half_width, width, half_hidden) + (width,) * 5
    terms_all = [
        [vector_terms[layer, row, :length] for row, length in enumerate(lengths_here)]
        for layer in range(layer_count)
    ]

    def placed(value, member):
        if member in (0, 1, 3):
            value = value.reshape(net.high, 1, net.step, lengths[member], rows_here)
            zero = jnp.zeros_like(value)
            first = net.core == 0
            return jnp.concatenate(
                [jnp.where(first, value, zero), jnp.where(first, zero, value)], axis=1
            )
        return value.reshape(net.high, 2, net.step, lengths[member], rows_here)

    terms = jnp.stack(
        [
            jnp.concatenate(
                [placed(value, member) for member, value in enumerate(terms_all[layer_index])], axis=3
            )
            for layer_index in range(layer_count)
        ],
        axis=3,
    )
    theirs = lax.dynamic_index_in_dim(terms, 1 - net.core, 1, keepdims=False)
    ours = lax.dynamic_index_in_dim(terms, net.core, 1, keepdims=False)
    terms = ours + net.over_core(theirs)
    terms = terms.reshape((net.pairs,) + terms.shape[2:])
    terms = net.sum_reps(net.scatter_chips(terms, list(range(net.bits))))
    vector_grads = []
    start = 0
    for length in lengths:
        vector_grads.append(terms[:, start : start + length].reshape(layer_count, -1))
        start += length

    factor = jnp.sqrt(tau / jnp.maximum(peak, tau))
    column_scale = jnp.repeat(factor, head_dim, axis=1)
    both_scale = jnp.concatenate([column_scale, column_scale], axis=1)
    clipped_qk = w_qkv[:, :, : 2 * width].astype(wide) * both_scale[:, None, :]
    start = lax.axis_index("shard") * rows_here
    scale_here = lax.dynamic_slice_in_dim(column_scale, start, rows_here, 1)
    clipped_bias_query = bias_query.astype(wide) * scale_here
    return (output, input_grad) + large + tuple(vector_grads) + (clipped_qk, clipped_bias_query)


def solution(mesh):
    tokens = P(("rep", "shard"), None)
    matrix = P(None, "shard", None)
    vector = P(None, "shard")
    in_specs = (tokens, tokens, tokens) + (matrix,) * 4 + (vector,) * 9 + (P(),)
    out_specs = (tokens, tokens) + (matrix,) * 4 + (vector,) * 9 + (matrix, vector)

    def local(*arrays):
        return shards(*arrays, shard_count=mesh.shape["shard"], rep_count=mesh.shape["rep"])

    return jax.shard_map(local, mesh=mesh, in_specs=in_specs, out_specs=out_specs, check_vma=False)
```

```python
import functools
import math

import jax
import jax.numpy as jnp
from jax import lax
from jax.experimental import pallas as pl
from jax.experimental.pallas import tpu as pltpu
from jax.sharding import PartitionSpec as P

HEADS = 16
MESH = pl.DeviceIdType.MESH
LEAD = 0


epsilon = 1e-05
neg_large = -1e30
low = jnp.bfloat16
wide = jnp.float32


class Net:
    def __init__(self, shards, reps, step):
        self.shards = shards
        self.reps = reps
        self.step = step
        self.pairs = shards // 2
        self.high = shards // (2 * step)
        self.bits = self.pairs.bit_length() - 1
        self.me = lax.axis_index("shard")
        self.core = (self.me // step) % 2
        self.rep = lax.axis_index("rep")

    def over_core(self, value):
        return lax.ppermute(value, "shard", [(i, i ^ self.step) for i in range(self.shards)])

    def stride(self, bit):
        return (1 << bit) if (1 << bit) < self.step else (2 << bit)

    def over_bit(self, value, bit):
        step = self.stride(bit)
        return lax.ppermute(value, "shard", [(i, i ^ step) for i in range(self.shards)])

    def chip_bit(self, bit):
        return (self.me // self.stride(bit)) % 2

    def rows_in_order(self, value):
        rest = value.shape[2:]
        value = value.reshape((self.high, self.step, 2) + rest)
        return jnp.swapaxes(value, 1, 2).reshape((self.shards,) + rest)

    def rows_by_pair(self, value):
        rest = value.shape[1:]
        value = value.reshape((self.high, 2, self.step) + rest)
        return jnp.swapaxes(value, 1, 2).reshape((self.pairs, 2) + rest)

    def in_order(self, mine, other, place):
        first = place == 0
        return jnp.stack([jnp.where(first, mine, other), jnp.where(first, other, mine)])

    def gather_chips(self, piece, order):
        shape = piece.shape
        for bit in order:
            piece = self.in_order(piece, self.over_bit(piece, bit), self.chip_bit(bit))
        axes = list(reversed(order))
        natural = [axes.index(bit) for bit in reversed(range(self.bits))]
        rest = list(range(self.bits, self.bits + len(shape)))
        return piece.transpose(natural + rest).reshape((self.pairs,) + shape)

    def scatter_chips(self, value, order):
        rest = value.shape[1:]
        value = value.reshape((2,) * self.bits + rest)
        left = list(reversed(range(self.bits)))
        for bit in order:
            axis = left.index(bit)
            place = self.chip_bit(bit)
            theirs = lax.dynamic_index_in_dim(value, 1 - place, axis, keepdims=False)
            ours = lax.dynamic_index_in_dim(value, place, axis, keepdims=False)
            got = self.over_bit(theirs, bit)
            value = (ours.astype(wide) + got.astype(wide)).astype(value.dtype)
            left.remove(bit)
        return value

    def sum_reps(self, value):
        reps, half = self.reps, self.reps // 2

        def add(one, other):
            return (one.astype(wide) + other.astype(wide)).astype(value.dtype)

        total = value
        for i in range(half - 1):
            got = lax.ppermute(total, "rep", [(i, i + 1), (reps - 1 - i, reps - 2 - i)])
            total = add(total, got)
        total = add(total, lax.ppermute(total, "rep", [(half - 1, half), (half, half - 1)]))
        for i in reversed(range(half - 1)):
            got = lax.ppermute(total, "rep", [(i + 1, i), (reps - 2 - i, reps - 1 - i)])
            outer = jnp.logical_or(self.rep == i, self.rep == reps - 1 - i)
            total = jnp.where(outer, got, total)
        return total


def by_half(weight, net, groups):
    layers, rows, columns = weight.shape
    split = weight.reshape(layers, rows, groups * net.high, 2, columns // (2 * groups * net.high))
    return split.transpose(0, 3, 1, 2, 4).reshape(layers, 2, rows, columns // 2)


def whole_columns(mine, other, net, groups):
    layers, rows, columns = mine.shape
    block = columns // (groups * net.high)
    both = [part.reshape(layers, rows, groups * net.high, block) for part in (mine, other)]
    first = net.core == 0
    stacked = jnp.stack(
        [jnp.where(first, both[0], both[1]), jnp.where(first, both[1], both[0])], axis=3
    )
    return stacked.reshape(layers, rows, 2 * columns).astype(wide)


class Place:
    def __init__(self, dims):
        self.dims = dims
        step = dims.step
        self.rep = lax.axis_index("rep")
        self.me = lax.axis_index("shard")
        self.half = (self.me // step) % 2
        self.pair = (self.me // (2 * step)) * step + self.me % step
        self.plane = self.rep % 2

    def flip(self, value, bit):
        size = 1 << bit
        return value + size * (1 - 2 * ((value // size) % 2))

    def mate(self):
        return (self.rep, self.me + self.dims.step * (1 - 2 * self.half))

    def over_bit(self, bit):
        stride = (1 << bit) if (1 << bit) < self.dims.step else (2 << bit)
        return (self.rep, self.me + stride * (1 - 2 * ((self.me // stride) % 2)))

    def over_plane(self):
        return (self.rep + 1 - 2 * self.plane, self.me)

    def first_shard(self, pair):
        step = self.dims.step
        return (pair // step) * (2 * step) + pair % step


class Dims:
    def __init__(self, shards, reps, step, layers, tokens, width, hidden):
        self.shards, self.reps, self.step = shards, reps, step
        self.pairs = shards // 2
        self.bits = self.pairs.bit_length() - 1
        self.layers, self.tokens, self.width, self.hidden = layers, tokens, width, hidden
        self.head_dim = width // HEADS
        self.third = width // 2
        self.rows = width // shards
        self.kinds = (
            (self.rows, width, 3 * width // 2, True),
            (self.rows, width // 2, width, False),
            (self.rows, width, hidden // 2, True),
            (hidden // shards, hidden // 2, width, False),
        )
        high = shards // (2 * step)
        self.block = (width // (2 * high), None, hidden // (2 * high), None)
        self.blocks = (3 * high, None, high, None)
        self.lengths = (1, 1, 1, hidden // width, 1, 1, 1, 1, 1)
        self.vector_rows = layers * sum(self.lengths)
        self.direct = self.rows % 128 == 0 and step == 1


def remote(src, dst, send, recv, where):
    return pltpu.make_async_remote_copy(
        src_ref=src, dst_ref=dst, send_sem=send, recv_sem=recv, device_id=where, device_id_type=MESH
    )


class Gather:
    def __init__(self, place, layer, kind, source, whole, sems, in_plane):
        self.place, self.dims = place, place.dims
        self.layer, self.kind = layer, kind
        self.source, self.whole = source, whole
        self.rows, self.held, self.columns, self.paired = self.dims.kinds[kind]
        self.local, self.send, self.recv = sems
        self.at = layer * 4 + kind
        self.in_plane = in_plane
        self.stage = 0
        self.stages = self.dims.bits + (2 if in_plane < self.columns else 1)

    def blocks(self, pair):
        if not self.paired:
            return [pair * self.rows], self.rows
        first = self.place.first_shard(pair) * self.rows
        if self.dims.step == 1:
            return [first], 2 * self.rows
        return [first, first + self.dims.step * self.rows], self.rows

    def window(self, part):
        size = self.in_plane // 2
        if (size % 128) and part < 2:
            low_size = size // 128 * 128
            size = low_size if part == 0 else self.in_plane - low_size
            offset = 0 if part == 0 else low_size
        else:
            offset = part * size
        start = self.place.plane * (self.columns - self.in_plane) + offset
        return pl.ds(pl.multiple_of(start, 128), size), size

    def order(self, part):
        bits = list(range(self.dims.bits))
        return bits if part == 0 else bits[::-1]

    def subset(self, done):
        pairs = [self.place.pair]
        for bit in done:
            pairs = pairs + [self.place.flip(pair, bit) for pair in pairs]
        return pairs

    def begin(self):
        place = self.place
        if self.paired:
            mine = place.me * self.rows
            rows = pl.ds(pl.multiple_of(mine, 16), self.rows)
            for theirs, ours in self.begin_blocks():
                pltpu.make_async_copy(
                    ours, self.whole.at[self.layer, rows, theirs[1]], self.local.at[self.at]
                ).start()
            for theirs, ours in self.begin_blocks():
                remote(
                    theirs[0],
                    self.whole.at[self.layer, rows, theirs[1]],
                    self.send.at[self.at, 0],
                    self.recv.at[self.at, 0],
                    place.mate(),
                ).start()
        else:
            rows = pl.ds(pl.multiple_of(place.pair * self.rows, 16), self.rows)
            pltpu.make_async_copy(
                self.source.at[self.layer], self.whole.at[self.layer, rows], self.local.at[self.at]
            ).start()

    def begin_blocks(self):
        place, width = self.place, self.dims.block[self.kind]
        if not self.dims.direct:
            every = pl.ds(0, self.columns)
            yield (
                (self.source.at[self.layer, 1 - place.half], every),
                self.source.at[self.layer, place.half],
            )
            return
        for block in range(self.dims.blocks[self.kind]):
            to = pl.ds(block * width, width)
            starts = [(2 * block + half) * width for half in (1 - place.half, place.half)]
            theirs, ours = (
                self.source.at[self.layer, :, pl.ds(pl.multiple_of(start, 128), width)] for start in starts
            )
            yield (theirs, to), ours

    def some(self, rows, columns):
        return self.whole.at[self.layer, pl.ds(0, rows), columns]

    def phase(self, turn):
        place = self.place
        for part in range(2):
            order = self.order(part)
            columns, _ = self.window(part)
            for pair in self.subset(order[:turn]):
                starts, count = self.blocks(pair)
                for start in starts:
                    block = self.whole.at[self.layer, pl.ds(pl.multiple_of(start, 16), count), columns]
                    remote(
                        block,
                        block,
                        self.send.at[self.at, 1 + 2 * turn + part],
                        self.recv.at[self.at, 1 + 2 * turn + part],
                        place.over_bit(order[turn]),
                    ).start()

    def phase_bytes(self, turn, part):
        columns = pl.ds(0, self.window(part)[1])
        per_pair = self.rows * (2 if self.paired else 1)
        block = self.some(per_pair << turn, columns)
        at = 1 + 2 * turn + part
        return remote(block, block, self.send.at[self.at, at], self.recv.at[self.at, at], self.place.mate())

    def across(self):
        place = self.place
        size = self.columns - self.in_plane
        columns = pl.ds(pl.multiple_of(place.plane * self.in_plane, 128), size)
        at = 1 + 2 * self.dims.bits
        for pair in self.subset(range(self.dims.bits))[1:]:
            starts, count = self.blocks(pair)
            for start in starts:
                block = self.whole.at[self.layer, pl.ds(pl.multiple_of(start, 16), count), columns]
                remote(block, block, self.send.at[self.at, at], self.recv.at[self.at, at], place.over_plane()).start()

    def across_bytes(self):
        per_pair = self.rows * (2 if self.paired else 1)
        block = self.some(per_pair * (self.dims.pairs - 1), pl.ds(0, self.columns - self.in_plane))
        at = 1 + 2 * self.dims.bits
        return remote(block, block, self.send.at[self.at, at], self.recv.at[self.at, at], self.place.over_plane())

    def own_bytes(self):
        if not self.paired:
            return None
        block = self.some(self.rows, pl.ds(0, self.columns))
        return remote(block, block, self.send.at[self.at, 0], self.recv.at[self.at, 0], self.place.mate())

    def advance(self):
        if self.stage == 0:
            own = self.some(self.rows, pl.ds(0, self.columns))
            pltpu.make_async_copy(own, own, self.local.at[self.at]).wait()
            if self.paired:
                self.own_bytes().wait_recv()
        elif self.stage <= self.dims.bits:
            for part in range(2):
                self.phase_bytes(self.stage - 1, part).wait_recv()
        else:
            self.across_bytes().wait_recv()
        if self.stage < self.dims.bits:
            self.phase(self.stage)
        elif self.stage + 1 < self.stages:
            self.across()
        self.stage += 1

    def reach(self, stage):
        while self.stage < min(stage, self.stages):
            self.advance()

    def finish_sends(self):
        if self.paired:
            self.own_bytes().wait_send()
        for turn in range(self.dims.bits):
            for part in range(2):
                self.phase_bytes(turn, part).wait_send()
        if self.in_plane < self.columns:
            self.across_bytes().wait_send()


class Reduce:
    def __init__(self, place, layer, kind, part, terms, arrived, lines, done, swapped, sems, bufs):
        self.place, self.dims = place, place.dims
        self.layer, self.kind, self.part = layer, kind, part
        self.terms, self.arrived, self.lines, self.done, self.swapped = terms, arrived, lines, done, swapped
        self.send, self.recv, self.own_sem = sems
        self.mine, self.other, self.load_sem, self.store_sem = bufs
        self.rows, self.held, self.columns, self.paired = self.dims.kinds[kind]
        self.size = self.columns // 2
        self.columns_here = pl.ds(part * self.size, self.size)
        self.at = (layer * 4 + kind) * 2 + part
        bits = list(range(self.dims.bits))
        self.order = bits if part == 0 else bits[::-1]
        self.moves = self.dims.reps - 1
        self.stage = 0
        self.stages = 1 + self.dims.bits + self.moves + (1 if self.paired else 0)
        self.split = self.paired and self.dims.step > 1
        self.piece = self.rows * (2 if self.paired and not self.split else 1)
        self.pieces = 2 if self.split else 1

    def row_of(self, pair, which):
        if not self.paired:
            return pair * self.rows
        return (self.place.first_shard(pair) + which * self.dims.step) * self.rows

    def sems(self, slot):
        return self.send.at[self.at, slot], self.recv.at[self.at, slot]

    def kept(self, index, turn, away):
        pair = self.place.pair
        for i, bit in enumerate(self.order[turn + 1 :]):
            size = 1 << bit
            wanted = (index // (1 << i)) % 2
            pair = pair + size * (wanted - (self.place.pair // size) % 2)
        if away:
            pair = self.place.flip(pair, self.order[turn])
        return pair

    def count(self, turn):
        return (self.dims.pairs >> (turn + 1)) * self.pieces

    def loop(self, count, body):
        if count <= 4:
            for i in range(count):
                body(i)
        else:
            tiles(count, body)

    def block(self, ref, index, turn, away):
        pair = self.kept(index // self.pieces, turn, away)
        start = self.row_of(pair, index % self.pieces)
        return ref.at[self.layer, pl.ds(pl.multiple_of(start, 16), self.piece), self.columns_here]

    def start_turn(self, turn):
        def one(index):
            remote(
                self.block(self.terms, index, turn, True),
                self.block(self.arrived[turn], index, turn, True),
                *self.sems(turn),
                self.place.over_bit(self.order[turn]),
            ).start()

        self.loop(self.count(turn), one)

    def turn_bytes(self, turn):
        ref = self.terms.at[self.layer, pl.ds(0, self.count(turn) * self.piece), self.columns_here]
        return remote(ref, ref, *self.sems(turn), self.place.over_bit(self.order[turn]))

    def add(self, count, own, other, result):
        step = min(self.piece, self.mine.shape[1])
        per = self.piece // step
        total = count * per

        def part_of(make, index):
            ref = make(index // per)
            return ref.at[pl.ds(pl.multiple_of((index % per) * step, 16), step)]

        def slots(index):
            slot = index % 2
            rows, cols = pl.ds(0, step), pl.ds(0, self.size)
            return self.mine.at[slot, rows, cols], self.other.at[slot, rows, cols], slot

        def load(index):
            one, two, slot = slots(index)
            return (
                pltpu.make_async_copy(part_of(own, index), one, self.load_sem.at[slot, 0]),
                pltpu.make_async_copy(part_of(other, index), two, self.load_sem.at[slot, 1]),
            )

        def store(index):
            one, _, slot = slots(index)
            return pltpu.make_async_copy(one, part_of(result, index), self.store_sem.at[slot])

        def body(index, first, last):
            @when(jnp.logical_not(last) if not isinstance(last, bool) else not last)
            def _():
                @when(jnp.logical_not(first) if not isinstance(first, bool) else not first)
                def _():
                    store(index - 1).wait()

                for copy in load(index + 1):
                    copy.start()

            for copy in load(index):
                copy.wait()
            one, two, _ = slots(index)
            one[...] = (one[...].astype(wide) + two[...].astype(wide)).astype(low)
            store(index).start()

        for copy in load(0):
            copy.start()
        if total <= 4:
            for index in range(total):
                body(index, index == 0, index == total - 1)
        else:
            tiles(total, lambda index: body(index, index == 0, index == total - 1))
        if total > 1:
            store(total - 2).wait()
        store(total - 1).wait()

    def finish_turn(self, turn):
        self.turn_bytes(turn).wait_recv()
        self.add(
            self.count(turn),
            lambda index: self.block(self.terms, index, turn, False),
            lambda index: self.block(self.arrived[turn], index, turn, False),
            lambda index: self.block(self.terms, index, turn, False),
        )

    def own(self, which):
        start = self.row_of(self.place.pair, which)
        return self.terms.at[self.layer, pl.ds(pl.multiple_of(start, 16), self.piece), self.columns_here]

    def line(self, move, which):
        return self.lines.at[self.layer, move, pl.ds(which * self.piece, self.piece), self.columns_here]

    def final(self, which):
        return self.done.at[self.layer, pl.ds(which * self.piece, self.piece), self.columns_here]

    def roles(self, move):
        reps, half = self.dims.reps, self.dims.reps // 2
        if move < half - 1:
            return (move, reps - 1 - move), (move + 1, reps - 2 - move)
        if move == half - 1:
            return (half - 1, half), (half, half - 1)
        back = reps - 2 - move
        return (back + 1, reps - 2 - back), (back, reps - 1 - back)

    def move_copies(self, move, target):
        half = self.dims.reps // 2
        slot = self.dims.bits + move
        for which in range(self.pieces):
            src = self.own(which) if move < half else self.final(which)
            dst = self.line(move, which) if move < half else self.final(which)
            yield remote(src, dst, *self.sems(slot), (target, self.place.me))

    def move_bytes(self, move):
        slot = self.dims.bits + move
        ref = self.done.at[self.layer, pl.ds(0, self.pieces * self.piece), self.columns_here]
        return remote(ref, ref, *self.sems(slot), self.place.mate())

    def start_move(self, move):
        senders, receivers = self.roles(move)
        for sender, receiver in zip(senders, receivers):

            @pl.when(self.place.rep == sender)
            def _(receiver=receiver):
                for copy in self.move_copies(move, receiver):
                    copy.start()

    def finish_move(self, move):
        half = self.dims.reps // 2
        _, receivers = self.roles(move)

        @pl.when(jnp.logical_or(self.place.rep == receivers[0], self.place.rep == receivers[1]))
        def _():
            self.move_bytes(move).wait_recv()
            if move < half:
                self.add(
                    self.pieces,
                    self.own,
                    lambda which: self.line(move, which),
                    self.own if move < half - 1 else self.final,
                )

    def part_blocks(self):
        width = self.dims.block[self.kind]
        count = self.dims.blocks[self.kind] // 2
        for block in range(self.part * count, (self.part + 1) * count):
            place = (2 * block + self.place.half) * width
            yield pl.ds(block * width, width), pl.ds(pl.multiple_of(place, 128), width)

    def rows_done(self, half, columns):
        start = pl.multiple_of(half * self.rows, 16)
        return self.done.at[self.layer, pl.ds(start, self.rows), columns]

    def start_swap(self):
        slot = self.sems(self.dims.bits + self.moves)
        if not self.dims.direct:
            remote(
                self.rows_done(1 - self.place.half, self.columns_here),
                self.swapped.at[self.layer, pl.ds(0, self.rows), self.columns_here],
                *slot,
                self.place.mate(),
            ).start()
            return
        for here, there in self.part_blocks():
            remote(
                self.rows_done(1 - self.place.half, here),
                self.swapped.at[self.layer, pl.ds(0, self.rows), there],
                *slot,
                self.place.mate(),
            ).start()
        for here, there in self.part_blocks():
            pltpu.make_async_copy(
                self.rows_done(self.place.half, here),
                self.swapped.at[self.layer, pl.ds(0, self.rows), there],
                self.own_sem.at[self.at],
            ).start()

    def swap_bytes(self):
        ref = self.done.at[self.layer, pl.ds(0, self.rows), self.columns_here]
        return remote(ref, ref, *self.sems(self.dims.bits + self.moves), self.place.mate())

    def finish_swap(self):
        self.swap_bytes().wait_recv()
        if self.dims.direct:
            ref = self.done.at[self.layer, pl.ds(0, self.rows), self.columns_here]
            pltpu.make_async_copy(ref, ref, self.own_sem.at[self.at]).wait()

    def advance(self):
        bits = self.dims.bits
        if self.stage == 0:
            self.start_turn(0)
        elif self.stage < bits:
            self.finish_turn(self.stage - 1)
            self.start_turn(self.stage)
        elif self.stage == bits:
            self.finish_turn(bits - 1)
            self.start_move(0)
        elif self.stage < bits + self.moves:
            self.finish_move(self.stage - bits - 1)
            self.start_move(self.stage - bits)
        elif self.stage == bits + self.moves:
            self.finish_move(self.moves - 1)
            if self.paired:
                self.start_swap()
        else:
            self.finish_swap()
        self.stage += 1

    def reach(self, stage):
        while self.stage < min(stage, self.stages):
            self.advance()

    def finish_sends(self):
        for turn in range(self.dims.bits):
            self.turn_bytes(turn).wait_send()
        for move in range(self.moves):
            senders, _ = self.roles(move)

            @pl.when(jnp.logical_or(self.place.rep == senders[0], self.place.rep == senders[1]))
            def _(move=move):
                self.move_bytes(move).wait_send()

        if self.paired:
            self.swap_bytes().wait_send()


def when(condition):
    if isinstance(condition, bool):
        return (lambda body: body()) if condition else (lambda body: None)
    return pl.when(condition)


def in_plane_columns(dims, layer, kind):
    columns = dims.kinds[kind][2]
    if dims.reps % 2:
        return columns
    blocks = columns // 128
    return {12: 8, 8: 6, 16: 10}.get(blocks, blocks - blocks // 3) * 128


def few(count, body):
    if count <= 8:
        for index in range(count):
            body(index)
    else:
        tiles(count, body)


def gelu_and_slope(pre):
    cdf = 0.5 * (1.0 + lax.erf(pre * (1.0 / math.sqrt(2.0))))
    slope = cdf + pre * jnp.exp(-0.5 * pre * pre) * (1.0 / math.sqrt(2.0 * math.pi))
    return pre * cdf, slope


def dot_last(left, right):
    return lax.dot_general(left, right, (((1,), (1,)), ((), ())), preferred_element_type=wide)


def dot_first(left, right):
    return lax.dot_general(left, right, (((0,), (0,)), ((), ())), preferred_element_type=wide)


def tiles(count, body):
    def step(j, carry):
        body(j)
        return carry

    lax.fori_loop(0, count, step, 0)


def layers_kernel(dims, *refs):
    refs = iter(refs)

    def take(count):
        return [next(refs) for _ in range(count)]

    x_ref, cotangent, seg_row, vector_ref = take(4)
    src_qkv, src_out, src_up, src_down = take(4)
    output, tops, vectors, input_grad = take(4)
    vector_out, peak_out = take(2) if dims.direct else (None, None)
    terms = take(4)
    arrived = [take(4) for _ in range(dims.bits)]
    lines, done = take(4), take(4)
    swapped = take(2)
    w_qkv, w_out, w_up, w_down = take(4)
    both_hidden, qkv, attended, probs, norm1, both_first, act, slope, norm2, rstd = take(10)
    hidden, first, total, away, back, bias, both_grad, ring, add_mine, add_other = take(10)
    seg_here, seg_rows = take(2)
    if dims.direct:
        vector_all, small, vector_away, vector_back, line_back = take(5)
    else:
        small = vector_ref
    gather_local, gather_send, gather_recv, mate_send, mate_recv = take(5)
    reduce_send, reduce_recv, own_sem, load_sem, store_sem, ring_sem, io_sem = take(7)
    if dims.direct:
        vector_send, vector_recv = take(2)
    place = Place(dims)
    tokens, width = dims.tokens, dims.width
    heads_row = 128 // dims.head_dim
    scale = 1.0 / math.sqrt(dims.head_dim)

    barrier = pltpu.get_barrier_semaphore()
    reps, shards = dims.reps, dims.shards

    def in_group(step):
        return place.rep, (place.me + step) % shards

    def greet(step):
        pl.semaphore_signal(barrier, 1, device_id=in_group(step), device_id_type=MESH)

    few(shards - 1, lambda index: greet(index + 1))
    for step in range(1, reps):
        line = (place.rep + step) % reps, place.me
        pl.semaphore_signal(barrier, 1, device_id=line, device_id_type=MESH)
    pl.semaphore_wait(barrier, shards + reps - 2)

    sources = (src_qkv, src_out, src_up, src_down)
    wholes = (w_qkv, w_out, w_up, w_down)
    gathers = [
        Gather(
            place,
            layer,
            kind,
            sources[kind],
            wholes[kind],
            (gather_local, gather_send, gather_recv),
            in_plane_columns(dims, layer, kind),
        )
        for layer in range(dims.layers)
        for kind in range(4)
    ]

    exchanges = []

    def to_mate(src, dst):
        at = len(exchanges)
        copy = remote(src, dst, mate_send.at[at], mate_recv.at[at], place.mate())
        copy.start()
        exchanges.append(copy)
        return copy

    seg_here[...] = jnp.broadcast_to(seg_row[...].astype(wide), seg_here.shape)
    rows_copy = to_mate(seg_here, seg_rows)

    def vector_bytes(buffer, slot, count):
        ref = buffer.at[pl.ds(0, count)]
        return remote(ref, ref, vector_send.at[slot], vector_recv.at[slot], place.mate())

    if dims.direct:

        def send_vector(index):
            remote(
                vector_ref,
                vector_all.at[place.me],
                vector_send.at[0],
                vector_recv.at[0],
                in_group(index + 1),
            ).start()

        vector_all[place.me] = vector_ref[...]
        few(shards - 1, send_vector)
    x_copy = pltpu.make_async_copy(x_ref, both_hidden.at[0, pl.ds(0, tokens)], io_sem.at[0])
    cotangent_copy = pltpu.make_async_copy(cotangent, both_grad.at[pl.ds(0, tokens)], io_sem.at[1])
    x_copy.start()
    cotangent_copy.start()
    x_copy.wait()
    hidden_copy = to_mate(both_hidden.at[0, pl.ds(0, tokens)], both_hidden.at[0, pl.ds(tokens, tokens)])
    for gather in gathers:
        gather.begin()
    turns = []

    def prepare(at):
        while len(turns) < at + gathers[at].stages:
            now = len(turns)
            turns.append(now)
            for number, gather in enumerate(gathers):
                gather.reach(max(now - number + 1, 1 if number <= now + LEAD else 0))

    hidden[...] = both_hidden[0, pl.ds(0, tokens)].astype(wide)
    vectors[...] = jnp.zeros(vectors.shape, wide)
    tops[...] = jnp.full(tops.shape, neg_large, wide)
    rows_copy.wait_recv()
    for s, row_ref in enumerate((seg_here, seg_rows)):
        row = row_ref[0:1, :]
        column = jnp.broadcast_to(row, (128, tokens)).T[:, 0:1]
        bias[s] = jnp.where(column == row, 0.0, neg_large)

    if dims.direct:
        vector_bytes(vector_all, 0, shards - 1).wait_recv()
        starts = [sum(dims.lengths[:member]) for member in range(9)]
        small[...] = jnp.zeros(small.shape, wide)
        for layer in range(dims.layers):
            base = layer * sum(dims.lengths)

            def spread(row, member, shard, at, layer=layer, base=base):
                for block in range(dims.lengths[member]):
                    lanes = pl.ds(at + block * dims.rows, dims.rows)
                    source = base + starts[member] + block
                    small[layer, row : row + 1, lanes] = vector_all[shard, source : source + 1, :]

            for shard in range(shards):
                for row, member in ((1, 2), (3, 4), (4, 5), (5, 6), (6, 7), (7, 8)):
                    spread(row, member, shard, shard * dims.rows)
            for pair in range(dims.pairs):
                shard = 2 * pair + place.half
                spread(0, 0, shard, pair * dims.rows)
                spread(0, 1, shard, 2 * dims.third + pair * dims.rows)
                spread(2, 3, shard, pair * dims.rows * dims.lengths[3])

    chunk = 32 if tokens % 32 == 0 else tokens

    def layer_norm(residual, partial, other, bias_row, gain_row, shift_row, normed, rstd_out, results):
        def body(j):
            rows = pl.ds(pl.multiple_of(j * chunk, chunk), chunk)
            value = residual[rows] + partial[rows] + other[rows].astype(wide) + bias_row
            centred = value - jnp.mean(value, axis=-1, keepdims=True)
            scale_row = lax.rsqrt(jnp.mean(centred * centred, axis=-1, keepdims=True) + epsilon)
            normal = centred * scale_row
            normed[rows] = normal
            rstd_out[rows] = jnp.broadcast_to(scale_row, (chunk, 128))
            results(rows, normal * gain_row + shift_row)

        tiles(tokens // chunk, body)

    flying = [None, None]

    def project(left, product, at):
        slot = at % 2
        if flying[slot] is not None:
            flying[slot].wait_send()
            settled.append(flying[slot])

        def far(j):
            cols = pl.ds(pl.multiple_of(j * tile, tile), tile)
            away[slot, :, cols] = product(left[pl.ds(tokens, tokens)], cols).astype(low)

        def near(j):
            cols = pl.ds(pl.multiple_of(j * tile, tile), tile)
            total[:, cols] = product(left[pl.ds(0, tokens)], cols)

        tiles(width // tile, far)
        flying[slot] = to_mate(away.at[slot], back.at[at % (2 * dims.layers)])
        tiles(width // tile, near)
        return flying[slot]

    settled = []
    tile = min(512, width)
    for layer in range(dims.layers):
        prepare(4 * layer)
        hidden_copy.wait_recv()

        def qkv_tile(j, layer=layer):
            cols = pl.ds(pl.multiple_of(j * tile, tile), tile)
            value = jnp.dot(both_hidden[layer], w_qkv[layer, :, cols], preferred_element_type=wide)
            qkv[layer, :, cols] = (value + small[layer, 0:1, cols]).astype(low)

        tiles(dims.kinds[0][2] // tile, qkv_tile)
        lane_blocks = dims.third // 128

        def attend(j, layer=layer):
            s, block = j // lane_blocks, j % lane_blocks
            rows = pl.ds(pl.multiple_of(s * tokens, tokens), tokens)

            def lanes(which):
                start = pl.multiple_of(which * dims.third + block * 128, 128)
                return qkv[layer, rows, pl.ds(start, 128)]

            query, key_rows, value_rows = lanes(0), lanes(1), lanes(2)
            mask = bias[s]
            outs = []
            for e in range(heads_row):
                part = slice(e * dims.head_dim, (e + 1) * dims.head_dim)
                scores = dot_last(query[:, part], key_rows[:, part]) * scale + mask
                top = jnp.max(scores, axis=1, keepdims=True)
                expo = jnp.exp(scores - top)
                prob = (expo * (1.0 / jnp.sum(expo, axis=1, keepdims=True))).astype(low)
                head = block * heads_row + e
                probs[layer, s * (lane_blocks * heads_row) + head] = prob
                outs.append(jnp.dot(prob, value_rows[:, part], preferred_element_type=wide))
                peak = jnp.broadcast_to(jnp.max(top, axis=0, keepdims=True), (1, 128))
                tops[layer, pl.ds(head, 1)] = jnp.maximum(tops[layer, pl.ds(head, 1)], peak)
            attended[layer, rows, pl.ds(pl.multiple_of(block * 128, 128), 128)] = jnp.concatenate(
                outs, axis=1
            ).astype(low)

        tiles(2 * lane_blocks, attend)

        prepare(4 * layer + 1)
        project(
            attended.at[layer],
            lambda left, cols, layer=layer: jnp.dot(
                left, w_out[layer, :, cols], preferred_element_type=wide
            ),
            2 * layer,
        ).wait_recv()

        def first_rows(rows, value, layer=layer):
            first[rows] = value
            both_first[layer, rows] = value.astype(low)

        layer_norm(
            hidden,
            total,
            back.at[2 * layer],
            small[layer, 1:2, :width],
            small[layer, 4:5, :width],
            small[layer, 5:6, :width],
            norm1.at[layer],
            rstd.at[layer, 0],
            first_rows,
        )
        first_copy = to_mate(
            both_first.at[layer, pl.ds(0, tokens)], both_first.at[layer, pl.ds(tokens, tokens)]
        )

        prepare(4 * layer + 2)
        first_copy.wait_recv()
        narrow = 256

        def up_tile(j, layer=layer):
            cols = pl.ds(pl.multiple_of(j * narrow, narrow), narrow)
            pre = jnp.dot(both_first[layer], w_up[layer, :, cols], preferred_element_type=wide)
            value, steep = gelu_and_slope(pre + small[layer, 2:3, cols])
            act[layer, :, cols] = value.astype(low)
            slope[layer, :, cols] = steep.astype(low)

        tiles(dims.kinds[2][2] // narrow, up_tile)

        prepare(4 * layer + 3)
        project(
            act.at[layer],
            lambda left, cols, layer=layer: jnp.dot(
                left, w_down[layer, :, cols], preferred_element_type=wide
            ),
            2 * layer + 1,
        ).wait_recv()
        last = layer == dims.layers - 1

        def second_rows(rows, value, layer=layer, last=last):
            if last:
                output[rows] = value.astype(low)
            else:
                hidden[rows] = value
                both_hidden[layer + 1, rows] = value.astype(low)

        layer_norm(
            first,
            total,
            back.at[2 * layer + 1],
            small[layer, 3:4, :width],
            small[layer, 6:7, :width],
            small[layer, 7:8, :width],
            norm2.at[layer],
            rstd.at[layer, 1],
            second_rows,
        )
        if not last:
            hidden_copy = to_mate(
                both_hidden.at[layer + 1, pl.ds(0, tokens)],
                both_hidden.at[layer + 1, pl.ds(tokens, tokens)],
            )
    reduces = {
        (layer, kind): [
            Reduce(
                place,
                layer,
                kind,
                part,
                terms[kind],
                [arrived[turn][kind] for turn in range(dims.bits)],
                lines[kind],
                done[kind],
                swapped[kind // 2],
                (reduce_send, reduce_recv, own_sem),
                (add_mine, add_other, load_sem, store_sem),
            )
            for part in range(2)
        ]
        for layer in range(dims.layers)
        for kind in range(4)
    }
    queue = [
        reduces[layer, kind] for layer in reversed(range(dims.layers)) for kind in (3, 2, 1, 0)
    ]
    stages = max(item.stages for pair in queue for item in pair)

    def pump(step, ahead=2):
        if step + ahead < len(queue):
            for item in queue[step + ahead]:
                item.reach(1)
        for behind in reversed(range(stages - 1)):
            at = step - behind
            if 0 <= at < len(queue):
                for item in queue[at]:
                    item.reach(2 + behind)

    def weight_terms(layer, kind, left, right):
        _, held, columns, _ = dims.kinds[kind]
        step = min(256, held)
        wide_cols = columns if columns <= ring.shape[2] else columns // 2
        across = columns // wide_cols
        count = (held // step) * across
        slots = ring.shape[0]

        def store(j):
            rows = pl.ds(pl.multiple_of((j // across) * step, step), step)
            cols = pl.ds(pl.multiple_of((j % across) * wide_cols, 128), wide_cols)
            return pltpu.make_async_copy(
                ring.at[j % slots, pl.ds(0, step), pl.ds(0, wide_cols)],
                terms[kind].at[layer, rows, cols],
                ring_sem.at[j % slots],
            )

        def body(j):
            @pl.when(j >= slots)
            def _():
                store(j - slots).wait()

            rows = pl.ds(pl.multiple_of((j // across) * step, step), step)
            cols = pl.ds(pl.multiple_of((j % across) * wide_cols, 128), wide_cols)
            ring[j % slots, pl.ds(0, step), pl.ds(0, wide_cols)] = dot_first(
                left[:, rows], right[:, cols]
            ).astype(low)
            store(j).start()

        tiles(count, body)
        for j in range(max(0, count - slots), count):
            store(j).wait()

    def count_up(layer, row, value, cols=None):
        cols = pl.ds(0, value.shape[1]) if cols is None else cols
        vectors[layer, pl.ds(row, 1), cols] += jnp.sum(value, axis=0, keepdims=True)

    def norm_grad(value, normed, scale_row, gain_row):
        grad = value * gain_row
        inner = jnp.mean(grad * normed, axis=-1, keepdims=True)
        return scale_row * (grad - jnp.mean(grad, axis=-1, keepdims=True) - normed * inner)

    def back_rows(j):
        return pl.ds(pl.multiple_of(j * chunk, chunk), chunk)

    grad_copy = None
    cotangent_copy.wait()
    pumped = 0
    for layer in reversed(range(dims.layers)):
        newest = layer == dims.layers - 1
        if grad_copy is not None:
            grad_copy.wait_send()
            settled.append(grad_copy)

        def second_back(j, layer=layer, newest=newest):
            rows = back_rows(j)
            value = both_grad[rows].astype(wide) if newest else hidden[rows]
            normed = norm2[layer, rows]
            count_up(layer, 7, value * normed)
            count_up(layer, 8, value)
            grad = norm_grad(value, normed, rstd[layer, 1, rows, 0:1], small[layer, 6:7, :width])
            first[rows] = grad
            rounded = grad.astype(low)
            both_grad[rows] = rounded
            count_up(layer, 4, rounded.astype(wide))

        tiles(tokens // chunk, second_back)
        grad_copy = to_mate(both_grad.at[pl.ds(0, tokens)], both_grad.at[pl.ds(tokens, tokens)])
        grad_copy.wait_recv()

        weight_terms(layer, 3, act.at[layer], both_grad)
        if newest:
            for item in queue[0]:
                item.reach(1)
        else:
            pump(pumped)
            pumped += 1

        def down_back(j, layer=layer):
            cols = pl.ds(pl.multiple_of(j * narrow, narrow), narrow)
            grad = dot_last(both_grad[...], w_down[layer, cols, :])
            rounded = (grad * slope[layer, :, cols].astype(wide)).astype(low)
            slope[layer, :, cols] = rounded
            count_up(layer, 3, rounded.astype(wide), cols)

        tiles(dims.hidden // 2 // narrow, down_back)
        weight_terms(layer, 2, both_first.at[layer], slope.at[layer])
        if newest:
            for item in queue[1]:
                item.reach(1)
        else:
            pump(pumped)
            pumped += 1
        exchange_at = 2 * (dims.layers - 1 - layer)
        project(
            slope.at[layer],
            lambda left, cols, layer=layer: dot_last(left, w_up[layer, cols, :]),
            2 * dims.layers + exchange_at,
        ).wait_recv()
        grad_copy.wait_send()
        settled.append(grad_copy)

        def first_back(j, layer=layer, exchange_at=exchange_at):
            rows = back_rows(j)
            value = first[rows] + total[rows] + back[exchange_at, rows].astype(wide)
            normed = norm1[layer, rows]
            count_up(layer, 5, value * normed)
            count_up(layer, 6, value)
            grad = norm_grad(value, normed, rstd[layer, 0, rows, 0:1], small[layer, 4:5, :width])
            first[rows] = grad
            rounded = grad.astype(low)
            both_grad[rows] = rounded
            count_up(layer, 2, rounded.astype(wide))

        tiles(tokens // chunk, first_back)
        grad_copy = to_mate(both_grad.at[pl.ds(0, tokens)], both_grad.at[pl.ds(tokens, tokens)])
        grad_copy.wait_recv()
        weight_terms(layer, 1, attended.at[layer], both_grad)

        out_tile = min(256, dims.third)

        def out_back(j, layer=layer):
            cols = pl.ds(pl.multiple_of(j * out_tile, out_tile), out_tile)
            attended[layer, :, cols] = dot_last(both_grad[...], w_out[layer, cols, :]).astype(low)

        tiles(dims.third // out_tile, out_back)
        if not newest:
            pump(pumped)
            pumped += 1

        def attend_back(j, layer=layer):
            s, block = j // lane_blocks, j % lane_blocks
            rows = pl.ds(pl.multiple_of(s * tokens, tokens), tokens)
            lanes = pl.ds(pl.multiple_of(block * 128, 128), 128)

            def at(which):
                return pl.ds(pl.multiple_of(which * dims.third + block * 128, 128), 128)

            query, key_rows, value_rows = (qkv[layer, rows, at(which)] for which in range(3))
            grad_out = attended[layer, rows, lanes]
            grads = [[], [], []]
            for e in range(heads_row):
                part = slice(e * dims.head_dim, (e + 1) * dims.head_dim)
                prob = probs[layer, s * (lane_blocks * heads_row) + block * heads_row + e]
                grads[2].append(dot_first(prob, grad_out[:, part]))
                prob = prob.astype(wide)
                grad_prob = dot_last(grad_out[:, part], value_rows[:, part])
                inner = jnp.sum(prob * grad_prob, axis=1, keepdims=True)
                grad_score = (prob * (grad_prob - inner)).astype(low)
                grads[0].append(
                    jnp.dot(grad_score, key_rows[:, part], preferred_element_type=wide) * scale
                )
                grads[1].append(dot_first(grad_score, query[:, part]) * scale)
            for which, row in ((0, 0), (1, None), (2, 1)):
                rounded = jnp.concatenate(grads[which], axis=1).astype(low)
                qkv[layer, rows, at(which)] = rounded
                if row is not None:
                    count_up(layer, row, rounded.astype(wide), lanes)

        tiles(2 * lane_blocks, attend_back)
        weight_terms(layer, 0, both_hidden.at[layer], qkv.at[layer])
        project(
            qkv.at[layer],
            lambda left, cols, layer=layer: dot_last(left, w_qkv[layer, cols, :]),
            2 * dims.layers + exchange_at + 1,
        ).wait_recv()

        def input_rows(j, exchange_at=exchange_at):
            rows = back_rows(j)
            hidden[rows] = first[rows] + total[rows] + back[exchange_at + 1, rows].astype(wide)

        tiles(tokens // chunk, input_rows)
        pump(pumped)
        pumped += 1

    grad_out_copy = pltpu.make_async_copy(hidden, input_grad, io_sem.at[0])
    grad_out_copy.start()

    if dims.direct:
        count = dims.vector_rows
        for shard in range(shards):
            for layer in range(dims.layers):
                at = layer * sum(dims.lengths)
                for member, length in enumerate(dims.lengths):
                    halved = member in (0, 1, 3)
                    for block in range(length):
                        first_lane = (shard // 2 if halved else shard) * length * dims.rows
                        lanes = pl.ds(first_lane + block * dims.rows, dims.rows)
                        value = vectors[layer, member : member + 1, lanes]
                        if halved:
                            value = jnp.where(place.half == shard % 2, value, 0.0)
                        vector_away[shard, at : at + 1, :] = value
                        at += 1
                heads = HEADS // 2
                vector_away[shard, pl.ds(count + layer * heads, heads)] = tops[layer]
        vector_back[place.me] = vector_away[place.me]

        def send_terms(index):
            target = in_group(index + 1)
            remote(
                vector_away.at[target[1]],
                vector_back.at[place.me],
                vector_send.at[1],
                vector_recv.at[1],
                target,
            ).start()

        few(shards - 1, send_terms)
    gathered = pumped + 1
    while pumped < len(queue) + stages:
        pump(pumped)
        pumped += 1
        if dims.direct and pumped == gathered:
            vector_bytes(vector_back, 1, shards - 1).wait_recv()
            total_rows = vector_back[0, pl.ds(0, count)]
            for shard in range(1, shards):
                total_rows = total_rows + vector_back[shard, pl.ds(0, count)]
            vector_out[...] = total_rows
            heads = dims.layers * HEADS // 2
            for half in range(2):
                peak = vector_back[half, pl.ds(count, heads)]
                for shard in range(2 + half, shards, 2):
                    peak = jnp.maximum(peak, vector_back[shard, pl.ds(count, heads)])
                peak_out[half] = peak
            line_back[place.rep, pl.ds(0, count)] = vector_out[...]
            for half in range(2):
                line_back[place.rep, pl.ds(count + half * heads, heads)] = peak_out[half]
            for step in range(1, reps):
                remote(
                    line_back.at[place.rep],
                    line_back.at[place.rep],
                    vector_send.at[2],
                    vector_recv.at[2],
                    ((place.rep + step) % reps, place.me),
                ).start()
    if dims.direct:
        vector_bytes(line_back, 2, reps - 1).wait_recv()
        total_rows = line_back[0, pl.ds(0, count)]
        for other in range(1, reps):
            total_rows = total_rows + line_back[other, pl.ds(0, count)]
        vector_out[...] = total_rows
        for half in range(2):
            peak = line_back[0, pl.ds(count + half * heads, heads)]
            for other in range(1, reps):
                peak = jnp.maximum(peak, line_back[other, pl.ds(count + half * heads, heads)])
            peak_out[half] = peak

    for copy in exchanges:
        if not any(copy is other for other in settled):
            copy.wait_send()
    if dims.direct:
        vector_bytes(vector_all, 0, shards - 1).wait_send()
        vector_bytes(vector_back, 1, shards - 1).wait_send()
        vector_bytes(line_back, 2, reps - 1).wait_send()
    for gather in gathers:
        gather.finish_sends()
    for pair in queue:
        for item in pair:
            item.finish_sends()
    grad_out_copy.wait()


def run_layers(dims, x, cotangent, segments, vectors, weights):
    layers, tokens, width = dims.layers, dims.tokens, dims.width
    both = 2 * tokens

    def shape(dims_of, dtype):
        return jax.ShapeDtypeStruct(dims_of, dtype)

    held = [shape((layers, rows, columns), low) for _, rows, columns, _ in dims.kinds]
    pair_rows = [rows * (2 if paired else 1) for rows, _, _, paired in dims.kinds]
    columns = [kind[2] for kind in dims.kinds]
    heads = HEADS // 2
    summed = []
    if dims.direct:
        summed = [
            shape((dims.vector_rows, dims.rows), wide),
            shape((2, layers * heads, 128), wide),
        ]
    outs = (
        [
            shape((tokens, width), low),
            shape((layers, HEADS // 2, 128), wide),
            shape((layers, 16, dims.hidden // 2), wide),
            shape((tokens, width), wide),
        ]
        + summed
        + held * (1 + dims.bits)
        + [shape((layers, dims.reps // 2, r, c), low) for r, c in zip(pair_rows, columns)]
        + [shape((layers, r, c), low) for r, c in zip(pair_rows, columns)]
        + [
            shape((layers, dims.rows, columns[kind] * (2 if dims.direct else 1)), low)
            for kind in (0, 2)
        ]
    )
    vmem = pl.BlockSpec(memory_space=pltpu.VMEM)
    anywhere = pl.BlockSpec(memory_space=pl.ANY)
    dma = pltpu.SemaphoreType.DMA
    scratch = [pltpu.VMEM(item.shape, item.dtype) for item in held] + [
        pltpu.VMEM(*item)
        for item in (
            ((layers, both, width), low),
            ((layers, both, 3 * dims.third), low),
            ((layers, both, dims.third), low),
            ((layers, HEADS, tokens, tokens), low),
            ((layers, tokens, width), wide),
            ((layers, both, width), low),
            ((layers, both, dims.hidden // 2), low),
            ((layers, both, dims.hidden // 2), low),
            ((layers, tokens, width), wide),
            ((layers, 2, tokens, 128), wide),
            ((tokens, width), wide),
            ((tokens, width), wide),
            ((tokens, width), wide),
            ((2, tokens, width), low),
            ((2 * layers, tokens, width), low),
            ((2, tokens, tokens), wide),
            ((both, width), low),
            ((3, 256, 1024), low),
            ((2, 256, 1024), low),
            ((2, 256, 1024), low),
            ((8, tokens), wide),
            ((8, tokens), wide),
        )
    ]
    if dims.direct:
        rows = dims.vector_rows
        scratch += [
            pltpu.VMEM(item, wide)
            for item in (
                (dims.shards, rows, dims.rows),
                (layers, 8, dims.hidden // 2),
                (dims.shards, rows + layers * heads, dims.rows),
                (dims.shards, rows + layers * heads, dims.rows),
                (dims.reps, rows + 2 * layers * heads, dims.rows),
            )
        ]
    slots = 2 + 2 * dims.bits
    exchange_count = 2 + 8 * layers
    reduce_slots = dims.bits + dims.reps
    scratch = scratch + [
        dma((4 * layers,)),
        dma((4 * layers, slots)),
        dma((4 * layers, slots)),
        dma((exchange_count,)),
        dma((exchange_count,)),
        dma((8 * layers, reduce_slots)),
        dma((8 * layers, reduce_slots)),
        dma((8 * layers,)),
        dma((2, 2)),
        dma((2,)),
        dma((3,)),
        dma((2,)),
    ]
    if dims.direct:
        scratch += [dma((3,)), dma((3,))]
    return pl.pallas_call(
        functools.partial(layers_kernel, dims),
        out_shape=outs,
        in_specs=[anywhere] * 2 + [vmem] * 2 + [anywhere] * 4,
        out_specs=[vmem] * 3 + [anywhere] + [vmem] * len(summed) + [anywhere] * (len(outs) - 4 - len(summed)),
        scratch_shapes=scratch,
        compiler_params=pltpu.CompilerParams(
            collective_id=0, has_side_effects=True, vmem_limit_bytes=63 * 2**20 + 2**19
        ),
        name="layers",
    )(x, cotangent, segments, vectors, *weights)


def own_rows(net, value):
    layers, rows, columns = value.shape
    split = value.reshape(layers, 2, rows // 2, columns)
    return lax.dynamic_index_in_dim(split, net.core, 1, keepdims=False)


def gathered_vectors(net, dims, packed):
    lengths = dims.lengths
    packed = net.in_order(packed, net.over_core(packed), net.core)
    packed = net.rows_in_order(net.gather_chips(packed, list(range(net.bits))))

    def whole(layer, member):
        start = sum(lengths[:member])
        return packed[:, layer, start : start + lengths[member]].astype(wide)

    def of_core(layer, member):
        split = whole(layer, member).reshape(net.high, 2, -1)
        return lax.dynamic_index_in_dim(split, net.core, 1, keepdims=False).reshape(-1)

    def wide_row(row):
        return jnp.pad(row, (0, dims.hidden // 2 - row.shape[0]))

    def rows(layer):
        bias_q = of_core(layer, 0)
        bias_qkv = jnp.concatenate([bias_q, jnp.zeros_like(bias_q), of_core(layer, 1)])
        singles = [whole(layer, member).reshape(-1) for member in (2, 4, 5, 6, 7, 8)]
        return [bias_qkv, singles[0], of_core(layer, 3)] + singles[1:]

    return jnp.stack(
        [jnp.stack([wide_row(row) for row in rows(layer)]) for layer in range(dims.layers)]
    )


def summed_vectors(net, dims, vectors, tops):
    layers, lengths, rows = dims.layers, dims.lengths, dims.rows
    half_width, half_hidden = dims.third, dims.hidden // 2
    here = (half_width, half_width, dims.width, half_hidden) + (dims.width,) * 5

    def placed(value, member):
        if member in (0, 1, 3):
            value = value.reshape(net.high, 1, net.step, lengths[member], rows)
            zero = jnp.zeros_like(value)
            first = net.core == 0
            return jnp.concatenate(
                [jnp.where(first, value, zero), jnp.where(first, zero, value)], axis=1
            )
        return value.reshape(net.high, 2, net.step, lengths[member], rows)

    terms = jnp.stack(
        [
            jnp.concatenate(
                [placed(vectors[layer, row, :size], row) for row, size in enumerate(here)], axis=3
            )
            for layer in range(layers)
        ],
        axis=3,
    )
    theirs = lax.dynamic_index_in_dim(terms, 1 - net.core, 1, keepdims=False)
    ours = lax.dynamic_index_in_dim(terms, net.core, 1, keepdims=False)
    terms = ours + net.over_core(theirs)
    terms = terms.reshape((net.pairs,) + terms.shape[2:])
    terms = net.sum_reps(net.scatter_chips(terms, list(range(net.bits))))

    local = tops[:, :, 0]
    local = net.in_order(local, net.over_core(local), net.core)
    local = local.reshape(2, layers, net.high, -1).transpose(1, 2, 0, 3).reshape(layers, HEADS)
    for bit in range(net.bits):
        local = jnp.maximum(local, net.over_bit(local, bit))
    step = 1
    while step < net.reps:
        swap = [(i, i ^ step) for i in range(net.reps)]
        local = jnp.maximum(local, lax.ppermute(local, "rep", swap))
        step *= 2
    return terms, local


def shards(
    inputs,
    cotangent,
    segments,
    w_qkv,
    w_out,
    w_up,
    w_down,
    bias_query,
    bias_value,
    bias_out,
    bias_up,
    bias_down,
    norm1_gain,
    norm1_bias,
    norm2_gain,
    norm2_bias,
    tau,
    *,
    shard_count,
    rep_count,
):
    layer_count = w_qkv.shape[0]
    width = w_qkv.shape[2] // 3
    rows_here = bias_query.shape[1]
    head_dim = width // HEADS
    net = Net(shard_count, rep_count, max(1, head_dim // rows_here))

    vectors = (
        bias_query,
        bias_value,
        bias_out,
        bias_up,
        bias_down,
        norm1_gain,
        norm1_bias,
        norm2_gain,
        norm2_bias,
    )
    lengths = [vector.shape[1] // rows_here for vector in vectors]
    packed = jnp.concatenate(
        [vector.reshape(layer_count, -1, rows_here) for vector in vectors], axis=1
    )
    tokens = inputs.shape[0]
    dims = Dims(shard_count, rep_count, net.step, layer_count, tokens, width, w_up.shape[2])
    if dims.direct:
        vector_in = packed.reshape(dims.vector_rows, rows_here).astype(wide)
        matrices = (w_qkv, w_out, w_up, w_down)
    else:
        vector_in = gathered_vectors(net, dims, packed)
        matrices = (by_half(w_qkv, net, 3), w_out, by_half(w_up, net, 1), w_down)
    results = run_layers(dims, inputs, cotangent, segments, vector_in, matrices)
    output, tops, vector_terms, input_grad = results[:4]
    done, swapped = results[-6:-2], results[-2:]

    if dims.direct:
        vector_grads, peak = results[4:6]
        vector_grads = vector_grads.reshape(layer_count, -1, rows_here)
        peak = peak[:, :, 0].reshape(2, layer_count, net.high, -1)
        peak = peak.transpose(1, 2, 0, 3).reshape(layer_count, HEADS)
        full = swapped[0], done[1], swapped[1], done[3]
    else:
        vector_grads, peak = summed_vectors(net, dims, vector_terms, tops)
        paired = [whole_columns(own_rows(net, done[k]), swapped[k // 2], net, 3 - k) for k in (0, 2)]
        full = paired[0], done[1], paired[1], done[3]
    large = tuple(value.astype(wide) for value in full)
    ends = [sum(lengths[: member + 1]) for member in range(len(lengths))]
    vector_grads = [
        vector_grads[:, end - length : end].reshape(layer_count, -1)
        for end, length in zip(ends, lengths)
    ]
    factor = jnp.sqrt(tau / jnp.maximum(peak, tau))
    column_scale = jnp.repeat(factor, head_dim, axis=1)
    both_scale = jnp.concatenate([column_scale, column_scale], axis=1)
    clipped_qk = w_qkv[:, :, : 2 * width].astype(wide) * both_scale[:, None, :]
    start = lax.axis_index("shard") * rows_here
    scale_here = lax.dynamic_slice_in_dim(column_scale, start, rows_here, 1)
    clipped_bias_query = bias_query.astype(wide) * scale_here
    return (output, input_grad) + large + tuple(vector_grads) + (clipped_qk, clipped_bias_query)


def solution(mesh):
    tokens = P(("rep", "shard"), None)
    matrix = P(None, "shard", None)
    vector = P(None, "shard")
    in_specs = (tokens, tokens, tokens) + (matrix,) * 4 + (vector,) * 9 + (P(),)
    out_specs = (tokens, tokens) + (matrix,) * 4 + (vector,) * 9 + (matrix, vector)

    def local(*arrays):
        return shards(*arrays, shard_count=mesh.shape["shard"], rep_count=mesh.shape["rep"])

    return jax.shard_map(local, mesh=mesh, in_specs=in_specs, out_specs=out_specs, check_vma=False)
```

```python
import functools
import math

import jax
import jax.numpy as jnp
from jax import lax
from jax.experimental import pallas as pl
from jax.experimental.pallas import tpu as pltpu
from jax.sharding import PartitionSpec as P

HEADS = 16
MESH = pl.DeviceIdType.MESH
LEAD = 1
CUTS = 2
AHEAD = 1
GROUPS = ((0,), (1, 2, 3, 4, 5))
IN_PLANE_FIRST = (11, 10, 10, 12)
IN_PLANE = (11, 10, 10, 12)


epsilon = 1e-05
neg_large = -1e30
low = jnp.bfloat16
wide = jnp.float32


class Net:
    def __init__(self, shards, reps, step):
        self.shards = shards
        self.reps = reps
        self.step = step
        self.pairs = shards // 2
        self.high = shards // (2 * step)
        self.bits = self.pairs.bit_length() - 1
        self.me = lax.axis_index("shard")
        self.core = (self.me // step) % 2
        self.rep = lax.axis_index("rep")

    def over_core(self, value):
        return lax.ppermute(value, "shard", [(i, i ^ self.step) for i in range(self.shards)])

    def stride(self, bit):
        return (1 << bit) if (1 << bit) < self.step else (2 << bit)

    def over_bit(self, value, bit):
        step = self.stride(bit)
        return lax.ppermute(value, "shard", [(i, i ^ step) for i in range(self.shards)])

    def chip_bit(self, bit):
        return (self.me // self.stride(bit)) % 2

    def rows_in_order(self, value):
        rest = value.shape[2:]
        value = value.reshape((self.high, self.step, 2) + rest)
        return jnp.swapaxes(value, 1, 2).reshape((self.shards,) + rest)

    def rows_by_pair(self, value):
        rest = value.shape[1:]
        value = value.reshape((self.high, 2, self.step) + rest)
        return jnp.swapaxes(value, 1, 2).reshape((self.pairs, 2) + rest)

    def in_order(self, mine, other, place):
        first = place == 0
        return jnp.stack([jnp.where(first, mine, other), jnp.where(first, other, mine)])

    def gather_chips(self, piece, order):
        shape = piece.shape
        for bit in order:
            piece = self.in_order(piece, self.over_bit(piece, bit), self.chip_bit(bit))
        axes = list(reversed(order))
        natural = [axes.index(bit) for bit in reversed(range(self.bits))]
        rest = list(range(self.bits, self.bits + len(shape)))
        return piece.transpose(natural + rest).reshape((self.pairs,) + shape)

    def scatter_chips(self, value, order):
        rest = value.shape[1:]
        value = value.reshape((2,) * self.bits + rest)
        left = list(reversed(range(self.bits)))
        for bit in order:
            axis = left.index(bit)
            place = self.chip_bit(bit)
            theirs = lax.dynamic_index_in_dim(value, 1 - place, axis, keepdims=False)
            ours = lax.dynamic_index_in_dim(value, place, axis, keepdims=False)
            got = self.over_bit(theirs, bit)
            value = (ours.astype(wide) + got.astype(wide)).astype(value.dtype)
            left.remove(bit)
        return value

    def sum_reps(self, value):
        reps, half = self.reps, self.reps // 2

        def add(one, other):
            return (one.astype(wide) + other.astype(wide)).astype(value.dtype)

        total = value
        for i in range(half - 1):
            got = lax.ppermute(total, "rep", [(i, i + 1), (reps - 1 - i, reps - 2 - i)])
            total = add(total, got)
        total = add(total, lax.ppermute(total, "rep", [(half - 1, half), (half, half - 1)]))
        for i in reversed(range(half - 1)):
            got = lax.ppermute(total, "rep", [(i + 1, i), (reps - 2 - i, reps - 1 - i)])
            outer = jnp.logical_or(self.rep == i, self.rep == reps - 1 - i)
            total = jnp.where(outer, got, total)
        return total


def by_half(weight, net, groups):
    layers, rows, columns = weight.shape
    split = weight.reshape(layers, rows, groups * net.high, 2, columns // (2 * groups * net.high))
    return split.transpose(0, 3, 1, 2, 4).reshape(layers, 2, rows, columns // 2)


def whole_columns(mine, other, net, groups):
    layers, rows, columns = mine.shape
    block = columns // (groups * net.high)
    both = [part.reshape(layers, rows, groups * net.high, block) for part in (mine, other)]
    first = net.core == 0
    stacked = jnp.stack(
        [jnp.where(first, both[0], both[1]), jnp.where(first, both[1], both[0])], axis=3
    )
    return stacked.reshape(layers, rows, 2 * columns).astype(wide)


class Place:
    def __init__(self, dims):
        self.dims = dims
        step = dims.step
        self.rep = lax.axis_index("rep")
        self.me = lax.axis_index("shard")
        self.half = (self.me // step) % 2
        self.pair = (self.me // (2 * step)) * step + self.me % step
        self.plane = self.rep % 2

    def flip(self, value, bit):
        size = 1 << bit
        return value + size * (1 - 2 * ((value // size) % 2))

    def mate(self):
        return (self.rep, self.me + self.dims.step * (1 - 2 * self.half))

    def over_bit(self, bit):
        stride = (1 << bit) if (1 << bit) < self.dims.step else (2 << bit)
        return (self.rep, self.me + stride * (1 - 2 * ((self.me // stride) % 2)))

    def over_plane(self):
        return (self.rep + 1 - 2 * self.plane, self.me)

    def first_shard(self, pair):
        step = self.dims.step
        return (pair // step) * (2 * step) + pair % step


class Dims:
    def __init__(self, shards, reps, step, layers, tokens, width, hidden):
        self.shards, self.reps, self.step = shards, reps, step
        self.pairs = shards // 2
        self.bits = self.pairs.bit_length() - 1
        self.layers, self.tokens, self.width, self.hidden = layers, tokens, width, hidden
        self.head_dim = width // HEADS
        self.third = width // 2
        self.rows = width // shards
        self.kinds = (
            (self.rows, width, 3 * width // 2, True),
            (self.rows, width // 2, width, False),
            (self.rows, width, hidden // 2, True),
            (hidden // shards, hidden // 2, width, False),
        )
        high = shards // (2 * step)
        self.block = (width // (2 * high), None, hidden // (2 * high), None)
        self.blocks = (3 * high, None, high, None)
        self.lengths = (1, 1, 1, hidden // width, 1, 1, 1, 1, 1)
        self.vector_rows = layers * sum(self.lengths)
        self.direct = self.rows % 128 == 0 and step == 1
        self.cuts = tuple(CUTS if self.direct and kind != 1 else 1 for kind in range(4))


def remote(src, dst, send, recv, where):
    return pltpu.make_async_remote_copy(
        src_ref=src, dst_ref=dst, send_sem=send, recv_sem=recv, device_id=where, device_id_type=MESH
    )


class Gather:
    def __init__(self, place, layer, kind, cut, source, whole, sems, last):
        self.place, self.dims = place, place.dims
        self.layer, self.kind = layer, kind
        self.source, self.whole = source, whole
        self.rows, self.held, columns, self.paired = self.dims.kinds[kind]
        self.local, self.send, self.recv = sems
        self.cut, self.cuts = cut, self.dims.cuts[kind]
        self.columns = columns // self.cuts
        self.base = cut * self.columns
        self.at = (layer * 4 + kind) * CUTS + cut
        self.in_plane = in_plane = in_plane_columns(self.dims, layer, kind, self.columns, last)
        self.stage = 0
        self.stages = self.dims.bits + (2 if in_plane < self.columns else 1)

    def blocks(self, pair):
        if not self.paired:
            return [pair * self.rows], self.rows
        first = self.place.first_shard(pair) * self.rows
        if self.dims.step == 1:
            return [first], 2 * self.rows
        return [first, first + self.dims.step * self.rows], self.rows

    def window(self, part):
        size = self.in_plane // 2
        if (size % 128) and part < 2:
            low_size = size // 128 * 128
            size = low_size if part == 0 else self.in_plane - low_size
            offset = 0 if part == 0 else low_size
        else:
            offset = part * size
        start = self.base + self.place.plane * (self.columns - self.in_plane) + offset
        return pl.ds(pl.multiple_of(start, 128), size), size

    def order(self, part):
        bits = list(range(self.dims.bits))
        return bits if part == 0 else bits[::-1]

    def subset(self, done):
        pairs = [self.place.pair]
        for bit in done:
            pairs = pairs + [self.place.flip(pair, bit) for pair in pairs]
        return pairs

    def begin(self):
        place = self.place
        if self.paired:
            mine = place.me * self.rows
            rows = pl.ds(pl.multiple_of(mine, 16), self.rows)
            for theirs, ours in self.begin_blocks():
                pltpu.make_async_copy(
                    ours, self.whole.at[self.layer, rows, theirs[1]], self.local.at[self.at]
                ).start()
            for theirs, ours in self.begin_blocks():
                remote(
                    theirs[0],
                    self.whole.at[self.layer, rows, theirs[1]],
                    self.send.at[self.at, 0],
                    self.recv.at[self.at, 0],
                    place.mate(),
                ).start()
        else:
            rows = pl.ds(pl.multiple_of(place.pair * self.rows, 16), self.rows)
            columns = pl.ds(self.base, self.columns)
            pltpu.make_async_copy(
                self.source.at[self.layer, :, columns],
                self.whole.at[self.layer, rows, columns],
                self.local.at[self.at],
            ).start()

    def begin_blocks(self):
        place, width = self.place, self.dims.block[self.kind]
        if not self.dims.direct:
            every = pl.ds(0, self.columns)
            yield (
                (self.source.at[self.layer, 1 - place.half], every),
                self.source.at[self.layer, place.half],
            )
            return
        count = self.dims.blocks[self.kind] // self.cuts
        for block in range(self.cut * count, (self.cut + 1) * count):
            to = pl.ds(block * width, width)
            starts = [(2 * block + half) * width for half in (1 - place.half, place.half)]
            theirs, ours = (
                self.source.at[self.layer, :, pl.ds(pl.multiple_of(start, 128), width)] for start in starts
            )
            yield (theirs, to), ours

    def some(self, rows, columns):
        return self.whole.at[self.layer, pl.ds(0, rows), columns]

    def phase(self, turn):
        place = self.place
        for part in range(2):
            order = self.order(part)
            columns, _ = self.window(part)
            for pair in self.subset(order[:turn]):
                starts, count = self.blocks(pair)
                for start in starts:
                    block = self.whole.at[self.layer, pl.ds(pl.multiple_of(start, 16), count), columns]
                    remote(
                        block,
                        block,
                        self.send.at[self.at, 1 + 2 * turn + part],
                        self.recv.at[self.at, 1 + 2 * turn + part],
                        place.over_bit(order[turn]),
                    ).start()

    def phase_bytes(self, turn, part):
        columns = pl.ds(0, self.window(part)[1])
        per_pair = self.rows * (2 if self.paired else 1)
        block = self.some(per_pair << turn, columns)
        at = 1 + 2 * turn + part
        return remote(block, block, self.send.at[self.at, at], self.recv.at[self.at, at], self.place.mate())

    def across(self):
        place = self.place
        size = self.columns - self.in_plane
        columns = pl.ds(pl.multiple_of(self.base + place.plane * self.in_plane, 128), size)
        at = 1 + 2 * self.dims.bits
        for pair in self.subset(range(self.dims.bits))[1:]:
            starts, count = self.blocks(pair)
            for start in starts:
                block = self.whole.at[self.layer, pl.ds(pl.multiple_of(start, 16), count), columns]
                remote(block, block, self.send.at[self.at, at], self.recv.at[self.at, at], place.over_plane()).start()

    def across_bytes(self):
        per_pair = self.rows * (2 if self.paired else 1)
        block = self.some(per_pair * (self.dims.pairs - 1), pl.ds(0, self.columns - self.in_plane))
        at = 1 + 2 * self.dims.bits
        return remote(block, block, self.send.at[self.at, at], self.recv.at[self.at, at], self.place.over_plane())

    def own_bytes(self):
        if not self.paired:
            return None
        block = self.some(self.rows, pl.ds(0, self.columns))
        return remote(block, block, self.send.at[self.at, 0], self.recv.at[self.at, 0], self.place.mate())

    def advance(self):
        if self.stage == 0:
            own = self.some(self.rows, pl.ds(0, self.columns))
            pltpu.make_async_copy(own, own, self.local.at[self.at]).wait()
            if self.paired:
                self.own_bytes().wait_recv()
        elif self.stage <= self.dims.bits:
            for part in range(2):
                self.phase_bytes(self.stage - 1, part).wait_recv()
        else:
            self.across_bytes().wait_recv()
        if self.stage < self.dims.bits:
            self.phase(self.stage)
        elif self.stage + 1 < self.stages:
            self.across()
        self.stage += 1

    def reach(self, stage):
        while self.stage < min(stage, self.stages):
            self.advance()

    def finish_sends(self):
        if self.paired:
            self.own_bytes().wait_send()
        for turn in range(self.dims.bits):
            for part in range(2):
                self.phase_bytes(turn, part).wait_send()
        if self.in_plane < self.columns:
            self.across_bytes().wait_send()


class Reduce:
    def __init__(self, place, layer, kind, cut, part, terms, arrived, lines, done, swapped, sems, bufs):
        self.place, self.dims = place, place.dims
        self.layer, self.kind, self.part = layer, kind, part
        self.terms, self.arrived, self.lines, self.done, self.swapped = terms, arrived, lines, done, swapped
        self.send, self.recv, self.own_sem = sems
        self.mine, self.other, self.load_sem, self.store_sem = bufs
        self.rows, self.held, self.columns, self.paired = self.dims.kinds[kind]
        cuts = self.dims.cuts[kind]
        self.slice_at, self.slices = cut * 2 + part, 2 * cuts
        self.size = self.columns // self.slices
        self.columns_here = pl.ds(self.slice_at * self.size, self.size)
        self.at = ((layer * 4 + kind) * CUTS + cut) * 2 + part
        bits = list(range(self.dims.bits))
        self.order = bits if part == 0 else bits[::-1]
        self.moves = self.dims.reps - 1
        self.stage = 0
        self.stages = 1 + self.dims.bits + self.moves + (1 if self.paired else 0)
        self.split = self.paired and self.dims.step > 1
        self.piece = self.rows * (2 if self.paired and not self.split else 1)
        self.pieces = 2 if self.split else 1

    def row_of(self, pair, which):
        if not self.paired:
            return pair * self.rows
        return (self.place.first_shard(pair) + which * self.dims.step) * self.rows

    def sems(self, slot):
        return self.send.at[self.at, slot], self.recv.at[self.at, slot]

    def kept(self, index, turn, away):
        pair = self.place.pair
        for i, bit in enumerate(self.order[turn + 1 :]):
            size = 1 << bit
            wanted = (index // (1 << i)) % 2
            pair = pair + size * (wanted - (self.place.pair // size) % 2)
        if away:
            pair = self.place.flip(pair, self.order[turn])
        return pair

    def count(self, turn):
        return (self.dims.pairs >> (turn + 1)) * self.pieces

    def loop(self, count, body):
        if count <= 4:
            for i in range(count):
                body(i)
        else:
            tiles(count, body)

    def block(self, ref, index, turn, away):
        pair = self.kept(index // self.pieces, turn, away)
        start = self.row_of(pair, index % self.pieces)
        return ref.at[self.layer, pl.ds(pl.multiple_of(start, 16), self.piece), self.columns_here]

    def start_turn(self, turn):
        def one(index):
            remote(
                self.block(self.terms, index, turn, True),
                self.block(self.arrived[turn], index, turn, True),
                *self.sems(turn),
                self.place.over_bit(self.order[turn]),
            ).start()

        self.loop(self.count(turn), one)

    def turn_bytes(self, turn):
        ref = self.terms.at[self.layer, pl.ds(0, self.count(turn) * self.piece), self.columns_here]
        return remote(ref, ref, *self.sems(turn), self.place.over_bit(self.order[turn]))

    def add(self, count, own, other, result):
        step = min(self.piece, self.mine.shape[1])
        per = self.piece // step
        total = count * per

        def part_of(make, index):
            ref = make(index // per)
            return ref.at[pl.ds(pl.multiple_of((index % per) * step, 16), step)]

        def slots(index):
            slot = index % 2
            rows, cols = pl.ds(0, step), pl.ds(0, self.size)
            return self.mine.at[slot, rows, cols], self.other.at[slot, rows, cols], slot

        def load(index):
            one, two, slot = slots(index)
            return (
                pltpu.make_async_copy(part_of(own, index), one, self.load_sem.at[slot, 0]),
                pltpu.make_async_copy(part_of(other, index), two, self.load_sem.at[slot, 1]),
            )

        def store(index):
            one, _, slot = slots(index)
            return pltpu.make_async_copy(one, part_of(result, index), self.store_sem.at[slot])

        def body(index, first, last):
            @when(jnp.logical_not(last) if not isinstance(last, bool) else not last)
            def _():
                @when(jnp.logical_not(first) if not isinstance(first, bool) else not first)
                def _():
                    store(index - 1).wait()

                for copy in load(index + 1):
                    copy.start()

            for copy in load(index):
                copy.wait()
            one, two, _ = slots(index)
            one[...] = (one[...].astype(wide) + two[...].astype(wide)).astype(low)
            store(index).start()

        for copy in load(0):
            copy.start()
        if total <= 4:
            for index in range(total):
                body(index, index == 0, index == total - 1)
        else:
            tiles(total, lambda index: body(index, index == 0, index == total - 1))
        if total > 1:
            store(total - 2).wait()
        store(total - 1).wait()

    def finish_turn(self, turn):
        self.turn_bytes(turn).wait_recv()
        self.add(
            self.count(turn),
            lambda index: self.block(self.terms, index, turn, False),
            lambda index: self.block(self.arrived[turn], index, turn, False),
            lambda index: self.block(self.terms, index, turn, False),
        )

    def own(self, which):
        start = self.row_of(self.place.pair, which)
        return self.terms.at[self.layer, pl.ds(pl.multiple_of(start, 16), self.piece), self.columns_here]

    def line(self, move, which):
        return self.lines.at[self.layer, move, pl.ds(which * self.piece, self.piece), self.columns_here]

    def final(self, which):
        return self.done.at[self.layer, pl.ds(which * self.piece, self.piece), self.columns_here]

    def roles(self, move):
        reps, half = self.dims.reps, self.dims.reps // 2
        if move < half - 1:
            return (move, reps - 1 - move), (move + 1, reps - 2 - move)
        if move == half - 1:
            return (half - 1, half), (half, half - 1)
        back = reps - 2 - move
        return (back + 1, reps - 2 - back), (back, reps - 1 - back)

    def move_copies(self, move, target):
        half = self.dims.reps // 2
        slot = self.dims.bits + move
        for which in range(self.pieces):
            src = self.own(which) if move < half else self.final(which)
            dst = self.line(move, which) if move < half else self.final(which)
            yield remote(src, dst, *self.sems(slot), (target, self.place.me))

    def move_bytes(self, move):
        slot = self.dims.bits + move
        ref = self.done.at[self.layer, pl.ds(0, self.pieces * self.piece), self.columns_here]
        return remote(ref, ref, *self.sems(slot), self.place.mate())

    def start_move(self, move):
        senders, receivers = self.roles(move)
        for sender, receiver in zip(senders, receivers):

            @pl.when(self.place.rep == sender)
            def _(receiver=receiver):
                for copy in self.move_copies(move, receiver):
                    copy.start()

    def finish_move(self, move):
        half = self.dims.reps // 2
        _, receivers = self.roles(move)

        @pl.when(jnp.logical_or(self.place.rep == receivers[0], self.place.rep == receivers[1]))
        def _():
            self.move_bytes(move).wait_recv()
            if move < half:
                self.add(
                    self.pieces,
                    self.own,
                    lambda which: self.line(move, which),
                    self.own if move < half - 1 else self.final,
                )

    def part_blocks(self):
        width = self.dims.block[self.kind]
        count = self.dims.blocks[self.kind] // self.slices
        for block in range(self.slice_at * count, (self.slice_at + 1) * count):
            place = (2 * block + self.place.half) * width
            yield pl.ds(block * width, width), pl.ds(pl.multiple_of(place, 128), width)

    def rows_done(self, half, columns):
        start = pl.multiple_of(half * self.rows, 16)
        return self.done.at[self.layer, pl.ds(start, self.rows), columns]

    def start_swap(self):
        slot = self.sems(self.dims.bits + self.moves)
        if not self.dims.direct:
            remote(
                self.rows_done(1 - self.place.half, self.columns_here),
                self.swapped.at[self.layer, pl.ds(0, self.rows), self.columns_here],
                *slot,
                self.place.mate(),
            ).start()
            return
        for here, there in self.part_blocks():
            remote(
                self.rows_done(1 - self.place.half, here),
                self.swapped.at[self.layer, pl.ds(0, self.rows), there],
                *slot,
                self.place.mate(),
            ).start()
        for here, there in self.part_blocks():
            pltpu.make_async_copy(
                self.rows_done(self.place.half, here),
                self.swapped.at[self.layer, pl.ds(0, self.rows), there],
                self.own_sem.at[self.at],
            ).start()

    def swap_bytes(self):
        ref = self.done.at[self.layer, pl.ds(0, self.rows), self.columns_here]
        return remote(ref, ref, *self.sems(self.dims.bits + self.moves), self.place.mate())

    def finish_swap(self):
        self.swap_bytes().wait_recv()
        if self.dims.direct:
            ref = self.done.at[self.layer, pl.ds(0, self.rows), self.columns_here]
            pltpu.make_async_copy(ref, ref, self.own_sem.at[self.at]).wait()

    def advance(self):
        bits = self.dims.bits
        if self.stage == 0:
            self.start_turn(0)
        elif self.stage < bits:
            self.finish_turn(self.stage - 1)
            self.start_turn(self.stage)
        elif self.stage == bits:
            self.finish_turn(bits - 1)
            self.start_move(0)
        elif self.stage < bits + self.moves:
            self.finish_move(self.stage - bits - 1)
            self.start_move(self.stage - bits)
        elif self.stage == bits + self.moves:
            self.finish_move(self.moves - 1)
            if self.paired:
                self.start_swap()
        else:
            self.finish_swap()
        self.stage += 1

    def additions(self, turn):
        bits, half = self.dims.bits, self.dims.reps // 2
        if turn < bits:
            wholes = [
                (
                    self.block(self.terms, index, turn, False),
                    self.block(self.arrived[turn], index, turn, False),
                    self.block(self.terms, index, turn, False),
                )
                for index in range(self.count(turn))
            ]
        elif turn - bits < half:
            move = turn - bits
            result = self.own(0) if move < half - 1 else self.final(0)
            wholes = [(self.own(0), self.line(move, 0), result)]
        else:
            wholes = []
        step = min(self.piece, 256)
        return [
            tuple(ref.at[pl.ds(start, step)] for ref in refs)
            for refs in wholes
            for start in range(0, self.piece, step)
        ]

    def arrive(self, turn):
        bits = self.dims.bits
        if turn < bits:
            self.turn_bytes(turn).wait_recv()
        elif turn < bits + self.moves:
            self.move_bytes(turn - bits).wait_recv()
        else:
            self.finish_swap()

    def taking_part(self, turn):
        bits = self.dims.bits
        if not bits <= turn < bits + self.moves:
            return True
        receivers = self.roles(turn - bits)[1]
        return jnp.logical_or(self.place.rep == receivers[0], self.place.rep == receivers[1])

    def depart(self, turn):
        bits = self.dims.bits
        if turn < bits:
            self.start_turn(turn)
        elif turn < bits + self.moves:
            self.start_move(turn - bits)
        elif self.paired and turn == bits + self.moves:
            self.start_swap()

    def reach(self, stage):
        while self.stage < min(stage, self.stages):
            self.advance()

    def finish_sends(self):
        for turn in range(self.dims.bits):
            self.turn_bytes(turn).wait_send()
        for move in range(self.moves):
            senders, _ = self.roles(move)

            @pl.when(jnp.logical_or(self.place.rep == senders[0], self.place.rep == senders[1]))
            def _(move=move):
                self.move_bytes(move).wait_send()

        if self.paired:
            self.swap_bytes().wait_send()


def when(condition):
    if isinstance(condition, bool):
        return (lambda body: body()) if condition else (lambda body: None)
    return pl.when(condition)


def in_plane_columns(dims, layer, kind, columns, last):
    if dims.reps % 2 or last:
        return columns
    blocks = columns // 128
    share = IN_PLANE[kind] if layer else IN_PLANE_FIRST[kind]
    return max(blocks * share // 16, blocks - blocks // 2) * 128


def few(count, body):
    if count <= 8:
        for index in range(count):
            body(index)
    else:
        tiles(count, body)


def gelu_and_slope(pre):
    cdf = 0.5 * (1.0 + lax.erf(pre * (1.0 / math.sqrt(2.0))))
    slope = cdf + pre * jnp.exp(-0.5 * pre * pre) * (1.0 / math.sqrt(2.0 * math.pi))
    return pre * cdf, slope


def dot_last(left, right):
    return lax.dot_general(left, right, (((1,), (1,)), ((), ())), preferred_element_type=wide)


def dot_first(left, right):
    return lax.dot_general(left, right, (((0,), (0,)), ((), ())), preferred_element_type=wide)


def tiles(count, body):
    def step(j, carry):
        body(j)
        return carry

    lax.fori_loop(0, count, step, 0)


def layers_kernel(dims, *refs):
    refs = iter(refs)

    def take(count):
        return [next(refs) for _ in range(count)]

    x_ref, cotangent, seg_row = take(3)
    vector_refs = take(9) if dims.direct else None
    vector_ref = None if dims.direct else take(1)[0]
    src_qkv, src_out, src_up, src_down = take(4)
    output, tops, vectors, input_grad = take(4)
    vector_out, peak_out = take(2) if dims.direct else (None, None)
    terms = take(4)
    arrived = [take(4) for _ in range(dims.bits)]
    lines, done = take(4), take(4)
    swapped = take(2)
    w_qkv, w_out, w_up, w_down = take(4)
    both_hidden, qkv, attended, probs, norm1, both_first, act, slope, norm2, rstd = take(10)
    hidden, first, total, away, back, bias, both_grad, ring, add_mine, add_other = take(10)
    seg_here, seg_rows = take(2)
    if dims.direct:
        vector_all, small, vector_away, vector_back, line_back, vector_here = take(6)
    else:
        small = vector_ref
    gather_local, gather_send, gather_recv, mate_send, mate_recv = take(5)
    reduce_send, reduce_recv, own_sem, load_sem, store_sem, ring_sem, io_sem = take(7)
    if dims.direct:
        vector_send, vector_recv, pool_load, pool_store = take(4)
    place = Place(dims)
    tokens, width = dims.tokens, dims.width
    heads_row = 128 // dims.head_dim
    scale = 1.0 / math.sqrt(dims.head_dim)

    barrier = pltpu.get_barrier_semaphore()
    reps, shards = dims.reps, dims.shards

    def in_group(step):
        return place.rep, (place.me + step) % shards

    def greet(step):
        pl.semaphore_signal(barrier, 1, device_id=in_group(step), device_id_type=MESH)

    few(shards - 1, lambda index: greet(index + 1))
    for step in range(1, reps):
        line = (place.rep + step) % reps, place.me
        pl.semaphore_signal(barrier, 1, device_id=line, device_id_type=MESH)
    pl.semaphore_wait(barrier, shards + reps - 2)

    sources = (src_qkv, src_out, src_up, src_down)
    wholes = (w_qkv, w_out, w_up, w_down)
    gathers = [
        Gather(
            place,
            layer,
            kind,
            cut,
            sources[kind],
            wholes[kind],
            (gather_local, gather_send, gather_recv),
            layer == dims.layers - 1 and kind == 3 and cut == dims.cuts[kind] - 1,
        )
        for layer in range(dims.layers)
        for kind in range(4)
        for cut in range(dims.cuts[kind])
    ]

    exchanges = []

    def to_mate(src, dst):
        at = len(exchanges)
        copy = remote(src, dst, mate_send.at[at], mate_recv.at[at], place.mate())
        copy.start()
        exchanges.append(copy)
        return copy

    seg_here[...] = jnp.broadcast_to(seg_row[...].astype(wide), seg_here.shape)
    rows_copy = to_mate(seg_here, seg_rows)

    def vector_bytes(buffer, slot, count):
        ref = buffer.at[pl.ds(0, count)]
        return remote(ref, ref, vector_send.at[slot], vector_recv.at[slot], place.mate())

    if dims.direct:

        def send_vector(index):
            remote(
                vector_here,
                vector_all.at[place.me],
                vector_send.at[0],
                vector_recv.at[0],
                in_group(index + 1),
            ).start()

        at = 0
        for layer in range(dims.layers):
            for ref, length in zip(vector_refs, dims.lengths):
                values = ref[...].astype(wide)
                for block in range(length):
                    lanes = slice(block * dims.rows, (block + 1) * dims.rows)
                    vector_here[at : at + 1, :] = values[layer : layer + 1, lanes]
                    at += 1
        vector_all[place.me] = vector_here[...]
        few(shards - 1, send_vector)
    x_copy = pltpu.make_async_copy(x_ref, both_hidden.at[0, pl.ds(0, tokens)], io_sem.at[0])
    cotangent_copy = pltpu.make_async_copy(cotangent, both_grad.at[pl.ds(0, tokens)], io_sem.at[1])
    x_copy.start()
    cotangent_copy.start()
    x_copy.wait()
    hidden_copy = to_mate(both_hidden.at[0, pl.ds(0, tokens)], both_hidden.at[0, pl.ds(tokens, tokens)])
    for gather in gathers:
        gather.begin()
    turns = []

    def turn_on():
        now = len(turns)
        turns.append(now)
        for number, gather in reversed(list(enumerate(gathers))):
            gather.reach(max(now - number + 1, 1 if number <= now + LEAD else 0))

    def prepare(at):
        last = max(
            number
            for number, gather in enumerate(gathers)
            if gather.layer * 4 + gather.kind == at
        )
        while len(turns) < last + gathers[last].stages:
            turn_on()

    hidden[...] = both_hidden[0, pl.ds(0, tokens)].astype(wide)
    vectors[...] = jnp.zeros(vectors.shape, wide)
    tops[...] = jnp.full(tops.shape, neg_large, wide)
    rows_copy.wait_recv()
    for s, row_ref in enumerate((seg_here, seg_rows)):
        row = row_ref[0:1, :]
        column = jnp.broadcast_to(row, (128, tokens)).T[:, 0:1]
        bias[s] = jnp.where(column == row, 0.0, neg_large)

    if dims.direct:
        vector_bytes(vector_all, 0, shards - 1).wait_recv()
        starts = [sum(dims.lengths[:member]) for member in range(9)]
        small[...] = jnp.zeros(small.shape, wide)
        for layer in range(dims.layers):
            base = layer * sum(dims.lengths)

            def spread(row, member, shard, at, layer=layer, base=base):
                for block in range(dims.lengths[member]):
                    lanes = pl.ds(at + block * dims.rows, dims.rows)
                    source = base + starts[member] + block
                    small[layer, row : row + 1, lanes] = vector_all[shard, source : source + 1, :]

            for shard in range(shards):
                for row, member in ((1, 2), (3, 4), (4, 5), (5, 6), (6, 7), (7, 8)):
                    spread(row, member, shard, shard * dims.rows)
            for pair in range(dims.pairs):
                shard = 2 * pair + place.half
                spread(0, 0, shard, pair * dims.rows)
                spread(0, 1, shard, 2 * dims.third + pair * dims.rows)
                spread(2, 3, shard, pair * dims.rows * dims.lengths[3])

    chunk = 32 if tokens % 32 == 0 else tokens

    def layer_norm(residual, partial, other, bias_row, gain_row, shift_row, normed, rstd_out, results):
        def body(j):
            rows = pl.ds(pl.multiple_of(j * chunk, chunk), chunk)
            value = residual[rows] + partial[rows] + other[rows].astype(wide) + bias_row
            centred = value - jnp.mean(value, axis=-1, keepdims=True)
            scale_row = lax.rsqrt(jnp.mean(centred * centred, axis=-1, keepdims=True) + epsilon)
            normal = centred * scale_row
            normed[rows] = normal
            rstd_out[rows] = jnp.broadcast_to(scale_row, (chunk, 128))
            results(rows, normal * gain_row + shift_row)

        tiles(tokens // chunk, body)

    flying = [None, None]

    def project(left, product, at):
        slot = at % 2
        if flying[slot] is not None:
            flying[slot].wait_send()
            settled.append(flying[slot])

        def far(j):
            cols = pl.ds(pl.multiple_of(j * tile, tile), tile)
            away[slot, :, cols] = product(left[pl.ds(tokens, tokens)], cols).astype(low)

        def near(j):
            cols = pl.ds(pl.multiple_of(j * tile, tile), tile)
            total[:, cols] = product(left[pl.ds(0, tokens)], cols)

        tiles(width // tile, far)
        flying[slot] = to_mate(away.at[slot], back.at[at % (2 * dims.layers)])
        tiles(width // tile, near)
        return flying[slot]

    settled = []
    tile = min(512, width)
    for layer in range(dims.layers):
        prepare(4 * layer)
        hidden_copy.wait_recv()

        def qkv_tile(j, layer=layer):
            cols = pl.ds(pl.multiple_of(j * tile, tile), tile)
            value = jnp.dot(both_hidden[layer], w_qkv[layer, :, cols], preferred_element_type=wide)
            qkv[layer, :, cols] = (value + small[layer, 0:1, cols]).astype(low)

        tiles(dims.kinds[0][2] // tile, qkv_tile)
        lane_blocks = dims.third // 128

        def attend(j, layer=layer):
            s, block = j // lane_blocks, j % lane_blocks
            rows = pl.ds(pl.multiple_of(s * tokens, tokens), tokens)

            def lanes(which):
                start = pl.multiple_of(which * dims.third + block * 128, 128)
                return qkv[layer, rows, pl.ds(start, 128)]

            query, key_rows, value_rows = lanes(0), lanes(1), lanes(2)
            mask = bias[s]
            outs = []
            for e in range(heads_row):
                part = slice(e * dims.head_dim, (e + 1) * dims.head_dim)
                scores = dot_last(query[:, part], key_rows[:, part]) * scale + mask
                top = jnp.max(scores, axis=1, keepdims=True)
                expo = jnp.exp(scores - top)
                prob = (expo * (1.0 / jnp.sum(expo, axis=1, keepdims=True))).astype(low)
                head = block * heads_row + e
                probs[layer, s * (lane_blocks * heads_row) + head] = prob
                outs.append(jnp.dot(prob, value_rows[:, part], preferred_element_type=wide))
                peak = jnp.broadcast_to(jnp.max(top, axis=0, keepdims=True), (1, 128))
                tops[layer, pl.ds(head, 1)] = jnp.maximum(tops[layer, pl.ds(head, 1)], peak)
            attended[layer, rows, pl.ds(pl.multiple_of(block * 128, 128), 128)] = jnp.concatenate(
                outs, axis=1
            ).astype(low)

        turn_on()
        tiles(lane_blocks, attend)
        turn_on()
        tiles(lane_blocks, lambda j, attend=attend: attend(j + lane_blocks))

        prepare(4 * layer + 1)
        project(
            attended.at[layer],
            lambda left, cols, layer=layer: jnp.dot(
                left, w_out[layer, :, cols], preferred_element_type=wide
            ),
            2 * layer,
        ).wait_recv()

        def first_rows(rows, value, layer=layer):
            first[rows] = value
            both_first[layer, rows] = value.astype(low)

        layer_norm(
            hidden,
            total,
            back.at[2 * layer],
            small[layer, 1:2, :width],
            small[layer, 4:5, :width],
            small[layer, 5:6, :width],
            norm1.at[layer],
            rstd.at[layer, 0],
            first_rows,
        )
        first_copy = to_mate(
            both_first.at[layer, pl.ds(0, tokens)], both_first.at[layer, pl.ds(tokens, tokens)]
        )

        prepare(4 * layer + 2)
        first_copy.wait_recv()
        narrow = 256

        def up_tile(j, layer=layer):
            cols = pl.ds(pl.multiple_of(j * narrow, narrow), narrow)
            pre = jnp.dot(both_first[layer], w_up[layer, :, cols], preferred_element_type=wide)
            value, steep = gelu_and_slope(pre + small[layer, 2:3, cols])
            act[layer, :, cols] = value.astype(low)
            slope[layer, :, cols] = steep.astype(low)

        tiles(dims.kinds[2][2] // narrow, up_tile)

        prepare(4 * layer + 3)
        project(
            act.at[layer],
            lambda left, cols, layer=layer: jnp.dot(
                left, w_down[layer, :, cols], preferred_element_type=wide
            ),
            2 * layer + 1,
        ).wait_recv()
        last = layer == dims.layers - 1

        def second_rows(rows, value, layer=layer, last=last):
            if last:
                output[rows] = value.astype(low)
            else:
                hidden[rows] = value
                both_hidden[layer + 1, rows] = value.astype(low)

        layer_norm(
            first,
            total,
            back.at[2 * layer + 1],
            small[layer, 3:4, :width],
            small[layer, 6:7, :width],
            small[layer, 7:8, :width],
            norm2.at[layer],
            rstd.at[layer, 1],
            second_rows,
        )
        if not last:
            hidden_copy = to_mate(
                both_hidden.at[layer + 1, pl.ds(0, tokens)],
                both_hidden.at[layer + 1, pl.ds(tokens, tokens)],
            )
    for gather in gathers:
        gather.finish_sends()
    queue = [
        [
            Reduce(
                place,
                layer,
                kind,
                cut,
                part,
                terms[kind],
                [arrived[turn][kind] for turn in range(dims.bits)],
                lines[kind],
                done[kind],
                swapped[kind // 2],
                (reduce_send, reduce_recv, own_sem),
                (add_mine, add_other, load_sem, store_sem),
            )
            for part in range(2)
        ]
        for layer in reversed(range(dims.layers))
        for kind in ((3, 2, 1, 0) if layer else (3, 2, 0, 1))
        for cut in range(dims.cuts[kind])
    ]
    stages = max(item.stages for pair in queue for item in pair)

    pools = [
        (ref, row, column)
        for ref in (w_down, w_up, act, slope, w_qkv)
        for row in range(0, ref.shape[1] - 255, 256)
        for column in range(0, ref.shape[2] - 1023, 1024)
    ]

    def together(items):
        work, used = [], 0
        for item in items:
            turn = item.stage - 1
            pieces = []
            for own, other, result in item.additions(turn):
                rows, cols = own.shape
                pair = []
                for ref in (own, other):
                    pool, row, column = pools[used]
                    slot = pool.at[dims.layers - 1, pl.ds(row, rows), pl.ds(column, cols)]
                    pair.append((slot, pltpu.make_async_copy(ref, slot, pool_load.at[used])))
                    used += 1
                back_copy = pltpu.make_async_copy(pair[0][0], result, pool_store.at[used // 2 - 1])
                pieces.append((pair, back_copy))
            work.append((item, turn, pieces))
        for item, turn, pieces in work:

            @when(item.taking_part(turn))
            def _(item=item, turn=turn, pieces=pieces):
                item.arrive(turn)
                for pair, _ in pieces:
                    for _, copy in pair:
                        copy.start()

        for item, turn, pieces in work:

            @when(item.taking_part(turn))
            def _(pieces=pieces):
                for pair, back_copy in pieces:
                    for _, copy in pair:
                        copy.wait()
                    one, two = pair[0][0], pair[1][0]
                    one[...] = one[...] + two[...]
                    back_copy.start()

        for item, turn, pieces in work:

            @when(item.taking_part(turn))
            def _(pieces=pieces):
                for _, back_copy in pieces:
                    back_copy.wait()

            item.depart(turn + 1)
            item.stage += 1

    def pump_together(step, ahead):
        if step + ahead < len(queue):
            for item in queue[step + ahead]:
                item.reach(1)
        for group in GROUPS:
            together(
                [
                    item
                    for behind in group
                    if 0 <= step - behind < len(queue)
                    for item in queue[step - behind]
                    if item.stage < min(2 + behind, item.stages)
                ]
            )

    def pump(step, ahead=AHEAD):
        if dims.direct:
            pump_together(step, ahead)
            return
        if step + ahead < len(queue):
            for item in queue[step + ahead]:
                item.reach(1)
        for behind in reversed(range(stages - 1)):
            at = step - behind
            if 0 <= at < len(queue):
                for item in queue[at]:
                    item.reach(2 + behind)

    def weight_terms(layer, kind, left, right):
        _, held, columns, _ = dims.kinds[kind]
        step = min(256, held)
        wide_cols = columns if columns <= ring.shape[2] else columns // 2
        across = columns // wide_cols
        count = (held // step) * across
        slots = ring.shape[0]

        def store(j):
            rows = pl.ds(pl.multiple_of((j // across) * step, step), step)
            cols = pl.ds(pl.multiple_of((j % across) * wide_cols, 128), wide_cols)
            return pltpu.make_async_copy(
                ring.at[j % slots, pl.ds(0, step), pl.ds(0, wide_cols)],
                terms[kind].at[layer, rows, cols],
                ring_sem.at[j % slots],
            )

        def body(j):
            @pl.when(j >= slots)
            def _():
                store(j - slots).wait()

            rows = pl.ds(pl.multiple_of((j // across) * step, step), step)
            cols = pl.ds(pl.multiple_of((j % across) * wide_cols, 128), wide_cols)
            ring[j % slots, pl.ds(0, step), pl.ds(0, wide_cols)] = dot_first(
                left[:, rows], right[:, cols]
            ).astype(low)
            store(j).start()

        tiles(count, body)
        for j in range(max(0, count - slots), count):
            store(j).wait()

    def count_up(layer, row, value, cols=None):
        cols = pl.ds(0, value.shape[1]) if cols is None else cols
        vectors[layer, pl.ds(row, 1), cols] += jnp.sum(value, axis=0, keepdims=True)

    def norm_grad(value, normed, scale_row, gain_row):
        grad = value * gain_row
        inner = jnp.mean(grad * normed, axis=-1, keepdims=True)
        return scale_row * (grad - jnp.mean(grad, axis=-1, keepdims=True) - normed * inner)

    def back_rows(j):
        return pl.ds(pl.multiple_of(j * chunk, chunk), chunk)

    grad_copy = None
    cotangent_copy.wait()
    pumped = 0
    for layer in reversed(range(dims.layers)):
        newest = layer == dims.layers - 1
        if grad_copy is not None:
            grad_copy.wait_send()
            settled.append(grad_copy)

        def second_back(j, layer=layer, newest=newest):
            rows = back_rows(j)
            value = both_grad[rows].astype(wide) if newest else hidden[rows]
            normed = norm2[layer, rows]
            count_up(layer, 7, value * normed)
            count_up(layer, 8, value)
            grad = norm_grad(value, normed, rstd[layer, 1, rows, 0:1], small[layer, 6:7, :width])
            first[rows] = grad
            rounded = grad.astype(low)
            both_grad[rows] = rounded
            count_up(layer, 4, rounded.astype(wide))

        tiles(tokens // chunk, second_back)
        grad_copy = to_mate(both_grad.at[pl.ds(0, tokens)], both_grad.at[pl.ds(tokens, tokens)])
        grad_copy.wait_recv()

        weight_terms(layer, 3, act.at[layer], both_grad)
        if newest:
            for item in queue[0] + queue[1]:
                item.reach(1)
        else:
            pump(pumped)
            pumped += 1

        def down_back(j, layer=layer):
            cols = pl.ds(pl.multiple_of(j * narrow, narrow), narrow)
            grad = dot_last(both_grad[...], w_down[layer, cols, :])
            rounded = (grad * slope[layer, :, cols].astype(wide)).astype(low)
            slope[layer, :, cols] = rounded
            count_up(layer, 3, rounded.astype(wide), cols)

        tiles(dims.hidden // 2 // narrow, down_back)
        weight_terms(layer, 2, both_first.at[layer], slope.at[layer])
        if newest:
            for item in queue[2]:
                item.reach(1)
        else:
            pump(pumped)
            pumped += 1
        exchange_at = 2 * (dims.layers - 1 - layer)
        project(
            slope.at[layer],
            lambda left, cols, layer=layer: dot_last(left, w_up[layer, cols, :]),
            2 * dims.layers + exchange_at,
        ).wait_recv()
        grad_copy.wait_send()
        settled.append(grad_copy)

        def first_back(j, layer=layer, exchange_at=exchange_at):
            rows = back_rows(j)
            value = first[rows] + total[rows] + back[exchange_at, rows].astype(wide)
            normed = norm1[layer, rows]
            count_up(layer, 5, value * normed)
            count_up(layer, 6, value)
            grad = norm_grad(value, normed, rstd[layer, 0, rows, 0:1], small[layer, 4:5, :width])
            first[rows] = grad
            rounded = grad.astype(low)
            both_grad[rows] = rounded
            count_up(layer, 2, rounded.astype(wide))

        tiles(tokens // chunk, first_back)
        grad_copy = to_mate(both_grad.at[pl.ds(0, tokens)], both_grad.at[pl.ds(tokens, tokens)])
        grad_copy.wait_recv()
        weight_terms(layer, 1, attended.at[layer], both_grad)

        out_tile = min(256, dims.third)

        def out_back(j, layer=layer):
            cols = pl.ds(pl.multiple_of(j * out_tile, out_tile), out_tile)
            attended[layer, :, cols] = dot_last(both_grad[...], w_out[layer, cols, :]).astype(low)

        tiles(dims.third // out_tile, out_back)
        pump(pumped)
        pumped += 1

        def attend_back(j, layer=layer):
            s, block = j // lane_blocks, j % lane_blocks
            rows = pl.ds(pl.multiple_of(s * tokens, tokens), tokens)
            lanes = pl.ds(pl.multiple_of(block * 128, 128), 128)

            def at(which):
                return pl.ds(pl.multiple_of(which * dims.third + block * 128, 128), 128)

            query, key_rows, value_rows = (qkv[layer, rows, at(which)] for which in range(3))
            grad_out = attended[layer, rows, lanes]
            grads = [[], [], []]
            for e in range(heads_row):
                part = slice(e * dims.head_dim, (e + 1) * dims.head_dim)
                prob = probs[layer, s * (lane_blocks * heads_row) + block * heads_row + e]
                grads[2].append(dot_first(prob, grad_out[:, part]))
                prob = prob.astype(wide)
                grad_prob = dot_last(grad_out[:, part], value_rows[:, part])
                inner = jnp.sum(prob * grad_prob, axis=1, keepdims=True)
                grad_score = (prob * (grad_prob - inner)).astype(low)
                grads[0].append(
                    jnp.dot(grad_score, key_rows[:, part], preferred_element_type=wide) * scale
                )
                grads[1].append(dot_first(grad_score, query[:, part]) * scale)
            for which, row in ((0, 0), (1, None), (2, 1)):
                rounded = jnp.concatenate(grads[which], axis=1).astype(low)
                qkv[layer, rows, at(which)] = rounded
                if row is not None:
                    count_up(layer, row, rounded.astype(wide), lanes)

        tiles(2 * lane_blocks, attend_back)
        pump(pumped)
        pumped += 1
        weight_terms(layer, 0, both_hidden.at[layer], qkv.at[layer])
        project(
            qkv.at[layer],
            lambda left, cols, layer=layer: dot_last(left, w_qkv[layer, cols, :]),
            2 * dims.layers + exchange_at + 1,
        ).wait_recv()

        def input_rows(j, exchange_at=exchange_at):
            rows = back_rows(j)
            hidden[rows] = first[rows] + total[rows] + back[exchange_at + 1, rows].astype(wide)

        tiles(tokens // chunk, input_rows)
        pump(pumped)
        pumped += 1

    grad_out_copy = pltpu.make_async_copy(hidden, input_grad, io_sem.at[0])
    grad_out_copy.start()

    if dims.direct:
        count = dims.vector_rows
        for shard in range(shards):
            for layer in range(dims.layers):
                at = layer * sum(dims.lengths)
                for member, length in enumerate(dims.lengths):
                    halved = member in (0, 1, 3)
                    for block in range(length):
                        first_lane = (shard // 2 if halved else shard) * length * dims.rows
                        lanes = pl.ds(first_lane + block * dims.rows, dims.rows)
                        value = vectors[layer, member : member + 1, lanes]
                        if halved:
                            value = jnp.where(place.half == shard % 2, value, 0.0)
                        vector_away[shard, at : at + 1, :] = value
                        at += 1
                heads = HEADS // 2
                vector_away[shard, pl.ds(count + layer * heads, heads)] = tops[layer]
        vector_back[place.me] = vector_away[place.me]

        def send_terms(index):
            target = in_group(index + 1)
            remote(
                vector_away.at[target[1]],
                vector_back.at[place.me],
                vector_send.at[1],
                vector_recv.at[1],
                target,
            ).start()

        few(shards - 1, send_terms)
    gathered = pumped + 1
    while pumped < len(queue) + stages:
        pump(pumped)
        pumped += 1
        if dims.direct and pumped == gathered:
            vector_bytes(vector_back, 1, shards - 1).wait_recv()
            total_rows = vector_back[0, pl.ds(0, count)]
            for shard in range(1, shards):
                total_rows = total_rows + vector_back[shard, pl.ds(0, count)]
            vector_out[...] = total_rows
            heads = dims.layers * HEADS // 2
            for half in range(2):
                peak = vector_back[half, pl.ds(count, heads)]
                for shard in range(2 + half, shards, 2):
                    peak = jnp.maximum(peak, vector_back[shard, pl.ds(count, heads)])
                peak_out[half] = peak
            line_back[place.rep, pl.ds(0, count)] = vector_out[...]
            for half in range(2):
                line_back[place.rep, pl.ds(count + half * heads, heads)] = peak_out[half]
            for step in range(1, reps):
                remote(
                    line_back.at[place.rep],
                    line_back.at[place.rep],
                    vector_send.at[2],
                    vector_recv.at[2],
                    ((place.rep + step) % reps, place.me),
                ).start()
    if dims.direct:
        vector_bytes(line_back, 2, reps - 1).wait_recv()
        total_rows = line_back[0, pl.ds(0, count)]
        for other in range(1, reps):
            total_rows = total_rows + line_back[other, pl.ds(0, count)]
        vector_out[...] = total_rows
        for half in range(2):
            peak = line_back[0, pl.ds(count + half * heads, heads)]
            for other in range(1, reps):
                peak = jnp.maximum(peak, line_back[other, pl.ds(count + half * heads, heads)])
            peak_out[half] = peak

    for copy in exchanges:
        if not any(copy is other for other in settled):
            copy.wait_send()
    if dims.direct:
        vector_bytes(vector_all, 0, shards - 1).wait_send()
        vector_bytes(vector_back, 1, shards - 1).wait_send()
        vector_bytes(line_back, 2, reps - 1).wait_send()
    for pair in queue:
        for item in pair:
            item.finish_sends()
    grad_out_copy.wait()


def run_layers(dims, x, cotangent, segments, vectors, weights):
    layers, tokens, width = dims.layers, dims.tokens, dims.width
    both = 2 * tokens

    def shape(dims_of, dtype):
        return jax.ShapeDtypeStruct(dims_of, dtype)

    held = [shape((layers, rows, columns), low) for _, rows, columns, _ in dims.kinds]
    pair_rows = [rows * (2 if paired else 1) for rows, _, _, paired in dims.kinds]
    columns = [kind[2] for kind in dims.kinds]
    heads = HEADS // 2
    summed = []
    if dims.direct:
        summed = [
            shape((dims.vector_rows, dims.rows), wide),
            shape((2, layers * heads, 128), wide),
        ]
    outs = (
        [
            shape((tokens, width), low),
            shape((layers, HEADS // 2, 128), wide),
            shape((layers, 16, dims.hidden // 2), wide),
            shape((tokens, width), wide),
        ]
        + summed
        + held * (1 + dims.bits)
        + [shape((layers, dims.reps // 2, r, c), low) for r, c in zip(pair_rows, columns)]
        + [shape((layers, r, c), low) for r, c in zip(pair_rows, columns)]
        + [
            shape((layers, dims.rows, columns[kind] * (2 if dims.direct else 1)), low)
            for kind in (0, 2)
        ]
    )
    vmem = pl.BlockSpec(memory_space=pltpu.VMEM)
    anywhere = pl.BlockSpec(memory_space=pl.ANY)
    dma = pltpu.SemaphoreType.DMA
    scratch = [pltpu.VMEM(item.shape, item.dtype) for item in held] + [
        pltpu.VMEM(*item)
        for item in (
            ((layers, both, width), low),
            ((layers, both, 3 * dims.third), low),
            ((layers, both, dims.third), low),
            ((layers, HEADS, tokens, tokens), low),
            ((layers, tokens, width), wide),
            ((layers, both, width), low),
            ((layers, both, dims.hidden // 2), low),
            ((layers, both, dims.hidden // 2), low),
            ((layers, tokens, width), wide),
            ((layers, 2, tokens, 128), wide),
            ((tokens, width), wide),
            ((tokens, width), wide),
            ((tokens, width), wide),
            ((2, tokens, width), low),
            ((2 * layers, tokens, width), low),
            ((2, tokens, tokens), wide),
            ((both, width), low),
            ((3, 256, 1024), low),
            ((2, 256, 1024), low),
            ((2, 256, 1024), low),
            ((8, tokens), wide),
            ((8, tokens), wide),
        )
    ]
    if dims.direct:
        rows = dims.vector_rows
        scratch += [
            pltpu.VMEM(item, wide)
            for item in (
                (dims.shards, rows, dims.rows),
                (layers, 8, dims.hidden // 2),
                (dims.shards, rows + layers * heads, dims.rows),
                (dims.shards, rows + layers * heads, dims.rows),
                (dims.reps, rows + 2 * layers * heads, dims.rows),
                (rows, dims.rows),
            )
        ]
    slots = 2 + 2 * dims.bits
    exchange_count = 2 + 8 * layers
    reduce_slots = dims.bits + dims.reps
    scratch = scratch + [
        dma((4 * layers * CUTS,)),
        dma((4 * layers * CUTS, slots)),
        dma((4 * layers * CUTS, slots)),
        dma((exchange_count,)),
        dma((exchange_count,)),
        dma((8 * layers * CUTS, reduce_slots)),
        dma((8 * layers * CUTS, reduce_slots)),
        dma((8 * layers * CUTS,)),
        dma((2, 2)),
        dma((2,)),
        dma((3,)),
        dma((2,)),
    ]
    if dims.direct:
        scratch += [dma((3,)), dma((3,)), dma((32,)), dma((16,))]
    return pl.pallas_call(
        functools.partial(layers_kernel, dims),
        out_shape=outs,
        in_specs=[anywhere] * 2 + [vmem] * (1 + len(vectors)) + [anywhere] * 4,
        out_specs=[vmem] * 3 + [anywhere] + [vmem] * len(summed) + [anywhere] * (len(outs) - 4 - len(summed)),
        scratch_shapes=scratch,
        compiler_params=pltpu.CompilerParams(
            collective_id=0, has_side_effects=True, vmem_limit_bytes=63 * 2**20 + 2**19
        ),
        name="layers",
    )(x, cotangent, segments, *vectors, *weights)


def own_rows(net, value):
    layers, rows, columns = value.shape
    split = value.reshape(layers, 2, rows // 2, columns)
    return lax.dynamic_index_in_dim(split, net.core, 1, keepdims=False)


def gathered_vectors(net, dims, packed):
    lengths = dims.lengths
    packed = net.in_order(packed, net.over_core(packed), net.core)
    packed = net.rows_in_order(net.gather_chips(packed, list(range(net.bits))))

    def whole(layer, member):
        start = sum(lengths[:member])
        return packed[:, layer, start : start + lengths[member]].astype(wide)

    def of_core(layer, member):
        split = whole(layer, member).reshape(net.high, 2, -1)
        return lax.dynamic_index_in_dim(split, net.core, 1, keepdims=False).reshape(-1)

    def wide_row(row):
        return jnp.pad(row, (0, dims.hidden // 2 - row.shape[0]))

    def rows(layer):
        bias_q = of_core(layer, 0)
        bias_qkv = jnp.concatenate([bias_q, jnp.zeros_like(bias_q), of_core(layer, 1)])
        singles = [whole(layer, member).reshape(-1) for member in (2, 4, 5, 6, 7, 8)]
        return [bias_qkv, singles[0], of_core(layer, 3)] + singles[1:]

    return jnp.stack(
        [jnp.stack([wide_row(row) for row in rows(layer)]) for layer in range(dims.layers)]
    )


def summed_vectors(net, dims, vectors, tops):
    layers, lengths, rows = dims.layers, dims.lengths, dims.rows
    half_width, half_hidden = dims.third, dims.hidden // 2
    here = (half_width, half_width, dims.width, half_hidden) + (dims.width,) * 5

    def placed(value, member):
        if member in (0, 1, 3):
            value = value.reshape(net.high, 1, net.step, lengths[member], rows)
            zero = jnp.zeros_like(value)
            first = net.core == 0
            return jnp.concatenate(
                [jnp.where(first, value, zero), jnp.where(first, zero, value)], axis=1
            )
        return value.reshape(net.high, 2, net.step, lengths[member], rows)

    terms = jnp.stack(
        [
            jnp.concatenate(
                [placed(vectors[layer, row, :size], row) for row, size in enumerate(here)], axis=3
            )
            for layer in range(layers)
        ],
        axis=3,
    )
    theirs = lax.dynamic_index_in_dim(terms, 1 - net.core, 1, keepdims=False)
    ours = lax.dynamic_index_in_dim(terms, net.core, 1, keepdims=False)
    terms = ours + net.over_core(theirs)
    terms = terms.reshape((net.pairs,) + terms.shape[2:])
    terms = net.sum_reps(net.scatter_chips(terms, list(range(net.bits))))

    local = tops[:, :, 0]
    local = net.in_order(local, net.over_core(local), net.core)
    local = local.reshape(2, layers, net.high, -1).transpose(1, 2, 0, 3).reshape(layers, HEADS)
    for bit in range(net.bits):
        local = jnp.maximum(local, net.over_bit(local, bit))
    step = 1
    while step < net.reps:
        swap = [(i, i ^ step) for i in range(net.reps)]
        local = jnp.maximum(local, lax.ppermute(local, "rep", swap))
        step *= 2
    return terms, local


def shards(
    inputs,
    cotangent,
    segments,
    w_qkv,
    w_out,
    w_up,
    w_down,
    bias_query,
    bias_value,
    bias_out,
    bias_up,
    bias_down,
    norm1_gain,
    norm1_bias,
    norm2_gain,
    norm2_bias,
    tau,
    *,
    shard_count,
    rep_count,
):
    layer_count = w_qkv.shape[0]
    width = w_qkv.shape[2] // 3
    rows_here = bias_query.shape[1]
    head_dim = width // HEADS
    net = Net(shard_count, rep_count, max(1, head_dim // rows_here))

    vectors = (
        bias_query,
        bias_value,
        bias_out,
        bias_up,
        bias_down,
        norm1_gain,
        norm1_bias,
        norm2_gain,
        norm2_bias,
    )
    lengths = [vector.shape[1] // rows_here for vector in vectors]
    tokens = inputs.shape[0]
    dims = Dims(shard_count, rep_count, net.step, layer_count, tokens, width, w_up.shape[2])
    if dims.direct:
        vector_in = vectors
        matrices = (w_qkv, w_out, w_up, w_down)
    else:
        packed = jnp.concatenate(
            [vector.reshape(layer_count, -1, rows_here) for vector in vectors], axis=1
        )
        vector_in = (gathered_vectors(net, dims, packed),)
        matrices = (by_half(w_qkv, net, 3), w_out, by_half(w_up, net, 1), w_down)
    results = run_layers(dims, inputs, cotangent, segments, vector_in, matrices)
    output, tops, vector_terms, input_grad = results[:4]
    done, swapped = results[-6:-2], results[-2:]

    if dims.direct:
        vector_grads, peak = results[4:6]
        vector_grads = vector_grads.reshape(layer_count, -1, rows_here)
        peak = peak[:, :, 0].reshape(2, layer_count, net.high, -1)
        peak = peak.transpose(1, 2, 0, 3).reshape(layer_count, HEADS)
        full = swapped[0], done[1], swapped[1], done[3]
    else:
        vector_grads, peak = summed_vectors(net, dims, vector_terms, tops)
        paired = [whole_columns(own_rows(net, done[k]), swapped[k // 2], net, 3 - k) for k in (0, 2)]
        full = paired[0], done[1], paired[1], done[3]
    large = tuple(value.astype(wide) for value in full)
    ends = [sum(lengths[: member + 1]) for member in range(len(lengths))]
    vector_grads = [
        vector_grads[:, end - length : end].reshape(layer_count, -1)
        for end, length in zip(ends, lengths)
    ]
    factor = jnp.sqrt(tau / jnp.maximum(peak, tau))
    column_scale = jnp.repeat(factor, head_dim, axis=1)
    both_scale = jnp.concatenate([column_scale, column_scale], axis=1)
    clipped_qk = w_qkv[:, :, : 2 * width].astype(wide) * both_scale[:, None, :]
    start = lax.axis_index("shard") * rows_here
    scale_here = lax.dynamic_slice_in_dim(column_scale, start, rows_here, 1)
    clipped_bias_query = bias_query.astype(wide) * scale_here
    return (output, input_grad) + large + tuple(vector_grads) + (clipped_qk, clipped_bias_query)


def solution(mesh):
    tokens = P(("rep", "shard"), None)
    matrix = P(None, "shard", None)
    vector = P(None, "shard")
    in_specs = (tokens, tokens, tokens) + (matrix,) * 4 + (vector,) * 9 + (P(),)
    out_specs = (tokens, tokens) + (matrix,) * 4 + (vector,) * 9 + (matrix, vector)

    def local(*arrays):
        return shards(*arrays, shard_count=mesh.shape["shard"], rep_count=mesh.shape["rep"])

    return jax.shard_map(local, mesh=mesh, in_specs=in_specs, out_specs=out_specs, check_vma=False)
```

```python
import functools
import math

import jax
import jax.numpy as jnp
from jax import lax
from jax.experimental import pallas as pl
from jax.experimental.pallas import tpu as pltpu
from jax.sharding import PartitionSpec as P

HEADS = 16
MESH = pl.DeviceIdType.MESH
LEAD = 1
CUTS = 2
AHEAD = 1
GROUPS = ((0,), (1, 2, 3, 4, 5))
IN_PLANE_FIRST = (11, 10, 10, 12)
IN_PLANE = (11, 10, 10, 12)


epsilon = 1e-05
neg_large = -1e30
low = jnp.bfloat16
wide = jnp.float32


class Net:
    def __init__(self, shards, reps, step):
        self.shards = shards
        self.reps = reps
        self.step = step
        self.pairs = shards // 2
        self.high = shards // (2 * step)
        self.bits = self.pairs.bit_length() - 1
        self.me = lax.axis_index("shard")
        self.core = (self.me // step) % 2
        self.rep = lax.axis_index("rep")

    def over_core(self, value):
        return lax.ppermute(value, "shard", [(i, i ^ self.step) for i in range(self.shards)])

    def stride(self, bit):
        return (1 << bit) if (1 << bit) < self.step else (2 << bit)

    def over_bit(self, value, bit):
        step = self.stride(bit)
        return lax.ppermute(value, "shard", [(i, i ^ step) for i in range(self.shards)])

    def chip_bit(self, bit):
        return (self.me // self.stride(bit)) % 2

    def rows_in_order(self, value):
        rest = value.shape[2:]
        value = value.reshape((self.high, self.step, 2) + rest)
        return jnp.swapaxes(value, 1, 2).reshape((self.shards,) + rest)

    def rows_by_pair(self, value):
        rest = value.shape[1:]
        value = value.reshape((self.high, 2, self.step) + rest)
        return jnp.swapaxes(value, 1, 2).reshape((self.pairs, 2) + rest)

    def in_order(self, mine, other, place):
        first = place == 0
        return jnp.stack([jnp.where(first, mine, other), jnp.where(first, other, mine)])

    def gather_chips(self, piece, order):
        shape = piece.shape
        for bit in order:
            piece = self.in_order(piece, self.over_bit(piece, bit), self.chip_bit(bit))
        axes = list(reversed(order))
        natural = [axes.index(bit) for bit in reversed(range(self.bits))]
        rest = list(range(self.bits, self.bits + len(shape)))
        return piece.transpose(natural + rest).reshape((self.pairs,) + shape)

    def scatter_chips(self, value, order):
        rest = value.shape[1:]
        value = value.reshape((2,) * self.bits + rest)
        left = list(reversed(range(self.bits)))
        for bit in order:
            axis = left.index(bit)
            place = self.chip_bit(bit)
            theirs = lax.dynamic_index_in_dim(value, 1 - place, axis, keepdims=False)
            ours = lax.dynamic_index_in_dim(value, place, axis, keepdims=False)
            got = self.over_bit(theirs, bit)
            value = (ours.astype(wide) + got.astype(wide)).astype(value.dtype)
            left.remove(bit)
        return value

    def sum_reps(self, value):
        reps, half = self.reps, self.reps // 2

        def add(one, other):
            return (one.astype(wide) + other.astype(wide)).astype(value.dtype)

        total = value
        for i in range(half - 1):
            got = lax.ppermute(total, "rep", [(i, i + 1), (reps - 1 - i, reps - 2 - i)])
            total = add(total, got)
        total = add(total, lax.ppermute(total, "rep", [(half - 1, half), (half, half - 1)]))
        for i in reversed(range(half - 1)):
            got = lax.ppermute(total, "rep", [(i + 1, i), (reps - 2 - i, reps - 1 - i)])
            outer = jnp.logical_or(self.rep == i, self.rep == reps - 1 - i)
            total = jnp.where(outer, got, total)
        return total


def by_half(weight, net, groups):
    layers, rows, columns = weight.shape
    split = weight.reshape(layers, rows, groups * net.high, 2, columns // (2 * groups * net.high))
    return split.transpose(0, 3, 1, 2, 4).reshape(layers, 2, rows, columns // 2)


def whole_columns(mine, other, net, groups):
    layers, rows, columns = mine.shape
    block = columns // (groups * net.high)
    both = [part.reshape(layers, rows, groups * net.high, block) for part in (mine, other)]
    first = net.core == 0
    stacked = jnp.stack(
        [jnp.where(first, both[0], both[1]), jnp.where(first, both[1], both[0])], axis=3
    )
    return stacked.reshape(layers, rows, 2 * columns).astype(wide)


class Place:
    def __init__(self, dims):
        self.dims = dims
        step = dims.step
        self.rep = lax.axis_index("rep")
        self.me = lax.axis_index("shard")
        self.half = (self.me // step) % 2
        self.pair = (self.me // (2 * step)) * step + self.me % step
        self.plane = self.rep % 2

    def flip(self, value, bit):
        size = 1 << bit
        return value + size * (1 - 2 * ((value // size) % 2))

    def mate(self):
        return (self.rep, self.me + self.dims.step * (1 - 2 * self.half))

    def over_bit(self, bit):
        stride = (1 << bit) if (1 << bit) < self.dims.step else (2 << bit)
        return (self.rep, self.me + stride * (1 - 2 * ((self.me // stride) % 2)))

    def over_plane(self):
        return (self.rep + 1 - 2 * self.plane, self.me)

    def first_shard(self, pair):
        step = self.dims.step
        return (pair // step) * (2 * step) + pair % step


class Dims:
    def __init__(self, shards, reps, step, layers, tokens, width, hidden):
        self.shards, self.reps, self.step = shards, reps, step
        self.pairs = shards // 2
        self.bits = self.pairs.bit_length() - 1
        self.layers, self.tokens, self.width, self.hidden = layers, tokens, width, hidden
        self.head_dim = width // HEADS
        self.third = width // 2
        self.rows = width // shards
        self.kinds = (
            (self.rows, width, 3 * width // 2, True),
            (self.rows, width // 2, width, False),
            (self.rows, width, hidden // 2, True),
            (hidden // shards, hidden // 2, width, False),
        )
        high = shards // (2 * step)
        self.block = (width // (2 * high), None, hidden // (2 * high), None)
        self.blocks = (3 * high, None, high, None)
        self.lengths = (1, 1, 1, hidden // width, 1, 1, 1, 1, 1)
        self.vector_rows = layers * sum(self.lengths)
        self.direct = self.rows % 128 == 0 and step == 1
        self.cuts = tuple(CUTS if self.direct and kind != 1 else 1 for kind in range(4))


def remote(src, dst, send, recv, where):
    return pltpu.make_async_remote_copy(
        src_ref=src, dst_ref=dst, send_sem=send, recv_sem=recv, device_id=where, device_id_type=MESH
    )


class Gather:
    def __init__(self, place, layer, kind, cut, source, whole, sems, last):
        self.place, self.dims = place, place.dims
        self.layer, self.kind = layer, kind
        self.source, self.whole = source, whole
        self.rows, self.held, columns, self.paired = self.dims.kinds[kind]
        self.local, self.send, self.recv = sems
        self.cut, self.cuts = cut, self.dims.cuts[kind]
        self.columns = columns // self.cuts
        self.base = cut * self.columns
        self.at = (layer * 4 + kind) * CUTS + cut
        self.in_plane = in_plane = in_plane_columns(self.dims, layer, kind, self.columns, last)
        self.stage = 0
        self.stages = self.dims.bits + (2 if in_plane < self.columns else 1)

    def blocks(self, pair):
        if not self.paired:
            return [pair * self.rows], self.rows
        first = self.place.first_shard(pair) * self.rows
        if self.dims.step == 1:
            return [first], 2 * self.rows
        return [first, first + self.dims.step * self.rows], self.rows

    def window(self, part):
        size = self.in_plane // 2
        if (size % 128) and part < 2:
            low_size = size // 128 * 128
            size = low_size if part == 0 else self.in_plane - low_size
            offset = 0 if part == 0 else low_size
        else:
            offset = part * size
        start = self.base + self.place.plane * (self.columns - self.in_plane) + offset
        return pl.ds(pl.multiple_of(start, 128), size), size

    def order(self, part):
        bits = list(range(self.dims.bits))
        return bits if part == 0 else bits[::-1]

    def subset(self, done):
        pairs = [self.place.pair]
        for bit in done:
            pairs = pairs + [self.place.flip(pair, bit) for pair in pairs]
        return pairs

    def begin(self):
        place = self.place
        if self.paired:
            mine = place.me * self.rows
            rows = pl.ds(pl.multiple_of(mine, 16), self.rows)
            for theirs, ours in self.begin_blocks():
                pltpu.make_async_copy(
                    ours, self.whole.at[self.layer, rows, theirs[1]], self.local.at[self.at]
                ).start()
            for theirs, ours in self.begin_blocks():
                remote(
                    theirs[0],
                    self.whole.at[self.layer, rows, theirs[1]],
                    self.send.at[self.at, 0],
                    self.recv.at[self.at, 0],
                    place.mate(),
                ).start()
        else:
            rows = pl.ds(pl.multiple_of(place.pair * self.rows, 16), self.rows)
            columns = pl.ds(self.base, self.columns)
            pltpu.make_async_copy(
                self.source.at[self.layer, :, columns],
                self.whole.at[self.layer, rows, columns],
                self.local.at[self.at],
            ).start()

    def begin_blocks(self):
        place, width = self.place, self.dims.block[self.kind]
        if not self.dims.direct:
            every = pl.ds(0, self.columns)
            yield (
                (self.source.at[self.layer, 1 - place.half], every),
                self.source.at[self.layer, place.half],
            )
            return
        count = self.dims.blocks[self.kind] // self.cuts
        for block in range(self.cut * count, (self.cut + 1) * count):
            to = pl.ds(block * width, width)
            starts = [(2 * block + half) * width for half in (1 - place.half, place.half)]
            theirs, ours = (
                self.source.at[self.layer, :, pl.ds(pl.multiple_of(start, 128), width)] for start in starts
            )
            yield (theirs, to), ours

    def some(self, rows, columns):
        return self.whole.at[self.layer, pl.ds(0, rows), columns]

    def phase(self, turn):
        place = self.place
        for part in range(2):
            order = self.order(part)
            columns, _ = self.window(part)
            for pair in self.subset(order[:turn]):
                starts, count = self.blocks(pair)
                for start in starts:
                    block = self.whole.at[self.layer, pl.ds(pl.multiple_of(start, 16), count), columns]
                    remote(
                        block,
                        block,
                        self.send.at[self.at, 1 + 2 * turn + part],
                        self.recv.at[self.at, 1 + 2 * turn + part],
                        place.over_bit(order[turn]),
                    ).start()

    def phase_bytes(self, turn, part):
        columns = pl.ds(0, self.window(part)[1])
        per_pair = self.rows * (2 if self.paired else 1)
        block = self.some(per_pair << turn, columns)
        at = 1 + 2 * turn + part
        return remote(block, block, self.send.at[self.at, at], self.recv.at[self.at, at], self.place.mate())

    def across(self):
        place = self.place
        size = self.columns - self.in_plane
        columns = pl.ds(pl.multiple_of(self.base + place.plane * self.in_plane, 128), size)
        at = 1 + 2 * self.dims.bits
        for pair in self.subset(range(self.dims.bits))[1:]:
            starts, count = self.blocks(pair)
            for start in starts:
                block = self.whole.at[self.layer, pl.ds(pl.multiple_of(start, 16), count), columns]
                remote(block, block, self.send.at[self.at, at], self.recv.at[self.at, at], place.over_plane()).start()

    def across_bytes(self):
        per_pair = self.rows * (2 if self.paired else 1)
        block = self.some(per_pair * (self.dims.pairs - 1), pl.ds(0, self.columns - self.in_plane))
        at = 1 + 2 * self.dims.bits
        return remote(block, block, self.send.at[self.at, at], self.recv.at[self.at, at], self.place.over_plane())

    def own_bytes(self):
        if not self.paired:
            return None
        block = self.some(self.rows, pl.ds(0, self.columns))
        return remote(block, block, self.send.at[self.at, 0], self.recv.at[self.at, 0], self.place.mate())

    def advance(self):
        if self.stage == 0:
            own = self.some(self.rows, pl.ds(0, self.columns))
            pltpu.make_async_copy(own, own, self.local.at[self.at]).wait()
            if self.paired:
                self.own_bytes().wait_recv()
        elif self.stage <= self.dims.bits:
            for part in range(2):
                self.phase_bytes(self.stage - 1, part).wait_recv()
        else:
            self.across_bytes().wait_recv()
        if self.stage < self.dims.bits:
            self.phase(self.stage)
        elif self.stage + 1 < self.stages:
            self.across()
        self.stage += 1

    def reach(self, stage):
        while self.stage < min(stage, self.stages):
            self.advance()

    def finish_sends(self):
        if self.paired:
            self.own_bytes().wait_send()
        for turn in range(self.dims.bits):
            for part in range(2):
                self.phase_bytes(turn, part).wait_send()
        if self.in_plane < self.columns:
            self.across_bytes().wait_send()


class Reduce:
    def __init__(self, place, layer, kind, cut, part, terms, arrived, lines, done, swapped, sems, bufs):
        self.place, self.dims = place, place.dims
        self.layer, self.kind, self.part = layer, kind, part
        self.terms, self.arrived, self.lines, self.done, self.swapped = terms, arrived, lines, done, swapped
        self.send, self.recv, self.own_sem = sems
        self.mine, self.other, self.load_sem, self.store_sem = bufs
        self.rows, self.held, self.columns, self.paired = self.dims.kinds[kind]
        cuts = self.dims.cuts[kind]
        self.slice_at, self.slices = cut * 2 + part, 2 * cuts
        self.size = self.columns // self.slices
        self.columns_here = pl.ds(self.slice_at * self.size, self.size)
        self.at = ((layer * 4 + kind) * CUTS + cut) * 2 + part
        bits = list(range(self.dims.bits))
        self.order = bits if part == 0 else bits[::-1]
        self.moves = self.dims.reps - 1
        self.stage = 0
        self.stages = 1 + self.dims.bits + self.moves + (1 if self.paired else 0)
        self.split = self.paired and self.dims.step > 1
        self.piece = self.rows * (2 if self.paired and not self.split else 1)
        self.pieces = 2 if self.split else 1

    def row_of(self, pair, which):
        if not self.paired:
            return pair * self.rows
        return (self.place.first_shard(pair) + which * self.dims.step) * self.rows

    def sems(self, slot):
        return self.send.at[self.at, slot], self.recv.at[self.at, slot]

    def kept(self, index, turn, away):
        pair = self.place.pair
        for i, bit in enumerate(self.order[turn + 1 :]):
            size = 1 << bit
            wanted = (index // (1 << i)) % 2
            pair = pair + size * (wanted - (self.place.pair // size) % 2)
        if away:
            pair = self.place.flip(pair, self.order[turn])
        return pair

    def count(self, turn):
        return (self.dims.pairs >> (turn + 1)) * self.pieces

    def loop(self, count, body):
        if count <= 4:
            for i in range(count):
                body(i)
        else:
            tiles(count, body)

    def block(self, ref, index, turn, away):
        pair = self.kept(index // self.pieces, turn, away)
        start = self.row_of(pair, index % self.pieces)
        return ref.at[self.layer, pl.ds(pl.multiple_of(start, 16), self.piece), self.columns_here]

    def start_turn(self, turn):
        def one(index):
            remote(
                self.block(self.terms, index, turn, True),
                self.block(self.arrived[turn], index, turn, True),
                *self.sems(turn),
                self.place.over_bit(self.order[turn]),
            ).start()

        self.loop(self.count(turn), one)

    def turn_bytes(self, turn):
        ref = self.terms.at[self.layer, pl.ds(0, self.count(turn) * self.piece), self.columns_here]
        return remote(ref, ref, *self.sems(turn), self.place.over_bit(self.order[turn]))

    def add(self, count, own, other, result):
        step = min(self.piece, self.mine.shape[1])
        per = self.piece // step
        total = count * per

        def part_of(make, index):
            ref = make(index // per)
            return ref.at[pl.ds(pl.multiple_of((index % per) * step, 16), step)]

        def slots(index):
            slot = index % 2
            rows, cols = pl.ds(0, step), pl.ds(0, self.size)
            return self.mine.at[slot, rows, cols], self.other.at[slot, rows, cols], slot

        def load(index):
            one, two, slot = slots(index)
            return (
                pltpu.make_async_copy(part_of(own, index), one, self.load_sem.at[slot, 0]),
                pltpu.make_async_copy(part_of(other, index), two, self.load_sem.at[slot, 1]),
            )

        def store(index):
            one, _, slot = slots(index)
            return pltpu.make_async_copy(one, part_of(result, index), self.store_sem.at[slot])

        def body(index, first, last):
            @when(jnp.logical_not(last) if not isinstance(last, bool) else not last)
            def _():
                @when(jnp.logical_not(first) if not isinstance(first, bool) else not first)
                def _():
                    store(index - 1).wait()

                for copy in load(index + 1):
                    copy.start()

            for copy in load(index):
                copy.wait()
            one, two, _ = slots(index)
            one[...] = (one[...].astype(wide) + two[...].astype(wide)).astype(low)
            store(index).start()

        for copy in load(0):
            copy.start()
        if total <= 4:
            for index in range(total):
                body(index, index == 0, index == total - 1)
        else:
            tiles(total, lambda index: body(index, index == 0, index == total - 1))
        if total > 1:
            store(total - 2).wait()
        store(total - 1).wait()

    def finish_turn(self, turn):
        self.turn_bytes(turn).wait_recv()
        self.add(
            self.count(turn),
            lambda index: self.block(self.terms, index, turn, False),
            lambda index: self.block(self.arrived[turn], index, turn, False),
            lambda index: self.block(self.terms, index, turn, False),
        )

    def own(self, which):
        start = self.row_of(self.place.pair, which)
        return self.terms.at[self.layer, pl.ds(pl.multiple_of(start, 16), self.piece), self.columns_here]

    def line(self, move, which):
        return self.lines.at[self.layer, move, pl.ds(which * self.piece, self.piece), self.columns_here]

    def final(self, which):
        return self.done.at[self.layer, pl.ds(which * self.piece, self.piece), self.columns_here]

    def roles(self, move):
        reps, half = self.dims.reps, self.dims.reps // 2
        if move < half - 1:
            return (move, reps - 1 - move), (move + 1, reps - 2 - move)
        if move == half - 1:
            return (half - 1, half), (half, half - 1)
        back = reps - 2 - move
        return (back + 1, reps - 2 - back), (back, reps - 1 - back)

    def move_copies(self, move, target):
        half = self.dims.reps // 2
        slot = self.dims.bits + move
        for which in range(self.pieces):
            src = self.own(which) if move < half else self.final(which)
            dst = self.line(move, which) if move < half else self.final(which)
            yield remote(src, dst, *self.sems(slot), (target, self.place.me))

    def move_bytes(self, move):
        slot = self.dims.bits + move
        ref = self.done.at[self.layer, pl.ds(0, self.pieces * self.piece), self.columns_here]
        return remote(ref, ref, *self.sems(slot), self.place.mate())

    def start_move(self, move):
        senders, receivers = self.roles(move)
        for sender, receiver in zip(senders, receivers):

            @pl.when(self.place.rep == sender)
            def _(receiver=receiver):
                for copy in self.move_copies(move, receiver):
                    copy.start()

    def finish_move(self, move):
        half = self.dims.reps // 2
        _, receivers = self.roles(move)

        @pl.when(jnp.logical_or(self.place.rep == receivers[0], self.place.rep == receivers[1]))
        def _():
            self.move_bytes(move).wait_recv()
            if move < half:
                self.add(
                    self.pieces,
                    self.own,
                    lambda which: self.line(move, which),
                    self.own if move < half - 1 else self.final,
                )

    def part_blocks(self):
        width = self.dims.block[self.kind]
        count = self.dims.blocks[self.kind] // self.slices
        for block in range(self.slice_at * count, (self.slice_at + 1) * count):
            place = (2 * block + self.place.half) * width
            yield pl.ds(block * width, width), pl.ds(pl.multiple_of(place, 128), width)

    def rows_done(self, half, columns):
        start = pl.multiple_of(half * self.rows, 16)
        return self.done.at[self.layer, pl.ds(start, self.rows), columns]

    def start_swap(self):
        slot = self.sems(self.dims.bits + self.moves)
        if not self.dims.direct:
            remote(
                self.rows_done(1 - self.place.half, self.columns_here),
                self.swapped.at[self.layer, pl.ds(0, self.rows), self.columns_here],
                *slot,
                self.place.mate(),
            ).start()
            return
        for here, there in self.part_blocks():
            remote(
                self.rows_done(1 - self.place.half, here),
                self.swapped.at[self.layer, pl.ds(0, self.rows), there],
                *slot,
                self.place.mate(),
            ).start()
        for here, there in self.part_blocks():
            pltpu.make_async_copy(
                self.rows_done(self.place.half, here),
                self.swapped.at[self.layer, pl.ds(0, self.rows), there],
                self.own_sem.at[self.at],
            ).start()

    def swap_bytes(self):
        ref = self.done.at[self.layer, pl.ds(0, self.rows), self.columns_here]
        return remote(ref, ref, *self.sems(self.dims.bits + self.moves), self.place.mate())

    def finish_swap(self):
        self.swap_bytes().wait_recv()
        if self.dims.direct:
            ref = self.done.at[self.layer, pl.ds(0, self.rows), self.columns_here]
            pltpu.make_async_copy(ref, ref, self.own_sem.at[self.at]).wait()

    def advance(self):
        bits = self.dims.bits
        if self.stage == 0:
            self.start_turn(0)
        elif self.stage < bits:
            self.finish_turn(self.stage - 1)
            self.start_turn(self.stage)
        elif self.stage == bits:
            self.finish_turn(bits - 1)
            self.start_move(0)
        elif self.stage < bits + self.moves:
            self.finish_move(self.stage - bits - 1)
            self.start_move(self.stage - bits)
        elif self.stage == bits + self.moves:
            self.finish_move(self.moves - 1)
            if self.paired:
                self.start_swap()
        else:
            self.finish_swap()
        self.stage += 1

    def additions(self, turn):
        bits, half = self.dims.bits, self.dims.reps // 2
        if turn < bits:
            wholes = [
                (
                    self.block(self.terms, index, turn, False),
                    self.block(self.arrived[turn], index, turn, False),
                    self.block(self.terms, index, turn, False),
                )
                for index in range(self.count(turn))
            ]
        elif turn - bits < half:
            move = turn - bits
            result = self.own(0) if move < half - 1 else self.final(0)
            wholes = [(self.own(0), self.line(move, 0), result)]
        else:
            wholes = []
        step = min(self.piece, 256)
        return [
            tuple(ref.at[pl.ds(start, step)] for ref in refs)
            for refs in wholes
            for start in range(0, self.piece, step)
        ]

    def arrive(self, turn):
        bits = self.dims.bits
        if turn < bits:
            self.turn_bytes(turn).wait_recv()
        elif turn < bits + self.moves:
            self.move_bytes(turn - bits).wait_recv()
        else:
            self.finish_swap()

    def taking_part(self, turn):
        bits = self.dims.bits
        if not bits <= turn < bits + self.moves:
            return True
        receivers = self.roles(turn - bits)[1]
        return jnp.logical_or(self.place.rep == receivers[0], self.place.rep == receivers[1])

    def depart(self, turn):
        bits = self.dims.bits
        if turn < bits:
            self.start_turn(turn)
        elif turn < bits + self.moves:
            self.start_move(turn - bits)
        elif self.paired and turn == bits + self.moves:
            self.start_swap()

    def reach(self, stage):
        while self.stage < min(stage, self.stages):
            self.advance()

    def finish_sends(self):
        for turn in range(self.dims.bits):
            self.turn_bytes(turn).wait_send()
        for move in range(self.moves):
            senders, _ = self.roles(move)

            @pl.when(jnp.logical_or(self.place.rep == senders[0], self.place.rep == senders[1]))
            def _(move=move):
                self.move_bytes(move).wait_send()

        if self.paired:
            self.swap_bytes().wait_send()


def when(condition):
    if isinstance(condition, bool):
        return (lambda body: body()) if condition else (lambda body: None)
    return pl.when(condition)


def in_plane_columns(dims, layer, kind, columns, last):
    if dims.reps % 2 or last:
        return columns
    blocks = columns // 128
    share = IN_PLANE[kind] if layer else IN_PLANE_FIRST[kind]
    return max(blocks * share // 16, blocks - blocks // 2) * 128


def few(count, body):
    if count <= 8:
        for index in range(count):
            body(index)
    else:
        tiles(count, body)


def gelu_and_slope(pre):
    cdf = 0.5 * (1.0 + lax.erf(pre * (1.0 / math.sqrt(2.0))))
    slope = cdf + pre * jnp.exp(-0.5 * pre * pre) * (1.0 / math.sqrt(2.0 * math.pi))
    return pre * cdf, slope


def dot_last(left, right):
    return lax.dot_general(left, right, (((1,), (1,)), ((), ())), preferred_element_type=wide)


def dot_first(left, right):
    return lax.dot_general(left, right, (((0,), (0,)), ((), ())), preferred_element_type=wide)


def tiles(count, body):
    def step(j, carry):
        body(j)
        return carry

    lax.fori_loop(0, count, step, 0)


def layers_kernel(dims, *refs):
    refs = iter(refs)

    def take(count):
        return [next(refs) for _ in range(count)]

    x_ref, cotangent, seg_row = take(3)
    vector_refs = take(9) if dims.direct else None
    vector_ref = None if dims.direct else take(1)[0]
    src_qkv, src_out, src_up, src_down = take(4)
    output, tops, vectors, input_grad = take(4)
    vector_out, peak_out = take(2) if dims.direct else (None, None)
    terms = take(4)
    arrived = [take(4) for _ in range(dims.bits)]
    lines, done = take(4), take(4)
    swapped = take(2)
    w_qkv, w_out, w_up, w_down = take(4)
    both_hidden, qkv, attended, probs, norm1, both_first, act, slope, norm2, rstd = take(10)
    hidden, first, total, away, back, bias, both_grad, ring, add_mine, add_other = take(10)
    seg_here, seg_rows = take(2)
    if dims.direct:
        vector_all, small, vector_away, vector_back, line_back, vector_here = take(6)
    else:
        small = vector_ref
    gather_local, gather_send, gather_recv, mate_send, mate_recv = take(5)
    reduce_send, reduce_recv, own_sem, load_sem, store_sem, ring_sem, io_sem = take(7)
    if dims.direct:
        vector_send, vector_recv, pool_load, pool_store = take(4)
    place = Place(dims)
    tokens, width = dims.tokens, dims.width
    heads_row = 128 // dims.head_dim
    scale = 1.0 / math.sqrt(dims.head_dim)

    barrier = pltpu.get_barrier_semaphore()
    reps, shards = dims.reps, dims.shards

    def in_group(step):
        return place.rep, (place.me + step) % shards

    def greet(step):
        pl.semaphore_signal(barrier, 1, device_id=in_group(step), device_id_type=MESH)

    few(shards - 1, lambda index: greet(index + 1))
    for step in range(1, reps):
        line = (place.rep + step) % reps, place.me
        pl.semaphore_signal(barrier, 1, device_id=line, device_id_type=MESH)
    pl.semaphore_wait(barrier, shards + reps - 2)

    sources = (src_qkv, src_out, src_up, src_down)
    wholes = (w_qkv, w_out, w_up, w_down)
    gathers = [
        Gather(
            place,
            layer,
            kind,
            cut,
            sources[kind],
            wholes[kind],
            (gather_local, gather_send, gather_recv),
            layer == dims.layers - 1 and kind == 3 and cut == dims.cuts[kind] - 1,
        )
        for layer in range(dims.layers)
        for kind in range(4)
        for cut in range(dims.cuts[kind])
    ]

    exchanges = []

    def to_mate(src, dst):
        at = len(exchanges)
        copy = remote(src, dst, mate_send.at[at], mate_recv.at[at], place.mate())
        copy.start()
        exchanges.append(copy)
        return copy

    seg_here[...] = jnp.broadcast_to(seg_row[...].astype(wide), seg_here.shape)
    rows_copy = to_mate(seg_here, seg_rows)

    def vector_bytes(buffer, slot, count):
        ref = buffer.at[pl.ds(0, count)]
        return remote(ref, ref, vector_send.at[slot], vector_recv.at[slot], place.mate())

    if dims.direct:

        def send_vector(index):
            remote(
                vector_here,
                vector_all.at[place.me],
                vector_send.at[0],
                vector_recv.at[0],
                in_group(index + 1),
            ).start()

        at = 0
        for layer in range(dims.layers):
            for ref, length in zip(vector_refs, dims.lengths):
                values = ref[...].astype(wide)
                for block in range(length):
                    lanes = slice(block * dims.rows, (block + 1) * dims.rows)
                    vector_here[at : at + 1, :] = values[layer : layer + 1, lanes]
                    at += 1
        vector_all[place.me] = vector_here[...]
        few(shards - 1, send_vector)
    x_copy = pltpu.make_async_copy(x_ref, both_hidden.at[0, pl.ds(0, tokens)], io_sem.at[0])
    cotangent_copy = pltpu.make_async_copy(cotangent, both_grad.at[pl.ds(0, tokens)], io_sem.at[1])
    x_copy.start()
    cotangent_copy.start()
    x_copy.wait()
    hidden_copy = to_mate(both_hidden.at[0, pl.ds(0, tokens)], both_hidden.at[0, pl.ds(tokens, tokens)])
    for gather in gathers:
        gather.begin()
    turns = []

    def turn_on():
        now = len(turns)
        turns.append(now)
        for number, gather in reversed(list(enumerate(gathers))):
            gather.reach(max(now - number + 1, 1 if number <= now + LEAD else 0))

    def prepare(at):
        last = max(
            number
            for number, gather in enumerate(gathers)
            if gather.layer * 4 + gather.kind == at
        )
        while len(turns) < last + gathers[last].stages:
            turn_on()

    hidden[...] = both_hidden[0, pl.ds(0, tokens)].astype(wide)
    vectors[...] = jnp.zeros(vectors.shape, wide)
    tops[...] = jnp.full(tops.shape, neg_large, wide)
    rows_copy.wait_recv()
    for s, row_ref in enumerate((seg_here, seg_rows)):
        row = row_ref[0:1, :]
        column = jnp.broadcast_to(row, (128, tokens)).T[:, 0:1]
        bias[s] = jnp.where(column == row, 0.0, neg_large)

    if dims.direct:
        vector_bytes(vector_all, 0, shards - 1).wait_recv()
        starts = [sum(dims.lengths[:member]) for member in range(9)]
        small[...] = jnp.zeros(small.shape, wide)
        for layer in range(dims.layers):
            base = layer * sum(dims.lengths)

            def spread(row, member, shard, at, layer=layer, base=base):
                for block in range(dims.lengths[member]):
                    lanes = pl.ds(at + block * dims.rows, dims.rows)
                    source = base + starts[member] + block
                    small[layer, row : row + 1, lanes] = vector_all[shard, source : source + 1, :]

            for shard in range(shards):
                for row, member in ((1, 2), (3, 4), (4, 5), (5, 6), (6, 7), (7, 8)):
                    spread(row, member, shard, shard * dims.rows)
            for pair in range(dims.pairs):
                shard = 2 * pair + place.half
                spread(0, 0, shard, pair * dims.rows)
                spread(0, 1, shard, 2 * dims.third + pair * dims.rows)
                spread(2, 3, shard, pair * dims.rows * dims.lengths[3])

    chunk = 32 if tokens % 32 == 0 else tokens

    def layer_norm(residual, partial, other, bias_row, gain_row, shift_row, normed, rstd_out, results):
        def body(j):
            rows = pl.ds(pl.multiple_of(j * chunk, chunk), chunk)
            value = residual[rows] + partial[rows] + other[rows].astype(wide) + bias_row
            centred = value - jnp.mean(value, axis=-1, keepdims=True)
            scale_row = lax.rsqrt(jnp.mean(centred * centred, axis=-1, keepdims=True) + epsilon)
            normal = centred * scale_row
            normed[rows] = normal
            rstd_out[rows] = jnp.broadcast_to(scale_row, (chunk, 128))
            results(rows, normal * gain_row + shift_row)

        tiles(tokens // chunk, body)

    flying = [None, None]

    def project(left, product, at):
        slot = at % 2
        if flying[slot] is not None:
            flying[slot].wait_send()
            settled.append(flying[slot])

        def far(j):
            cols = pl.ds(pl.multiple_of(j * tile, tile), tile)
            away[slot, :, cols] = product(left[pl.ds(tokens, tokens)], cols).astype(low)

        def near(j):
            cols = pl.ds(pl.multiple_of(j * tile, tile), tile)
            total[:, cols] = product(left[pl.ds(0, tokens)], cols)

        tiles(width // tile, far)
        flying[slot] = to_mate(away.at[slot], back.at[at % (2 * dims.layers)])
        tiles(width // tile, near)
        return flying[slot]

    settled = []
    tile = min(512, width)
    for layer in range(dims.layers):
        prepare(4 * layer)
        hidden_copy.wait_recv()

        def qkv_tile(j, layer=layer):
            cols = pl.ds(pl.multiple_of(j * tile, tile), tile)
            value = jnp.dot(both_hidden[layer], w_qkv[layer, :, cols], preferred_element_type=wide)
            qkv[layer, :, cols] = (value + small[layer, 0:1, cols]).astype(low)

        tiles(dims.kinds[0][2] // tile, qkv_tile)
        lane_blocks = dims.third // 128

        def attend(j, layer=layer):
            s, block = j // lane_blocks, j % lane_blocks
            rows = pl.ds(pl.multiple_of(s * tokens, tokens), tokens)

            def lanes(which):
                start = pl.multiple_of(which * dims.third + block * 128, 128)
                return qkv[layer, rows, pl.ds(start, 128)]

            query, key_rows, value_rows = lanes(0), lanes(1), lanes(2)
            mask = bias[s]
            outs = []
            for e in range(heads_row):
                part = slice(e * dims.head_dim, (e + 1) * dims.head_dim)
                scores = dot_last(query[:, part], key_rows[:, part]) * scale + mask
                top = jnp.max(scores, axis=1, keepdims=True)
                expo = jnp.exp(scores - top)
                prob = (expo * (1.0 / jnp.sum(expo, axis=1, keepdims=True))).astype(low)
                head = block * heads_row + e
                probs[layer, s * (lane_blocks * heads_row) + head] = prob
                outs.append(jnp.dot(prob, value_rows[:, part], preferred_element_type=wide))
                peak = jnp.broadcast_to(jnp.max(top, axis=0, keepdims=True), (1, 128))
                tops[layer, pl.ds(head, 1)] = jnp.maximum(tops[layer, pl.ds(head, 1)], peak)
            attended[layer, rows, pl.ds(pl.multiple_of(block * 128, 128), 128)] = jnp.concatenate(
                outs, axis=1
            ).astype(low)

        turn_on()
        tiles(lane_blocks, attend)
        turn_on()
        tiles(lane_blocks, lambda j, attend=attend: attend(j + lane_blocks))

        prepare(4 * layer + 1)
        project(
            attended.at[layer],
            lambda left, cols, layer=layer: jnp.dot(
                left, w_out[layer, :, cols], preferred_element_type=wide
            ),
            2 * layer,
        ).wait_recv()

        def first_rows(rows, value, layer=layer):
            first[rows] = value
            both_first[layer, rows] = value.astype(low)

        layer_norm(
            hidden,
            total,
            back.at[2 * layer],
            small[layer, 1:2, :width],
            small[layer, 4:5, :width],
            small[layer, 5:6, :width],
            norm1.at[layer],
            rstd.at[layer, 0],
            first_rows,
        )
        first_copy = to_mate(
            both_first.at[layer, pl.ds(0, tokens)], both_first.at[layer, pl.ds(tokens, tokens)]
        )

        prepare(4 * layer + 2)
        first_copy.wait_recv()
        narrow = 256

        def up_tile(j, layer=layer):
            cols = pl.ds(pl.multiple_of(j * narrow, narrow), narrow)
            pre = jnp.dot(both_first[layer], w_up[layer, :, cols], preferred_element_type=wide)
            value, steep = gelu_and_slope(pre + small[layer, 2:3, cols])
            act[layer, :, cols] = value.astype(low)
            slope[layer, :, cols] = steep.astype(low)

        tiles(dims.kinds[2][2] // narrow, up_tile)

        prepare(4 * layer + 3)
        project(
            act.at[layer],
            lambda left, cols, layer=layer: jnp.dot(
                left, w_down[layer, :, cols], preferred_element_type=wide
            ),
            2 * layer + 1,
        ).wait_recv()
        last = layer == dims.layers - 1

        def second_rows(rows, value, layer=layer, last=last):
            if last:
                output[rows] = value.astype(low)
            else:
                hidden[rows] = value
                both_hidden[layer + 1, rows] = value.astype(low)

        layer_norm(
            first,
            total,
            back.at[2 * layer + 1],
            small[layer, 3:4, :width],
            small[layer, 6:7, :width],
            small[layer, 7:8, :width],
            norm2.at[layer],
            rstd.at[layer, 1],
            second_rows,
        )
        if not last:
            hidden_copy = to_mate(
                both_hidden.at[layer + 1, pl.ds(0, tokens)],
                both_hidden.at[layer + 1, pl.ds(tokens, tokens)],
            )
    for gather in gathers:
        gather.finish_sends()
    queue = [
        [
            Reduce(
                place,
                layer,
                kind,
                cut,
                part,
                terms[kind],
                [arrived[turn][kind] for turn in range(dims.bits)],
                lines[kind],
                done[kind],
                swapped[kind // 2],
                (reduce_send, reduce_recv, own_sem),
                (add_mine, add_other, load_sem, store_sem),
            )
            for part in range(2)
        ]
        for kinds in ((3, 2), (0,), (1,))
        for layer in reversed(range(dims.layers))
        for kind in kinds
        for cut in range(dims.cuts[kind])
    ]
    stages = max(item.stages for pair in queue for item in pair)

    pools = [
        (ref, row, column)
        for ref in (w_down, w_up, act, slope, w_qkv)
        for row in range(0, ref.shape[1] - 255, 256)
        for column in range(0, ref.shape[2] - 1023, 1024)
    ]

    def together(items):
        work, used = [], 0
        for item in items:
            turn = item.stage - 1
            pieces = []
            for own, other, result in item.additions(turn):
                rows, cols = own.shape
                pair = []
                for ref in (own, other):
                    pool, row, column = pools[used]
                    slot = pool.at[dims.layers - 1, pl.ds(row, rows), pl.ds(column, cols)]
                    pair.append((slot, pltpu.make_async_copy(ref, slot, pool_load.at[used])))
                    used += 1
                back_copy = pltpu.make_async_copy(pair[0][0], result, pool_store.at[used // 2 - 1])
                pieces.append((pair, back_copy))
            work.append((item, turn, pieces))
        for item, turn, pieces in work:

            @when(item.taking_part(turn))
            def _(item=item, turn=turn, pieces=pieces):
                item.arrive(turn)
                for pair, _ in pieces:
                    for _, copy in pair:
                        copy.start()

        for item, turn, pieces in work:

            @when(item.taking_part(turn))
            def _(pieces=pieces):
                for pair, back_copy in pieces:
                    for _, copy in pair:
                        copy.wait()
                    one, two = pair[0][0], pair[1][0]
                    one[...] = one[...] + two[...]
                    back_copy.start()

        for item, turn, pieces in work:

            @when(item.taking_part(turn))
            def _(pieces=pieces):
                for _, back_copy in pieces:
                    back_copy.wait()

            item.depart(turn + 1)
            item.stage += 1

    def pump_together(step, ahead):
        if step + ahead < len(queue):
            for item in queue[step + ahead]:
                item.reach(1)
        for group in GROUPS:
            together(
                [
                    item
                    for behind in group
                    if 0 <= step - behind < len(queue)
                    for item in queue[step - behind]
                    if item.stage < min(2 + behind, item.stages)
                ]
            )

    def pump(step, ahead=AHEAD):
        if dims.direct:
            pump_together(step, ahead)
            return
        if step + ahead < len(queue):
            for item in queue[step + ahead]:
                item.reach(1)
        for behind in reversed(range(stages - 1)):
            at = step - behind
            if 0 <= at < len(queue):
                for item in queue[at]:
                    item.reach(2 + behind)

    def weight_terms(layer, kind, left, right):
        _, held, columns, _ = dims.kinds[kind]
        step = min(256, held)
        wide_cols = columns if columns <= ring.shape[2] else columns // 2
        across = columns // wide_cols
        count = (held // step) * across
        slots = ring.shape[0]

        def store(j):
            rows = pl.ds(pl.multiple_of((j // across) * step, step), step)
            cols = pl.ds(pl.multiple_of((j % across) * wide_cols, 128), wide_cols)
            return pltpu.make_async_copy(
                ring.at[j % slots, pl.ds(0, step), pl.ds(0, wide_cols)],
                terms[kind].at[layer, rows, cols],
                ring_sem.at[j % slots],
            )

        def body(j):
            @pl.when(j >= slots)
            def _():
                store(j - slots).wait()

            rows = pl.ds(pl.multiple_of((j // across) * step, step), step)
            cols = pl.ds(pl.multiple_of((j % across) * wide_cols, 128), wide_cols)
            ring[j % slots, pl.ds(0, step), pl.ds(0, wide_cols)] = dot_first(
                left[:, rows], right[:, cols]
            ).astype(low)
            store(j).start()

        tiles(count, body)
        for j in range(max(0, count - slots), count):
            store(j).wait()

    def count_up(layer, row, value, cols=None):
        cols = pl.ds(0, value.shape[1]) if cols is None else cols
        vectors[layer, pl.ds(row, 1), cols] += jnp.sum(value, axis=0, keepdims=True)

    def norm_grad(value, normed, scale_row, gain_row):
        grad = value * gain_row
        inner = jnp.mean(grad * normed, axis=-1, keepdims=True)
        return scale_row * (grad - jnp.mean(grad, axis=-1, keepdims=True) - normed * inner)

    def back_rows(j):
        return pl.ds(pl.multiple_of(j * chunk, chunk), chunk)

    grad_copy = None
    cotangent_copy.wait()
    pumped = 0
    for layer in reversed(range(dims.layers)):
        newest = layer == dims.layers - 1
        if grad_copy is not None:
            grad_copy.wait_send()
            settled.append(grad_copy)

        def second_back(j, layer=layer, newest=newest):
            rows = back_rows(j)
            value = both_grad[rows].astype(wide) if newest else hidden[rows]
            normed = norm2[layer, rows]
            count_up(layer, 7, value * normed)
            count_up(layer, 8, value)
            grad = norm_grad(value, normed, rstd[layer, 1, rows, 0:1], small[layer, 6:7, :width])
            first[rows] = grad
            rounded = grad.astype(low)
            both_grad[rows] = rounded
            count_up(layer, 4, rounded.astype(wide))

        tiles(tokens // chunk, second_back)
        grad_copy = to_mate(both_grad.at[pl.ds(0, tokens)], both_grad.at[pl.ds(tokens, tokens)])
        grad_copy.wait_recv()

        weight_terms(layer, 3, act.at[layer], both_grad)
        if newest:
            for item in queue[0] + queue[1]:
                item.reach(1)
        else:
            pump(pumped)
            pumped += 1

        def down_back(j, layer=layer):
            cols = pl.ds(pl.multiple_of(j * narrow, narrow), narrow)
            grad = dot_last(both_grad[...], w_down[layer, cols, :])
            rounded = (grad * slope[layer, :, cols].astype(wide)).astype(low)
            slope[layer, :, cols] = rounded
            count_up(layer, 3, rounded.astype(wide), cols)

        tiles(dims.hidden // 2 // narrow, down_back)
        weight_terms(layer, 2, both_first.at[layer], slope.at[layer])
        if not newest:
            pump(pumped)
            pumped += 1
        exchange_at = 2 * (dims.layers - 1 - layer)
        project(
            slope.at[layer],
            lambda left, cols, layer=layer: dot_last(left, w_up[layer, cols, :]),
            2 * dims.layers + exchange_at,
        ).wait_recv()
        grad_copy.wait_send()
        settled.append(grad_copy)

        def first_back(j, layer=layer, exchange_at=exchange_at):
            rows = back_rows(j)
            value = first[rows] + total[rows] + back[exchange_at, rows].astype(wide)
            normed = norm1[layer, rows]
            count_up(layer, 5, value * normed)
            count_up(layer, 6, value)
            grad = norm_grad(value, normed, rstd[layer, 0, rows, 0:1], small[layer, 4:5, :width])
            first[rows] = grad
            rounded = grad.astype(low)
            both_grad[rows] = rounded
            count_up(layer, 2, rounded.astype(wide))

        tiles(tokens // chunk, first_back)
        grad_copy = to_mate(both_grad.at[pl.ds(0, tokens)], both_grad.at[pl.ds(tokens, tokens)])
        grad_copy.wait_recv()
        weight_terms(layer, 1, attended.at[layer], both_grad)

        out_tile = min(256, dims.third)

        def out_back(j, layer=layer):
            cols = pl.ds(pl.multiple_of(j * out_tile, out_tile), out_tile)
            attended[layer, :, cols] = dot_last(both_grad[...], w_out[layer, cols, :]).astype(low)

        tiles(dims.third // out_tile, out_back)
        pump(pumped)
        pumped += 1

        def attend_back(j, layer=layer):
            s, block = j // lane_blocks, j % lane_blocks
            rows = pl.ds(pl.multiple_of(s * tokens, tokens), tokens)
            lanes = pl.ds(pl.multiple_of(block * 128, 128), 128)

            def at(which):
                return pl.ds(pl.multiple_of(which * dims.third + block * 128, 128), 128)

            query, key_rows, value_rows = (qkv[layer, rows, at(which)] for which in range(3))
            grad_out = attended[layer, rows, lanes]
            grads = [[], [], []]
            for e in range(heads_row):
                part = slice(e * dims.head_dim, (e + 1) * dims.head_dim)
                prob = probs[layer, s * (lane_blocks * heads_row) + block * heads_row + e]
                grads[2].append(dot_first(prob, grad_out[:, part]))
                prob = prob.astype(wide)
                grad_prob = dot_last(grad_out[:, part], value_rows[:, part])
                inner = jnp.sum(prob * grad_prob, axis=1, keepdims=True)
                grad_score = (prob * (grad_prob - inner)).astype(low)
                grads[0].append(
                    jnp.dot(grad_score, key_rows[:, part], preferred_element_type=wide) * scale
                )
                grads[1].append(dot_first(grad_score, query[:, part]) * scale)
            for which, row in ((0, 0), (1, None), (2, 1)):
                rounded = jnp.concatenate(grads[which], axis=1).astype(low)
                qkv[layer, rows, at(which)] = rounded
                if row is not None:
                    count_up(layer, row, rounded.astype(wide), lanes)

        tiles(2 * lane_blocks, attend_back)
        pump(pumped)
        pumped += 1
        weight_terms(layer, 0, both_hidden.at[layer], qkv.at[layer])
        project(
            qkv.at[layer],
            lambda left, cols, layer=layer: dot_last(left, w_qkv[layer, cols, :]),
            2 * dims.layers + exchange_at + 1,
        ).wait_recv()

        def input_rows(j, exchange_at=exchange_at):
            rows = back_rows(j)
            hidden[rows] = first[rows] + total[rows] + back[exchange_at + 1, rows].astype(wide)

        tiles(tokens // chunk, input_rows)
        pump(pumped)
        pumped += 1

    grad_out_copy = pltpu.make_async_copy(hidden, input_grad, io_sem.at[0])
    grad_out_copy.start()

    if dims.direct:
        count = dims.vector_rows
        for shard in range(shards):
            for layer in range(dims.layers):
                at = layer * sum(dims.lengths)
                for member, length in enumerate(dims.lengths):
                    halved = member in (0, 1, 3)
                    for block in range(length):
                        first_lane = (shard // 2 if halved else shard) * length * dims.rows
                        lanes = pl.ds(first_lane + block * dims.rows, dims.rows)
                        value = vectors[layer, member : member + 1, lanes]
                        if halved:
                            value = jnp.where(place.half == shard % 2, value, 0.0)
                        vector_away[shard, at : at + 1, :] = value
                        at += 1
                heads = HEADS // 2
                vector_away[shard, pl.ds(count + layer * heads, heads)] = tops[layer]
        vector_back[place.me] = vector_away[place.me]

        def send_terms(index):
            target = in_group(index + 1)
            remote(
                vector_away.at[target[1]],
                vector_back.at[place.me],
                vector_send.at[1],
                vector_recv.at[1],
                target,
            ).start()

        few(shards - 1, send_terms)
    gathered = pumped + 1
    while pumped < len(queue) + stages:
        pump(pumped)
        pumped += 1
        if dims.direct and pumped == gathered:
            vector_bytes(vector_back, 1, shards - 1).wait_recv()
            total_rows = vector_back[0, pl.ds(0, count)]
            for shard in range(1, shards):
                total_rows = total_rows + vector_back[shard, pl.ds(0, count)]
            vector_out[...] = total_rows
            heads = dims.layers * HEADS // 2
            for half in range(2):
                peak = vector_back[half, pl.ds(count, heads)]
                for shard in range(2 + half, shards, 2):
                    peak = jnp.maximum(peak, vector_back[shard, pl.ds(count, heads)])
                peak_out[half] = peak
            line_back[place.rep, pl.ds(0, count)] = vector_out[...]
            for half in range(2):
                line_back[place.rep, pl.ds(count + half * heads, heads)] = peak_out[half]
            for step in range(1, reps):
                remote(
                    line_back.at[place.rep],
                    line_back.at[place.rep],
                    vector_send.at[2],
                    vector_recv.at[2],
                    ((place.rep + step) % reps, place.me),
                ).start()
    if dims.direct:
        vector_bytes(line_back, 2, reps - 1).wait_recv()
        total_rows = line_back[0, pl.ds(0, count)]
        for other in range(1, reps):
            total_rows = total_rows + line_back[other, pl.ds(0, count)]
        vector_out[...] = total_rows
        for half in range(2):
            peak = line_back[0, pl.ds(count + half * heads, heads)]
            for other in range(1, reps):
                peak = jnp.maximum(peak, line_back[other, pl.ds(count + half * heads, heads)])
            peak_out[half] = peak

    for copy in exchanges:
        if not any(copy is other for other in settled):
            copy.wait_send()
    if dims.direct:
        vector_bytes(vector_all, 0, shards - 1).wait_send()
        vector_bytes(vector_back, 1, shards - 1).wait_send()
        vector_bytes(line_back, 2, reps - 1).wait_send()
    for pair in queue:
        for item in pair:
            item.finish_sends()
    grad_out_copy.wait()


def run_layers(dims, x, cotangent, segments, vectors, weights):
    layers, tokens, width = dims.layers, dims.tokens, dims.width
    both = 2 * tokens

    def shape(dims_of, dtype):
        return jax.ShapeDtypeStruct(dims_of, dtype)

    held = [shape((layers, rows, columns), low) for _, rows, columns, _ in dims.kinds]
    pair_rows = [rows * (2 if paired else 1) for rows, _, _, paired in dims.kinds]
    columns = [kind[2] for kind in dims.kinds]
    heads = HEADS // 2
    summed = []
    if dims.direct:
        summed = [
            shape((dims.vector_rows, dims.rows), wide),
            shape((2, layers * heads, 128), wide),
        ]
    outs = (
        [
            shape((tokens, width), low),
            shape((layers, HEADS // 2, 128), wide),
            shape((layers, 16, dims.hidden // 2), wide),
            shape((tokens, width), wide),
        ]
        + summed
        + held * (1 + dims.bits)
        + [shape((layers, dims.reps // 2, r, c), low) for r, c in zip(pair_rows, columns)]
        + [shape((layers, r, c), low) for r, c in zip(pair_rows, columns)]
        + [
            shape((layers, dims.rows, columns[kind] * (2 if dims.direct else 1)), low)
            for kind in (0, 2)
        ]
    )
    vmem = pl.BlockSpec(memory_space=pltpu.VMEM)
    anywhere = pl.BlockSpec(memory_space=pl.ANY)
    dma = pltpu.SemaphoreType.DMA
    scratch = [pltpu.VMEM(item.shape, item.dtype) for item in held] + [
        pltpu.VMEM(*item)
        for item in (
            ((layers, both, width), low),
            ((layers, both, 3 * dims.third), low),
            ((layers, both, dims.third), low),
            ((layers, HEADS, tokens, tokens), low),
            ((layers, tokens, width), wide),
            ((layers, both, width), low),
            ((layers, both, dims.hidden // 2), low),
            ((layers, both, dims.hidden // 2), low),
            ((layers, tokens, width), wide),
            ((layers, 2, tokens, 128), wide),
            ((tokens, width), wide),
            ((tokens, width), wide),
            ((tokens, width), wide),
            ((2, tokens, width), low),
            ((2 * layers, tokens, width), low),
            ((2, tokens, tokens), wide),
            ((both, width), low),
            ((3, 256, 1024), low),
            ((2, 256, 1024), low),
            ((2, 256, 1024), low),
            ((8, tokens), wide),
            ((8, tokens), wide),
        )
    ]
    if dims.direct:
        rows = dims.vector_rows
        scratch += [
            pltpu.VMEM(item, wide)
            for item in (
                (dims.shards, rows, dims.rows),
                (layers, 8, dims.hidden // 2),
                (dims.shards, rows + layers * heads, dims.rows),
                (dims.shards, rows + layers * heads, dims.rows),
                (dims.reps, rows + 2 * layers * heads, dims.rows),
                (rows, dims.rows),
            )
        ]
    slots = 2 + 2 * dims.bits
    exchange_count = 2 + 8 * layers
    reduce_slots = dims.bits + dims.reps
    scratch = scratch + [
        dma((4 * layers * CUTS,)),
        dma((4 * layers * CUTS, slots)),
        dma((4 * layers * CUTS, slots)),
        dma((exchange_count,)),
        dma((exchange_count,)),
        dma((8 * layers * CUTS, reduce_slots)),
        dma((8 * layers * CUTS, reduce_slots)),
        dma((8 * layers * CUTS,)),
        dma((2, 2)),
        dma((2,)),
        dma((3,)),
        dma((2,)),
    ]
    if dims.direct:
        scratch += [dma((3,)), dma((3,)), dma((32,)), dma((16,))]
    return pl.pallas_call(
        functools.partial(layers_kernel, dims),
        out_shape=outs,
        in_specs=[anywhere] * 2 + [vmem] * (1 + len(vectors)) + [anywhere] * 4,
        out_specs=[vmem] * 3 + [anywhere] + [vmem] * len(summed) + [anywhere] * (len(outs) - 4 - len(summed)),
        scratch_shapes=scratch,
        compiler_params=pltpu.CompilerParams(
            collective_id=0, has_side_effects=True, vmem_limit_bytes=63 * 2**20 + 2**19
        ),
        name="layers",
    )(x, cotangent, segments, *vectors, *weights)


def own_rows(net, value):
    layers, rows, columns = value.shape
    split = value.reshape(layers, 2, rows // 2, columns)
    return lax.dynamic_index_in_dim(split, net.core, 1, keepdims=False)


def gathered_vectors(net, dims, packed):
    lengths = dims.lengths
    packed = net.in_order(packed, net.over_core(packed), net.core)
    packed = net.rows_in_order(net.gather_chips(packed, list(range(net.bits))))

    def whole(layer, member):
        start = sum(lengths[:member])
        return packed[:, layer, start : start + lengths[member]].astype(wide)

    def of_core(layer, member):
        split = whole(layer, member).reshape(net.high, 2, -1)
        return lax.dynamic_index_in_dim(split, net.core, 1, keepdims=False).reshape(-1)

    def wide_row(row):
        return jnp.pad(row, (0, dims.hidden // 2 - row.shape[0]))

    def rows(layer):
        bias_q = of_core(layer, 0)
        bias_qkv = jnp.concatenate([bias_q, jnp.zeros_like(bias_q), of_core(layer, 1)])
        singles = [whole(layer, member).reshape(-1) for member in (2, 4, 5, 6, 7, 8)]
        return [bias_qkv, singles[0], of_core(layer, 3)] + singles[1:]

    return jnp.stack(
        [jnp.stack([wide_row(row) for row in rows(layer)]) for layer in range(dims.layers)]
    )


def summed_vectors(net, dims, vectors, tops):
    layers, lengths, rows = dims.layers, dims.lengths, dims.rows
    half_width, half_hidden = dims.third, dims.hidden // 2
    here = (half_width, half_width, dims.width, half_hidden) + (dims.width,) * 5

    def placed(value, member):
        if member in (0, 1, 3):
            value = value.reshape(net.high, 1, net.step, lengths[member], rows)
            zero = jnp.zeros_like(value)
            first = net.core == 0
            return jnp.concatenate(
                [jnp.where(first, value, zero), jnp.where(first, zero, value)], axis=1
            )
        return value.reshape(net.high, 2, net.step, lengths[member], rows)

    terms = jnp.stack(
        [
            jnp.concatenate(
                [placed(vectors[layer, row, :size], row) for row, size in enumerate(here)], axis=3
            )
            for layer in range(layers)
        ],
        axis=3,
    )
    theirs = lax.dynamic_index_in_dim(terms, 1 - net.core, 1, keepdims=False)
    ours = lax.dynamic_index_in_dim(terms, net.core, 1, keepdims=False)
    terms = ours + net.over_core(theirs)
    terms = terms.reshape((net.pairs,) + terms.shape[2:])
    terms = net.sum_reps(net.scatter_chips(terms, list(range(net.bits))))

    local = tops[:, :, 0]
    local = net.in_order(local, net.over_core(local), net.core)
    local = local.reshape(2, layers, net.high, -1).transpose(1, 2, 0, 3).reshape(layers, HEADS)
    for bit in range(net.bits):
        local = jnp.maximum(local, net.over_bit(local, bit))
    step = 1
    while step < net.reps:
        swap = [(i, i ^ step) for i in range(net.reps)]
        local = jnp.maximum(local, lax.ppermute(local, "rep", swap))
        step *= 2
    return terms, local


def shards(
    inputs,
    cotangent,
    segments,
    w_qkv,
    w_out,
    w_up,
    w_down,
    bias_query,
    bias_value,
    bias_out,
    bias_up,
    bias_down,
    norm1_gain,
    norm1_bias,
    norm2_gain,
    norm2_bias,
    tau,
    *,
    shard_count,
    rep_count,
):
    layer_count = w_qkv.shape[0]
    width = w_qkv.shape[2] // 3
    rows_here = bias_query.shape[1]
    head_dim = width // HEADS
    net = Net(shard_count, rep_count, max(1, head_dim // rows_here))

    vectors = (
        bias_query,
        bias_value,
        bias_out,
        bias_up,
        bias_down,
        norm1_gain,
        norm1_bias,
        norm2_gain,
        norm2_bias,
    )
    lengths = [vector.shape[1] // rows_here for vector in vectors]
    tokens = inputs.shape[0]
    dims = Dims(shard_count, rep_count, net.step, layer_count, tokens, width, w_up.shape[2])
    if dims.direct:
        vector_in = vectors
        matrices = (w_qkv, w_out, w_up, w_down)
    else:
        packed = jnp.concatenate(
            [vector.reshape(layer_count, -1, rows_here) for vector in vectors], axis=1
        )
        vector_in = (gathered_vectors(net, dims, packed),)
        matrices = (by_half(w_qkv, net, 3), w_out, by_half(w_up, net, 1), w_down)
    results = run_layers(dims, inputs, cotangent, segments, vector_in, matrices)
    output, tops, vector_terms, input_grad = results[:4]
    done, swapped = results[-6:-2], results[-2:]

    if dims.direct:
        vector_grads, peak = results[4:6]
        vector_grads = vector_grads.reshape(layer_count, -1, rows_here)
        peak = peak[:, :, 0].reshape(2, layer_count, net.high, -1)
        peak = peak.transpose(1, 2, 0, 3).reshape(layer_count, HEADS)
        full = swapped[0], done[1], swapped[1], done[3]
    else:
        vector_grads, peak = summed_vectors(net, dims, vector_terms, tops)
        paired = [whole_columns(own_rows(net, done[k]), swapped[k // 2], net, 3 - k) for k in (0, 2)]
        full = paired[0], done[1], paired[1], done[3]
    large = tuple(value.astype(wide) for value in full)
    ends = [sum(lengths[: member + 1]) for member in range(len(lengths))]
    vector_grads = [
        vector_grads[:, end - length : end].reshape(layer_count, -1)
        for end, length in zip(ends, lengths)
    ]
    factor = jnp.sqrt(tau / jnp.maximum(peak, tau))
    column_scale = jnp.repeat(factor, head_dim, axis=1)
    both_scale = jnp.concatenate([column_scale, column_scale], axis=1)
    clipped_qk = w_qkv[:, :, : 2 * width].astype(wide) * both_scale[:, None, :]
    start = lax.axis_index("shard") * rows_here
    scale_here = lax.dynamic_slice_in_dim(column_scale, start, rows_here, 1)
    clipped_bias_query = bias_query.astype(wide) * scale_here
    return (output, input_grad) + large + tuple(vector_grads) + (clipped_qk, clipped_bias_query)


def solution(mesh):
    tokens = P(("rep", "shard"), None)
    matrix = P(None, "shard", None)
    vector = P(None, "shard")
    in_specs = (tokens, tokens, tokens) + (matrix,) * 4 + (vector,) * 9 + (P(),)
    out_specs = (tokens, tokens) + (matrix,) * 4 + (vector,) * 9 + (matrix, vector)

    def local(*arrays):
        return shards(*arrays, shard_count=mesh.shape["shard"], rep_count=mesh.shape["rep"])

    return jax.shard_map(local, mesh=mesh, in_specs=in_specs, out_specs=out_specs, check_vma=False)
```

```python
import functools
import math

import jax
import jax.numpy as jnp
from jax import lax
from jax.experimental import pallas as pl
from jax.experimental.pallas import tpu as pltpu
from jax.sharding import PartitionSpec as P

HEADS = 16
MESH = pl.DeviceIdType.MESH
LEAD = 1
CUTS = 2
AHEAD = 1
GROUPS = ((0,), (1, 2, 3, 4, 5))
IN_PLANE_FIRST = (11, 10, 10, 12)
IN_PLANE = (11, 10, 10, 12)


epsilon = 1e-05
neg_large = -1e30
low = jnp.bfloat16
wide = jnp.float32


class Net:
    def __init__(self, shards, reps, step):
        self.shards = shards
        self.reps = reps
        self.step = step
        self.pairs = shards // 2
        self.high = shards // (2 * step)
        self.bits = self.pairs.bit_length() - 1
        self.me = lax.axis_index("shard")
        self.core = (self.me // step) % 2
        self.rep = lax.axis_index("rep")

    def over_core(self, value):
        return lax.ppermute(value, "shard", [(i, i ^ self.step) for i in range(self.shards)])

    def stride(self, bit):
        return (1 << bit) if (1 << bit) < self.step else (2 << bit)

    def over_bit(self, value, bit):
        step = self.stride(bit)
        return lax.ppermute(value, "shard", [(i, i ^ step) for i in range(self.shards)])

    def chip_bit(self, bit):
        return (self.me // self.stride(bit)) % 2

    def rows_in_order(self, value):
        rest = value.shape[2:]
        value = value.reshape((self.high, self.step, 2) + rest)
        return jnp.swapaxes(value, 1, 2).reshape((self.shards,) + rest)

    def rows_by_pair(self, value):
        rest = value.shape[1:]
        value = value.reshape((self.high, 2, self.step) + rest)
        return jnp.swapaxes(value, 1, 2).reshape((self.pairs, 2) + rest)

    def in_order(self, mine, other, place):
        first = place == 0
        return jnp.stack([jnp.where(first, mine, other), jnp.where(first, other, mine)])

    def gather_chips(self, piece, order):
        shape = piece.shape
        for bit in order:
            piece = self.in_order(piece, self.over_bit(piece, bit), self.chip_bit(bit))
        axes = list(reversed(order))
        natural = [axes.index(bit) for bit in reversed(range(self.bits))]
        rest = list(range(self.bits, self.bits + len(shape)))
        return piece.transpose(natural + rest).reshape((self.pairs,) + shape)

    def scatter_chips(self, value, order):
        rest = value.shape[1:]
        value = value.reshape((2,) * self.bits + rest)
        left = list(reversed(range(self.bits)))
        for bit in order:
            axis = left.index(bit)
            place = self.chip_bit(bit)
            theirs = lax.dynamic_index_in_dim(value, 1 - place, axis, keepdims=False)
            ours = lax.dynamic_index_in_dim(value, place, axis, keepdims=False)
            got = self.over_bit(theirs, bit)
            value = (ours.astype(wide) + got.astype(wide)).astype(value.dtype)
            left.remove(bit)
        return value

    def sum_reps(self, value):
        reps, half = self.reps, self.reps // 2

        def add(one, other):
            return (one.astype(wide) + other.astype(wide)).astype(value.dtype)

        total = value
        for i in range(half - 1):
            got = lax.ppermute(total, "rep", [(i, i + 1), (reps - 1 - i, reps - 2 - i)])
            total = add(total, got)
        total = add(total, lax.ppermute(total, "rep", [(half - 1, half), (half, half - 1)]))
        for i in reversed(range(half - 1)):
            got = lax.ppermute(total, "rep", [(i + 1, i), (reps - 2 - i, reps - 1 - i)])
            outer = jnp.logical_or(self.rep == i, self.rep == reps - 1 - i)
            total = jnp.where(outer, got, total)
        return total


def by_half(weight, net, groups):
    layers, rows, columns = weight.shape
    split = weight.reshape(layers, rows, groups * net.high, 2, columns // (2 * groups * net.high))
    return split.transpose(0, 3, 1, 2, 4).reshape(layers, 2, rows, columns // 2)


def whole_columns(mine, other, net, groups):
    layers, rows, columns = mine.shape
    block = columns // (groups * net.high)
    both = [part.reshape(layers, rows, groups * net.high, block) for part in (mine, other)]
    first = net.core == 0
    stacked = jnp.stack(
        [jnp.where(first, both[0], both[1]), jnp.where(first, both[1], both[0])], axis=3
    )
    return stacked.reshape(layers, rows, 2 * columns).astype(wide)


class Place:
    def __init__(self, dims):
        self.dims = dims
        step = dims.step
        self.rep = lax.axis_index("rep")
        self.me = lax.axis_index("shard")
        self.half = (self.me // step) % 2
        self.pair = (self.me // (2 * step)) * step + self.me % step
        self.plane = self.rep % 2

    def flip(self, value, bit):
        size = 1 << bit
        return value + size * (1 - 2 * ((value // size) % 2))

    def mate(self):
        return (self.rep, self.me + self.dims.step * (1 - 2 * self.half))

    def over_bit(self, bit):
        stride = (1 << bit) if (1 << bit) < self.dims.step else (2 << bit)
        return (self.rep, self.me + stride * (1 - 2 * ((self.me // stride) % 2)))

    def over_plane(self):
        return (self.rep + 1 - 2 * self.plane, self.me)

    def first_shard(self, pair):
        step = self.dims.step
        return (pair // step) * (2 * step) + pair % step


class Dims:
    def __init__(self, shards, reps, step, layers, tokens, width, hidden):
        self.shards, self.reps, self.step = shards, reps, step
        self.pairs = shards // 2
        self.bits = self.pairs.bit_length() - 1
        self.layers, self.tokens, self.width, self.hidden = layers, tokens, width, hidden
        self.head_dim = width // HEADS
        self.third = width // 2
        self.rows = width // shards
        self.kinds = (
            (self.rows, width, 3 * width // 2, True),
            (self.rows, width // 2, width, False),
            (self.rows, width, hidden // 2, True),
            (hidden // shards, hidden // 2, width, False),
        )
        high = shards // (2 * step)
        self.block = (width // (2 * high), None, hidden // (2 * high), None)
        self.blocks = (3 * high, None, high, None)
        self.lengths = (1, 1, 1, hidden // width, 1, 1, 1, 1, 1)
        self.vector_rows = layers * sum(self.lengths)
        self.direct = self.rows % 128 == 0 and step == 1
        self.cuts = tuple(CUTS if self.direct and kind != 1 else 1 for kind in range(4))


def remote(src, dst, send, recv, where):
    return pltpu.make_async_remote_copy(
        src_ref=src, dst_ref=dst, send_sem=send, recv_sem=recv, device_id=where, device_id_type=MESH
    )


class Gather:
    def __init__(self, place, layer, kind, cut, source, whole, sems, last):
        self.place, self.dims = place, place.dims
        self.layer, self.kind = layer, kind
        self.source, self.whole = source, whole
        self.rows, self.held, columns, self.paired = self.dims.kinds[kind]
        self.local, self.send, self.recv = sems
        self.cut, self.cuts = cut, self.dims.cuts[kind]
        self.columns = columns // self.cuts
        self.base = cut * self.columns
        self.at = (layer * 4 + kind) * CUTS + cut
        self.in_plane = in_plane = in_plane_columns(self.dims, layer, kind, self.columns, last)
        self.stage = 0
        self.stages = self.dims.bits + (2 if in_plane < self.columns else 1)

    def blocks(self, pair):
        if not self.paired:
            return [pair * self.rows], self.rows
        first = self.place.first_shard(pair) * self.rows
        if self.dims.step == 1:
            return [first], 2 * self.rows
        return [first, first + self.dims.step * self.rows], self.rows

    def window(self, part):
        size = self.in_plane // 2
        if (size % 128) and part < 2:
            low_size = size // 128 * 128
            size = low_size if part == 0 else self.in_plane - low_size
            offset = 0 if part == 0 else low_size
        else:
            offset = part * size
        start = self.base + self.place.plane * (self.columns - self.in_plane) + offset
        return pl.ds(pl.multiple_of(start, 128), size), size

    def order(self, part):
        bits = list(range(self.dims.bits))
        return bits if part == 0 else bits[::-1]

    def subset(self, done):
        pairs = [self.place.pair]
        for bit in done:
            pairs = pairs + [self.place.flip(pair, bit) for pair in pairs]
        return pairs

    def begin(self):
        place = self.place
        if self.paired:
            mine = place.me * self.rows
            rows = pl.ds(pl.multiple_of(mine, 16), self.rows)
            for theirs, ours in self.begin_blocks():
                pltpu.make_async_copy(
                    ours, self.whole.at[self.layer, rows, theirs[1]], self.local.at[self.at]
                ).start()
            for theirs, ours in self.begin_blocks():
                remote(
                    theirs[0],
                    self.whole.at[self.layer, rows, theirs[1]],
                    self.send.at[self.at, 0],
                    self.recv.at[self.at, 0],
                    place.mate(),
                ).start()
        else:
            rows = pl.ds(pl.multiple_of(place.pair * self.rows, 16), self.rows)
            columns = pl.ds(self.base, self.columns)
            pltpu.make_async_copy(
                self.source.at[self.layer, :, columns],
                self.whole.at[self.layer, rows, columns],
                self.local.at[self.at],
            ).start()

    def begin_blocks(self):
        place, width = self.place, self.dims.block[self.kind]
        if not self.dims.direct:
            every = pl.ds(0, self.columns)
            yield (
                (self.source.at[self.layer, 1 - place.half], every),
                self.source.at[self.layer, place.half],
            )
            return
        count = self.dims.blocks[self.kind] // self.cuts
        for block in range(self.cut * count, (self.cut + 1) * count):
            to = pl.ds(block * width, width)
            starts = [(2 * block + half) * width for half in (1 - place.half, place.half)]
            theirs, ours = (
                self.source.at[self.layer, :, pl.ds(pl.multiple_of(start, 128), width)] for start in starts
            )
            yield (theirs, to), ours

    def some(self, rows, columns):
        return self.whole.at[self.layer, pl.ds(0, rows), columns]

    def phase(self, turn):
        place = self.place
        for part in range(2):
            order = self.order(part)
            columns, _ = self.window(part)
            for pair in self.subset(order[:turn]):
                starts, count = self.blocks(pair)
                for start in starts:
                    block = self.whole.at[self.layer, pl.ds(pl.multiple_of(start, 16), count), columns]
                    remote(
                        block,
                        block,
                        self.send.at[self.at, 1 + 2 * turn + part],
                        self.recv.at[self.at, 1 + 2 * turn + part],
                        place.over_bit(order[turn]),
                    ).start()

    def phase_bytes(self, turn, part):
        columns = pl.ds(0, self.window(part)[1])
        per_pair = self.rows * (2 if self.paired else 1)
        block = self.some(per_pair << turn, columns)
        at = 1 + 2 * turn + part
        return remote(block, block, self.send.at[self.at, at], self.recv.at[self.at, at], self.place.mate())

    def across(self):
        place = self.place
        size = self.columns - self.in_plane
        columns = pl.ds(pl.multiple_of(self.base + place.plane * self.in_plane, 128), size)
        at = 1 + 2 * self.dims.bits
        for pair in self.subset(range(self.dims.bits))[1:]:
            starts, count = self.blocks(pair)
            for start in starts:
                block = self.whole.at[self.layer, pl.ds(pl.multiple_of(start, 16), count), columns]
                remote(block, block, self.send.at[self.at, at], self.recv.at[self.at, at], place.over_plane()).start()

    def across_bytes(self):
        per_pair = self.rows * (2 if self.paired else 1)
        block = self.some(per_pair * (self.dims.pairs - 1), pl.ds(0, self.columns - self.in_plane))
        at = 1 + 2 * self.dims.bits
        return remote(block, block, self.send.at[self.at, at], self.recv.at[self.at, at], self.place.over_plane())

    def own_bytes(self):
        if not self.paired:
            return None
        block = self.some(self.rows, pl.ds(0, self.columns))
        return remote(block, block, self.send.at[self.at, 0], self.recv.at[self.at, 0], self.place.mate())

    def advance(self):
        if self.stage == 0:
            own = self.some(self.rows, pl.ds(0, self.columns))
            pltpu.make_async_copy(own, own, self.local.at[self.at]).wait()
            if self.paired:
                self.own_bytes().wait_recv()
        elif self.stage <= self.dims.bits:
            for part in range(2):
                self.phase_bytes(self.stage - 1, part).wait_recv()
        else:
            self.across_bytes().wait_recv()
        if self.stage < self.dims.bits:
            self.phase(self.stage)
        elif self.stage + 1 < self.stages:
            self.across()
        self.stage += 1

    def reach(self, stage):
        while self.stage < min(stage, self.stages):
            self.advance()

    def finish_sends(self):
        if self.paired:
            self.own_bytes().wait_send()
        for turn in range(self.dims.bits):
            for part in range(2):
                self.phase_bytes(turn, part).wait_send()
        if self.in_plane < self.columns:
            self.across_bytes().wait_send()


class Reduce:
    def __init__(self, place, layer, kind, cut, part, terms, arrived, lines, done, swapped, sems, bufs):
        self.place, self.dims = place, place.dims
        self.layer, self.kind, self.part = layer, kind, part
        self.terms, self.arrived, self.lines, self.done, self.swapped = terms, arrived, lines, done, swapped
        self.send, self.recv, self.own_sem = sems
        self.mine, self.other, self.load_sem, self.store_sem = bufs
        self.rows, self.held, self.columns, self.paired = self.dims.kinds[kind]
        cuts = self.dims.cuts[kind]
        self.slice_at, self.slices = cut * 2 + part, 2 * cuts
        self.size = self.columns // self.slices
        self.columns_here = pl.ds(self.slice_at * self.size, self.size)
        self.at = ((layer * 4 + kind) * CUTS + cut) * 2 + part
        bits = list(range(self.dims.bits))
        self.order = bits if part == 0 else bits[::-1]
        self.moves = self.dims.reps - 1
        self.stage = 0
        self.stages = 1 + self.dims.bits + self.moves + (1 if self.paired else 0)
        self.split = self.paired and self.dims.step > 1
        self.piece = self.rows * (2 if self.paired and not self.split else 1)
        self.pieces = 2 if self.split else 1

    def row_of(self, pair, which):
        if not self.paired:
            return pair * self.rows
        return (self.place.first_shard(pair) + which * self.dims.step) * self.rows

    def sems(self, slot):
        return self.send.at[self.at, slot], self.recv.at[self.at, slot]

    def kept(self, index, turn, away):
        pair = self.place.pair
        for i, bit in enumerate(self.order[turn + 1 :]):
            size = 1 << bit
            wanted = (index // (1 << i)) % 2
            pair = pair + size * (wanted - (self.place.pair // size) % 2)
        if away:
            pair = self.place.flip(pair, self.order[turn])
        return pair

    def count(self, turn):
        return (self.dims.pairs >> (turn + 1)) * self.pieces

    def loop(self, count, body):
        if count <= 4:
            for i in range(count):
                body(i)
        else:
            tiles(count, body)

    def block(self, ref, index, turn, away):
        pair = self.kept(index // self.pieces, turn, away)
        start = self.row_of(pair, index % self.pieces)
        return ref.at[self.layer, pl.ds(pl.multiple_of(start, 16), self.piece), self.columns_here]

    def start_turn(self, turn):
        def one(index):
            remote(
                self.block(self.terms, index, turn, True),
                self.block(self.arrived[turn], index, turn, True),
                *self.sems(turn),
                self.place.over_bit(self.order[turn]),
            ).start()

        self.loop(self.count(turn), one)

    def turn_bytes(self, turn):
        ref = self.terms.at[self.layer, pl.ds(0, self.count(turn) * self.piece), self.columns_here]
        return remote(ref, ref, *self.sems(turn), self.place.over_bit(self.order[turn]))

    def add(self, count, own, other, result):
        step = min(self.piece, self.mine.shape[1])
        per = self.piece // step
        total = count * per

        def part_of(make, index):
            ref = make(index // per)
            return ref.at[pl.ds(pl.multiple_of((index % per) * step, 16), step)]

        def slots(index):
            slot = index % 2
            rows, cols = pl.ds(0, step), pl.ds(0, self.size)
            return self.mine.at[slot, rows, cols], self.other.at[slot, rows, cols], slot

        def load(index):
            one, two, slot = slots(index)
            return (
                pltpu.make_async_copy(part_of(own, index), one, self.load_sem.at[slot, 0]),
                pltpu.make_async_copy(part_of(other, index), two, self.load_sem.at[slot, 1]),
            )

        def store(index):
            one, _, slot = slots(index)
            return pltpu.make_async_copy(one, part_of(result, index), self.store_sem.at[slot])

        def body(index, first, last):
            @when(jnp.logical_not(last) if not isinstance(last, bool) else not last)
            def _():
                @when(jnp.logical_not(first) if not isinstance(first, bool) else not first)
                def _():
                    store(index - 1).wait()

                for copy in load(index + 1):
                    copy.start()

            for copy in load(index):
                copy.wait()
            one, two, _ = slots(index)
            one[...] = (one[...].astype(wide) + two[...].astype(wide)).astype(low)
            store(index).start()

        for copy in load(0):
            copy.start()
        if total <= 4:
            for index in range(total):
                body(index, index == 0, index == total - 1)
        else:
            tiles(total, lambda index: body(index, index == 0, index == total - 1))
        if total > 1:
            store(total - 2).wait()
        store(total - 1).wait()

    def finish_turn(self, turn):
        self.turn_bytes(turn).wait_recv()
        self.add(
            self.count(turn),
            lambda index: self.block(self.terms, index, turn, False),
            lambda index: self.block(self.arrived[turn], index, turn, False),
            lambda index: self.block(self.terms, index, turn, False),
        )

    def own(self, which):
        start = self.row_of(self.place.pair, which)
        return self.terms.at[self.layer, pl.ds(pl.multiple_of(start, 16), self.piece), self.columns_here]

    def line(self, move, which):
        return self.lines.at[self.layer, move, pl.ds(which * self.piece, self.piece), self.columns_here]

    def final(self, which):
        return self.done.at[self.layer, pl.ds(which * self.piece, self.piece), self.columns_here]

    def roles(self, move):
        reps, half = self.dims.reps, self.dims.reps // 2
        if move < half - 1:
            return (move, reps - 1 - move), (move + 1, reps - 2 - move)
        if move == half - 1:
            return (half - 1, half), (half, half - 1)
        back = reps - 2 - move
        return (back + 1, reps - 2 - back), (back, reps - 1 - back)

    def move_copies(self, move, target):
        half = self.dims.reps // 2
        slot = self.dims.bits + move
        for which in range(self.pieces):
            src = self.own(which) if move < half else self.final(which)
            dst = self.line(move, which) if move < half else self.final(which)
            yield remote(src, dst, *self.sems(slot), (target, self.place.me))

    def move_bytes(self, move):
        slot = self.dims.bits + move
        ref = self.done.at[self.layer, pl.ds(0, self.pieces * self.piece), self.columns_here]
        return remote(ref, ref, *self.sems(slot), self.place.mate())

    def start_move(self, move):
        senders, receivers = self.roles(move)
        for sender, receiver in zip(senders, receivers):

            @pl.when(self.place.rep == sender)
            def _(receiver=receiver):
                for copy in self.move_copies(move, receiver):
                    copy.start()

    def finish_move(self, move):
        half = self.dims.reps // 2
        _, receivers = self.roles(move)

        @pl.when(jnp.logical_or(self.place.rep == receivers[0], self.place.rep == receivers[1]))
        def _():
            self.move_bytes(move).wait_recv()
            if move < half:
                self.add(
                    self.pieces,
                    self.own,
                    lambda which: self.line(move, which),
                    self.own if move < half - 1 else self.final,
                )

    def part_blocks(self):
        width = self.dims.block[self.kind]
        count = self.dims.blocks[self.kind] // self.slices
        for block in range(self.slice_at * count, (self.slice_at + 1) * count):
            place = (2 * block + self.place.half) * width
            yield pl.ds(block * width, width), pl.ds(pl.multiple_of(place, 128), width)

    def rows_done(self, half, columns):
        start = pl.multiple_of(half * self.rows, 16)
        return self.done.at[self.layer, pl.ds(start, self.rows), columns]

    def start_swap(self):
        slot = self.sems(self.dims.bits + self.moves)
        if not self.dims.direct:
            remote(
                self.rows_done(1 - self.place.half, self.columns_here),
                self.swapped.at[self.layer, pl.ds(0, self.rows), self.columns_here],
                *slot,
                self.place.mate(),
            ).start()
            return
        for here, there in self.part_blocks():
            remote(
                self.rows_done(1 - self.place.half, here),
                self.swapped.at[self.layer, pl.ds(0, self.rows), there],
                *slot,
                self.place.mate(),
            ).start()
        for here, there in self.part_blocks():
            pltpu.make_async_copy(
                self.rows_done(self.place.half, here),
                self.swapped.at[self.layer, pl.ds(0, self.rows), there],
                self.own_sem.at[self.at],
            ).start()

    def swap_bytes(self):
        ref = self.done.at[self.layer, pl.ds(0, self.rows), self.columns_here]
        return remote(ref, ref, *self.sems(self.dims.bits + self.moves), self.place.mate())

    def finish_swap(self):
        self.swap_bytes().wait_recv()
        if self.dims.direct:
            ref = self.done.at[self.layer, pl.ds(0, self.rows), self.columns_here]
            pltpu.make_async_copy(ref, ref, self.own_sem.at[self.at]).wait()

    def advance(self):
        bits = self.dims.bits
        if self.stage == 0:
            self.start_turn(0)
        elif self.stage < bits:
            self.finish_turn(self.stage - 1)
            self.start_turn(self.stage)
        elif self.stage == bits:
            self.finish_turn(bits - 1)
            self.start_move(0)
        elif self.stage < bits + self.moves:
            self.finish_move(self.stage - bits - 1)
            self.start_move(self.stage - bits)
        elif self.stage == bits + self.moves:
            self.finish_move(self.moves - 1)
            if self.paired:
                self.start_swap()
        else:
            self.finish_swap()
        self.stage += 1

    def additions(self, turn):
        bits, half = self.dims.bits, self.dims.reps // 2
        if turn < bits:
            wholes = [
                (
                    self.block(self.terms, index, turn, False),
                    self.block(self.arrived[turn], index, turn, False),
                    self.block(self.terms, index, turn, False),
                )
                for index in range(self.count(turn))
            ]
        elif turn - bits < half:
            move = turn - bits
            result = self.own(0) if move < half - 1 else self.final(0)
            wholes = [(self.own(0), self.line(move, 0), result)]
        else:
            wholes = []
        step = min(self.piece, 256)
        return [
            tuple(ref.at[pl.ds(start, step)] for ref in refs)
            for refs in wholes
            for start in range(0, self.piece, step)
        ]

    def arrive(self, turn):
        bits = self.dims.bits
        if turn < bits:
            self.turn_bytes(turn).wait_recv()
        elif turn < bits + self.moves:
            self.move_bytes(turn - bits).wait_recv()
        else:
            self.finish_swap()

    def taking_part(self, turn):
        bits = self.dims.bits
        if not bits <= turn < bits + self.moves:
            return True
        receivers = self.roles(turn - bits)[1]
        return jnp.logical_or(self.place.rep == receivers[0], self.place.rep == receivers[1])

    def depart(self, turn):
        bits = self.dims.bits
        if turn < bits:
            self.start_turn(turn)
        elif turn < bits + self.moves:
            self.start_move(turn - bits)
        elif self.paired and turn == bits + self.moves:
            self.start_swap()

    def reach(self, stage):
        while self.stage < min(stage, self.stages):
            self.advance()

    def finish_sends(self):
        for turn in range(self.dims.bits):
            self.turn_bytes(turn).wait_send()
        for move in range(self.moves):
            senders, _ = self.roles(move)

            @pl.when(jnp.logical_or(self.place.rep == senders[0], self.place.rep == senders[1]))
            def _(move=move):
                self.move_bytes(move).wait_send()

        if self.paired:
            self.swap_bytes().wait_send()


def when(condition):
    if isinstance(condition, bool):
        return (lambda body: body()) if condition else (lambda body: None)
    return pl.when(condition)


def in_plane_columns(dims, layer, kind, columns, last):
    if dims.reps % 2 or last:
        return columns
    blocks = columns // 128
    share = IN_PLANE[kind] if layer else IN_PLANE_FIRST[kind]
    return max(blocks * share // 16, blocks - blocks // 2) * 128


def few(count, body):
    if count <= 8:
        for index in range(count):
            body(index)
    else:
        tiles(count, body)


def gelu_and_slope(pre):
    cdf = 0.5 * (1.0 + lax.erf(pre * (1.0 / math.sqrt(2.0))))
    slope = cdf + pre * jnp.exp(-0.5 * pre * pre) * (1.0 / math.sqrt(2.0 * math.pi))
    return pre * cdf, slope


def dot_last(left, right):
    return lax.dot_general(left, right, (((1,), (1,)), ((), ())), preferred_element_type=wide)


def dot_first(left, right):
    return lax.dot_general(left, right, (((0,), (0,)), ((), ())), preferred_element_type=wide)


def tiles(count, body):
    def step(j, carry):
        body(j)
        return carry

    lax.fori_loop(0, count, step, 0)


def layers_kernel(dims, *refs):
    refs = iter(refs)

    def take(count):
        return [next(refs) for _ in range(count)]

    x_ref, cotangent, seg_row = take(3)
    vector_refs = take(9) if dims.direct else None
    vector_ref = None if dims.direct else take(1)[0]
    src_qkv, src_out, src_up, src_down = take(4)
    output, tops, vectors, input_grad = take(4)
    vector_out, peak_out = take(2) if dims.direct else (None, None)
    terms = take(4)
    arrived = [take(4) for _ in range(dims.bits)]
    lines, done = take(4), take(4)
    swapped = take(2)
    w_qkv, w_out, w_up, w_down = take(4)
    both_hidden, qkv, attended, probs, norm1, both_first, act, slope, norm2, rstd = take(10)
    hidden, first, total, away, back, bias, both_grad, ring, add_mine, add_other = take(10)
    seg_here, seg_rows = take(2)
    if dims.direct:
        vector_all, small, vector_away, vector_back, line_back, vector_here = take(6)
    else:
        small = vector_ref
    gather_local, gather_send, gather_recv, mate_send, mate_recv = take(5)
    reduce_send, reduce_recv, own_sem, load_sem, store_sem, ring_sem, io_sem = take(7)
    if dims.direct:
        vector_send, vector_recv, pool_load, pool_store = take(4)
    place = Place(dims)
    tokens, width = dims.tokens, dims.width
    heads_row = 128 // dims.head_dim
    scale = 1.0 / math.sqrt(dims.head_dim)

    barrier = pltpu.get_barrier_semaphore()
    reps, shards = dims.reps, dims.shards

    def in_group(step):
        return place.rep, (place.me + step) % shards

    def greet(step):
        pl.semaphore_signal(barrier, 1, device_id=in_group(step), device_id_type=MESH)

    few(shards - 1, lambda index: greet(index + 1))
    for step in range(1, reps):
        line = (place.rep + step) % reps, place.me
        pl.semaphore_signal(barrier, 1, device_id=line, device_id_type=MESH)
    pl.semaphore_wait(barrier, shards + reps - 2)

    sources = (src_qkv, src_out, src_up, src_down)
    wholes = (w_qkv, w_out, w_up, w_down)
    gathers = [
        Gather(
            place,
            layer,
            kind,
            cut,
            sources[kind],
            wholes[kind],
            (gather_local, gather_send, gather_recv),
            layer == dims.layers - 1 and kind == 3 and cut == dims.cuts[kind] - 1,
        )
        for layer in range(dims.layers)
        for kind in range(4)
        for cut in range(dims.cuts[kind])
    ]

    exchanges = []

    def to_mate(src, dst):
        at = len(exchanges)
        copy = remote(src, dst, mate_send.at[at], mate_recv.at[at], place.mate())
        copy.start()
        exchanges.append(copy)
        return copy

    seg_here[...] = jnp.broadcast_to(seg_row[...].astype(wide), seg_here.shape)
    rows_copy = to_mate(seg_here, seg_rows)

    def vector_bytes(buffer, slot, count):
        ref = buffer.at[pl.ds(0, count)]
        return remote(ref, ref, vector_send.at[slot], vector_recv.at[slot], place.mate())

    if dims.direct:

        def send_vector(index):
            remote(
                vector_here,
                vector_all.at[place.me],
                vector_send.at[0],
                vector_recv.at[0],
                in_group(index + 1),
            ).start()

        at = 0
        for layer in range(dims.layers):
            for ref, length in zip(vector_refs, dims.lengths):
                values = ref[...].astype(wide)
                for block in range(length):
                    lanes = slice(block * dims.rows, (block + 1) * dims.rows)
                    vector_here[at : at + 1, :] = values[layer : layer + 1, lanes]
                    at += 1
        vector_all[place.me] = vector_here[...]
        few(shards - 1, send_vector)
    x_copy = pltpu.make_async_copy(x_ref, both_hidden.at[0, pl.ds(0, tokens)], io_sem.at[0])
    cotangent_copy = pltpu.make_async_copy(cotangent, both_grad.at[pl.ds(0, tokens)], io_sem.at[1])
    x_copy.start()
    cotangent_copy.start()
    x_copy.wait()
    hidden_copy = to_mate(both_hidden.at[0, pl.ds(0, tokens)], both_hidden.at[0, pl.ds(tokens, tokens)])
    for gather in gathers:
        gather.begin()
    turns = []

    def turn_on():
        now = len(turns)
        turns.append(now)
        for number, gather in reversed(list(enumerate(gathers))):
            gather.reach(max(now - number + 1, 1 if number <= now + LEAD else 0))

    def prepare(at):
        last = max(
            number
            for number, gather in enumerate(gathers)
            if gather.layer * 4 + gather.kind == at
        )
        while len(turns) < last + gathers[last].stages:
            turn_on()

    hidden[...] = both_hidden[0, pl.ds(0, tokens)].astype(wide)
    vectors[...] = jnp.zeros(vectors.shape, wide)
    tops[...] = jnp.full(tops.shape, neg_large, wide)
    rows_copy.wait_recv()
    for s, row_ref in enumerate((seg_here, seg_rows)):
        row = row_ref[0:1, :]
        column = jnp.broadcast_to(row, (128, tokens)).T[:, 0:1]
        bias[s] = jnp.where(column == row, 0.0, neg_large)

    if dims.direct:
        vector_bytes(vector_all, 0, shards - 1).wait_recv()
        starts = [sum(dims.lengths[:member]) for member in range(9)]
        small[...] = jnp.zeros(small.shape, wide)
        for layer in range(dims.layers):
            base = layer * sum(dims.lengths)

            def spread(row, member, shard, at, layer=layer, base=base):
                for block in range(dims.lengths[member]):
                    lanes = pl.ds(at + block * dims.rows, dims.rows)
                    source = base + starts[member] + block
                    small[layer, row : row + 1, lanes] = vector_all[shard, source : source + 1, :]

            for shard in range(shards):
                for row, member in ((1, 2), (3, 4), (4, 5), (5, 6), (6, 7), (7, 8)):
                    spread(row, member, shard, shard * dims.rows)
            for pair in range(dims.pairs):
                shard = 2 * pair + place.half
                spread(0, 0, shard, pair * dims.rows)
                spread(0, 1, shard, 2 * dims.third + pair * dims.rows)
                spread(2, 3, shard, pair * dims.rows * dims.lengths[3])

    chunk = 32 if tokens % 32 == 0 else tokens

    def layer_norm(residual, partial, other, bias_row, gain_row, shift_row, normed, rstd_out, results):
        def body(j):
            rows = pl.ds(pl.multiple_of(j * chunk, chunk), chunk)
            value = residual[rows] + partial[rows] + other[rows].astype(wide) + bias_row
            centred = value - jnp.mean(value, axis=-1, keepdims=True)
            scale_row = lax.rsqrt(jnp.mean(centred * centred, axis=-1, keepdims=True) + epsilon)
            normal = centred * scale_row
            normed[rows] = normal
            rstd_out[rows] = jnp.broadcast_to(scale_row, (chunk, 128))
            results(rows, normal * gain_row + shift_row)

        tiles(tokens // chunk, body)

    flying = [None, None]

    def project(left, product, at):
        slot = at % 2
        if flying[slot] is not None:
            flying[slot].wait_send()
            settled.append(flying[slot])

        def far(j):
            cols = pl.ds(pl.multiple_of(j * tile, tile), tile)
            away[slot, :, cols] = product(left[pl.ds(tokens, tokens)], cols).astype(low)

        def near(j):
            cols = pl.ds(pl.multiple_of(j * tile, tile), tile)
            total[:, cols] = product(left[pl.ds(0, tokens)], cols)

        tiles(width // tile, far)
        flying[slot] = to_mate(away.at[slot], back.at[at % (2 * dims.layers)])
        tiles(width // tile, near)
        return flying[slot]

    settled = []
    tile = min(512, width)
    for layer in range(dims.layers):
        prepare(4 * layer)
        hidden_copy.wait_recv()

        def qkv_tile(j, layer=layer):
            cols = pl.ds(pl.multiple_of(j * tile, tile), tile)
            value = jnp.dot(both_hidden[layer], w_qkv[layer, :, cols], preferred_element_type=wide)
            qkv[layer, :, cols] = (value + small[layer, 0:1, cols]).astype(low)

        tiles(dims.kinds[0][2] // tile, qkv_tile)
        lane_blocks = dims.third // 128

        def attend(j, layer=layer):
            s, block = j // lane_blocks, j % lane_blocks
            rows = pl.ds(pl.multiple_of(s * tokens, tokens), tokens)

            def lanes(which):
                start = pl.multiple_of(which * dims.third + block * 128, 128)
                return qkv[layer, rows, pl.ds(start, 128)]

            query, key_rows, value_rows = lanes(0), lanes(1), lanes(2)
            mask = bias[s]
            outs = []
            for e in range(heads_row):
                part = slice(e * dims.head_dim, (e + 1) * dims.head_dim)
                scores = dot_last(query[:, part], key_rows[:, part]) * scale + mask
                top = jnp.max(scores, axis=1, keepdims=True)
                expo = jnp.exp(scores - top)
                prob = (expo * (1.0 / jnp.sum(expo, axis=1, keepdims=True))).astype(low)
                head = block * heads_row + e
                probs[layer, s * (lane_blocks * heads_row) + head] = prob
                outs.append(jnp.dot(prob, value_rows[:, part], preferred_element_type=wide))
                peak = jnp.broadcast_to(jnp.max(top, axis=0, keepdims=True), (1, 128))
                tops[layer, pl.ds(head, 1)] = jnp.maximum(tops[layer, pl.ds(head, 1)], peak)
            attended[layer, rows, pl.ds(pl.multiple_of(block * 128, 128), 128)] = jnp.concatenate(
                outs, axis=1
            ).astype(low)

        turn_on()
        tiles(lane_blocks, attend)
        turn_on()
        tiles(lane_blocks, lambda j, attend=attend: attend(j + lane_blocks))

        prepare(4 * layer + 1)
        project(
            attended.at[layer],
            lambda left, cols, layer=layer: jnp.dot(
                left, w_out[layer, :, cols], preferred_element_type=wide
            ),
            2 * layer,
        ).wait_recv()

        def first_rows(rows, value, layer=layer):
            first[rows] = value
            both_first[layer, rows] = value.astype(low)

        layer_norm(
            hidden,
            total,
            back.at[2 * layer],
            small[layer, 1:2, :width],
            small[layer, 4:5, :width],
            small[layer, 5:6, :width],
            norm1.at[layer],
            rstd.at[layer, 0],
            first_rows,
        )
        first_copy = to_mate(
            both_first.at[layer, pl.ds(0, tokens)], both_first.at[layer, pl.ds(tokens, tokens)]
        )

        prepare(4 * layer + 2)
        first_copy.wait_recv()
        narrow = 256

        def up_tile(j, layer=layer):
            cols = pl.ds(pl.multiple_of(j * narrow, narrow), narrow)
            pre = jnp.dot(both_first[layer], w_up[layer, :, cols], preferred_element_type=wide)
            value, steep = gelu_and_slope(pre + small[layer, 2:3, cols])
            act[layer, :, cols] = value.astype(low)
            slope[layer, :, cols] = steep.astype(low)

        tiles(dims.kinds[2][2] // narrow, up_tile)

        prepare(4 * layer + 3)
        project(
            act.at[layer],
            lambda left, cols, layer=layer: jnp.dot(
                left, w_down[layer, :, cols], preferred_element_type=wide
            ),
            2 * layer + 1,
        ).wait_recv()
        last = layer == dims.layers - 1

        def second_rows(rows, value, layer=layer, last=last):
            if last:
                output[rows] = value.astype(low)
            else:
                hidden[rows] = value
                both_hidden[layer + 1, rows] = value.astype(low)

        layer_norm(
            first,
            total,
            back.at[2 * layer + 1],
            small[layer, 3:4, :width],
            small[layer, 6:7, :width],
            small[layer, 7:8, :width],
            norm2.at[layer],
            rstd.at[layer, 1],
            second_rows,
        )
        if not last:
            hidden_copy = to_mate(
                both_hidden.at[layer + 1, pl.ds(0, tokens)],
                both_hidden.at[layer + 1, pl.ds(tokens, tokens)],
            )
    for gather in gathers:
        gather.finish_sends()
    queue = [
        [
            Reduce(
                place,
                layer,
                kind,
                cut,
                part,
                terms[kind],
                [arrived[turn][kind] for turn in range(dims.bits)],
                lines[kind],
                done[kind],
                swapped[kind // 2],
                (reduce_send, reduce_recv, own_sem),
                (add_mine, add_other, load_sem, store_sem),
            )
            for part in range(2)
        ]
        for kinds in ((3, 2), (0,), (1,))
        for layer in reversed(range(dims.layers))
        for kind in kinds
        for cut in range(dims.cuts[kind])
    ]
    stages = max(item.stages for pair in queue for item in pair)

    pools = [
        (ref, row, column)
        for ref in (w_down, w_up, act, slope, w_qkv)
        for row in range(0, ref.shape[1] - 255, 256)
        for column in range(0, ref.shape[2] - 1023, 1024)
    ]

    def together(items):
        work, used = [], 0
        for item in items:
            turn = item.stage - 1
            pieces = []
            for own, other, result in item.additions(turn):
                rows, cols = own.shape
                pair = []
                for ref in (own, other):
                    pool, row, column = pools[used]
                    slot = pool.at[dims.layers - 1, pl.ds(row, rows), pl.ds(column, cols)]
                    pair.append((slot, pltpu.make_async_copy(ref, slot, pool_load.at[used])))
                    used += 1
                back_copy = pltpu.make_async_copy(pair[0][0], result, pool_store.at[used // 2 - 1])
                pieces.append((pair, back_copy))
            work.append((item, turn, pieces))
        for item, turn, pieces in work:

            @when(item.taking_part(turn))
            def _(item=item, turn=turn, pieces=pieces):
                item.arrive(turn)
                for pair, _ in pieces:
                    for _, copy in pair:
                        copy.start()

        for item, turn, pieces in work:

            @when(item.taking_part(turn))
            def _(pieces=pieces):
                for pair, back_copy in pieces:
                    for _, copy in pair:
                        copy.wait()
                    one, two = pair[0][0], pair[1][0]
                    one[...] = one[...] + two[...]
                    back_copy.start()

        for item, turn, pieces in work:

            @when(item.taking_part(turn))
            def _(pieces=pieces):
                for _, back_copy in pieces:
                    back_copy.wait()

            item.depart(turn + 1)
            item.stage += 1

    ready = set()

    def start_ready(last):
        for items in queue[: last + 1]:
            for item in items:
                if (item.layer, item.kind) in ready:
                    item.reach(1)

    def pump_together(step, ahead):
        start_ready(step + ahead)
        for group in GROUPS:
            together(
                [
                    item
                    for behind in group
                    if 0 <= step - behind < len(queue)
                    for item in queue[step - behind]
                    if 0 < item.stage < min(2 + behind, item.stages)
                ]
            )

    def pump(step, ahead=AHEAD):
        if dims.direct:
            pump_together(step, ahead)
            return
        start_ready(step + ahead)
        for behind in reversed(range(stages - 1)):
            at = step - behind
            if 0 <= at < len(queue):
                for item in queue[at]:
                    if item.stage:
                        item.reach(2 + behind)

    def weight_terms(layer, kind, left, right):
        ready.add((layer, kind))
        _, held, columns, _ = dims.kinds[kind]
        step = min(256, held)
        wide_cols = columns if columns <= ring.shape[2] else columns // 2
        across = columns // wide_cols
        count = (held // step) * across
        slots = ring.shape[0]

        def store(j):
            rows = pl.ds(pl.multiple_of((j // across) * step, step), step)
            cols = pl.ds(pl.multiple_of((j % across) * wide_cols, 128), wide_cols)
            return pltpu.make_async_copy(
                ring.at[j % slots, pl.ds(0, step), pl.ds(0, wide_cols)],
                terms[kind].at[layer, rows, cols],
                ring_sem.at[j % slots],
            )

        def body(j):
            @pl.when(j >= slots)
            def _():
                store(j - slots).wait()

            rows = pl.ds(pl.multiple_of((j // across) * step, step), step)
            cols = pl.ds(pl.multiple_of((j % across) * wide_cols, 128), wide_cols)
            ring[j % slots, pl.ds(0, step), pl.ds(0, wide_cols)] = dot_first(
                left[:, rows], right[:, cols]
            ).astype(low)
            store(j).start()

        tiles(count, body)
        for j in range(max(0, count - slots), count):
            store(j).wait()

    def count_up(layer, row, value, cols=None):
        cols = pl.ds(0, value.shape[1]) if cols is None else cols
        vectors[layer, pl.ds(row, 1), cols] += jnp.sum(value, axis=0, keepdims=True)

    def norm_grad(value, normed, scale_row, gain_row):
        grad = value * gain_row
        inner = jnp.mean(grad * normed, axis=-1, keepdims=True)
        return scale_row * (grad - jnp.mean(grad, axis=-1, keepdims=True) - normed * inner)

    def back_rows(j):
        return pl.ds(pl.multiple_of(j * chunk, chunk), chunk)

    grad_copy = None
    cotangent_copy.wait()
    pumped = 0
    for layer in reversed(range(dims.layers)):
        newest = layer == dims.layers - 1
        if grad_copy is not None:
            grad_copy.wait_send()
            settled.append(grad_copy)

        def second_back(j, layer=layer, newest=newest):
            rows = back_rows(j)
            value = both_grad[rows].astype(wide) if newest else hidden[rows]
            normed = norm2[layer, rows]
            count_up(layer, 7, value * normed)
            count_up(layer, 8, value)
            grad = norm_grad(value, normed, rstd[layer, 1, rows, 0:1], small[layer, 6:7, :width])
            first[rows] = grad
            rounded = grad.astype(low)
            both_grad[rows] = rounded
            count_up(layer, 4, rounded.astype(wide))

        tiles(tokens // chunk, second_back)
        grad_copy = to_mate(both_grad.at[pl.ds(0, tokens)], both_grad.at[pl.ds(tokens, tokens)])
        grad_copy.wait_recv()

        weight_terms(layer, 3, act.at[layer], both_grad)
        if newest:
            start_ready(1)
        else:
            pump(pumped)
            pumped += 1

        def down_back(j, layer=layer):
            cols = pl.ds(pl.multiple_of(j * narrow, narrow), narrow)
            grad = dot_last(both_grad[...], w_down[layer, cols, :])
            rounded = (grad * slope[layer, :, cols].astype(wide)).astype(low)
            slope[layer, :, cols] = rounded
            count_up(layer, 3, rounded.astype(wide), cols)

        tiles(dims.hidden // 2 // narrow, down_back)
        weight_terms(layer, 2, both_first.at[layer], slope.at[layer])
        if not newest:
            pump(pumped)
            pumped += 1
        exchange_at = 2 * (dims.layers - 1 - layer)
        project(
            slope.at[layer],
            lambda left, cols, layer=layer: dot_last(left, w_up[layer, cols, :]),
            2 * dims.layers + exchange_at,
        ).wait_recv()
        grad_copy.wait_send()
        settled.append(grad_copy)

        def first_back(j, layer=layer, exchange_at=exchange_at):
            rows = back_rows(j)
            value = first[rows] + total[rows] + back[exchange_at, rows].astype(wide)
            normed = norm1[layer, rows]
            count_up(layer, 5, value * normed)
            count_up(layer, 6, value)
            grad = norm_grad(value, normed, rstd[layer, 0, rows, 0:1], small[layer, 4:5, :width])
            first[rows] = grad
            rounded = grad.astype(low)
            both_grad[rows] = rounded
            count_up(layer, 2, rounded.astype(wide))

        tiles(tokens // chunk, first_back)
        grad_copy = to_mate(both_grad.at[pl.ds(0, tokens)], both_grad.at[pl.ds(tokens, tokens)])
        grad_copy.wait_recv()
        weight_terms(layer, 1, attended.at[layer], both_grad)

        out_tile = min(256, dims.third)

        def out_back(j, layer=layer):
            cols = pl.ds(pl.multiple_of(j * out_tile, out_tile), out_tile)
            attended[layer, :, cols] = dot_last(both_grad[...], w_out[layer, cols, :]).astype(low)

        tiles(dims.third // out_tile, out_back)
        pump(pumped)
        pumped += 1

        def attend_back(j, layer=layer):
            s, block = j // lane_blocks, j % lane_blocks
            rows = pl.ds(pl.multiple_of(s * tokens, tokens), tokens)
            lanes = pl.ds(pl.multiple_of(block * 128, 128), 128)

            def at(which):
                return pl.ds(pl.multiple_of(which * dims.third + block * 128, 128), 128)

            query, key_rows, value_rows = (qkv[layer, rows, at(which)] for which in range(3))
            grad_out = attended[layer, rows, lanes]
            grads = [[], [], []]
            for e in range(heads_row):
                part = slice(e * dims.head_dim, (e + 1) * dims.head_dim)
                prob = probs[layer, s * (lane_blocks * heads_row) + block * heads_row + e]
                grads[2].append(dot_first(prob, grad_out[:, part]))
                prob = prob.astype(wide)
                grad_prob = dot_last(grad_out[:, part], value_rows[:, part])
                inner = jnp.sum(prob * grad_prob, axis=1, keepdims=True)
                grad_score = (prob * (grad_prob - inner)).astype(low)
                grads[0].append(
                    jnp.dot(grad_score, key_rows[:, part], preferred_element_type=wide) * scale
                )
                grads[1].append(dot_first(grad_score, query[:, part]) * scale)
            for which, row in ((0, 0), (1, None), (2, 1)):
                rounded = jnp.concatenate(grads[which], axis=1).astype(low)
                qkv[layer, rows, at(which)] = rounded
                if row is not None:
                    count_up(layer, row, rounded.astype(wide), lanes)

        tiles(2 * lane_blocks, attend_back)
        pump(pumped)
        pumped += 1
        weight_terms(layer, 0, both_hidden.at[layer], qkv.at[layer])
        project(
            qkv.at[layer],
            lambda left, cols, layer=layer: dot_last(left, w_qkv[layer, cols, :]),
            2 * dims.layers + exchange_at + 1,
        ).wait_recv()

        def input_rows(j, exchange_at=exchange_at):
            rows = back_rows(j)
            hidden[rows] = first[rows] + total[rows] + back[exchange_at + 1, rows].astype(wide)

        tiles(tokens // chunk, input_rows)
        pump(pumped)
        pumped += 1

    grad_out_copy = pltpu.make_async_copy(hidden, input_grad, io_sem.at[0])
    grad_out_copy.start()

    if dims.direct:
        count = dims.vector_rows
        for shard in range(shards):
            for layer in range(dims.layers):
                at = layer * sum(dims.lengths)
                for member, length in enumerate(dims.lengths):
                    halved = member in (0, 1, 3)
                    for block in range(length):
                        first_lane = (shard // 2 if halved else shard) * length * dims.rows
                        lanes = pl.ds(first_lane + block * dims.rows, dims.rows)
                        value = vectors[layer, member : member + 1, lanes]
                        if halved:
                            value = jnp.where(place.half == shard % 2, value, 0.0)
                        vector_away[shard, at : at + 1, :] = value
                        at += 1
                heads = HEADS // 2
                vector_away[shard, pl.ds(count + layer * heads, heads)] = tops[layer]
        vector_back[place.me] = vector_away[place.me]

        def send_terms(index):
            target = in_group(index + 1)
            remote(
                vector_away.at[target[1]],
                vector_back.at[place.me],
                vector_send.at[1],
                vector_recv.at[1],
                target,
            ).start()

        few(shards - 1, send_terms)
    gathered = pumped + 1
    while pumped < len(queue) + stages:
        pump(pumped)
        pumped += 1
        if dims.direct and pumped == gathered:
            vector_bytes(vector_back, 1, shards - 1).wait_recv()
            total_rows = vector_back[0, pl.ds(0, count)]
            for shard in range(1, shards):
                total_rows = total_rows + vector_back[shard, pl.ds(0, count)]
            vector_out[...] = total_rows
            heads = dims.layers * HEADS // 2
            for half in range(2):
                peak = vector_back[half, pl.ds(count, heads)]
                for shard in range(2 + half, shards, 2):
                    peak = jnp.maximum(peak, vector_back[shard, pl.ds(count, heads)])
                peak_out[half] = peak
            line_back[place.rep, pl.ds(0, count)] = vector_out[...]
            for half in range(2):
                line_back[place.rep, pl.ds(count + half * heads, heads)] = peak_out[half]
            for step in range(1, reps):
                remote(
                    line_back.at[place.rep],
                    line_back.at[place.rep],
                    vector_send.at[2],
                    vector_recv.at[2],
                    ((place.rep + step) % reps, place.me),
                ).start()
    if dims.direct:
        vector_bytes(line_back, 2, reps - 1).wait_recv()
        total_rows = line_back[0, pl.ds(0, count)]
        for other in range(1, reps):
            total_rows = total_rows + line_back[other, pl.ds(0, count)]
        vector_out[...] = total_rows
        for half in range(2):
            peak = line_back[0, pl.ds(count + half * heads, heads)]
            for other in range(1, reps):
                peak = jnp.maximum(peak, line_back[other, pl.ds(count + half * heads, heads)])
            peak_out[half] = peak

    for copy in exchanges:
        if not any(copy is other for other in settled):
            copy.wait_send()
    if dims.direct:
        vector_bytes(vector_all, 0, shards - 1).wait_send()
        vector_bytes(vector_back, 1, shards - 1).wait_send()
        vector_bytes(line_back, 2, reps - 1).wait_send()
    for pair in queue:
        for item in pair:
            item.finish_sends()
    grad_out_copy.wait()


def run_layers(dims, x, cotangent, segments, vectors, weights):
    layers, tokens, width = dims.layers, dims.tokens, dims.width
    both = 2 * tokens

    def shape(dims_of, dtype):
        return jax.ShapeDtypeStruct(dims_of, dtype)

    held = [shape((layers, rows, columns), low) for _, rows, columns, _ in dims.kinds]
    pair_rows = [rows * (2 if paired else 1) for rows, _, _, paired in dims.kinds]
    columns = [kind[2] for kind in dims.kinds]
    heads = HEADS // 2
    summed = []
    if dims.direct:
        summed = [
            shape((dims.vector_rows, dims.rows), wide),
            shape((2, layers * heads, 128), wide),
        ]
    outs = (
        [
            shape((tokens, width), low),
            shape((layers, HEADS // 2, 128), wide),
            shape((layers, 16, dims.hidden // 2), wide),
            shape((tokens, width), wide),
        ]
        + summed
        + held * (1 + dims.bits)
        + [shape((layers, dims.reps // 2, r, c), low) for r, c in zip(pair_rows, columns)]
        + [shape((layers, r, c), low) for r, c in zip(pair_rows, columns)]
        + [
            shape((layers, dims.rows, columns[kind] * (2 if dims.direct else 1)), low)
            for kind in (0, 2)
        ]
    )
    vmem = pl.BlockSpec(memory_space=pltpu.VMEM)
    anywhere = pl.BlockSpec(memory_space=pl.ANY)
    dma = pltpu.SemaphoreType.DMA
    scratch = [pltpu.VMEM(item.shape, item.dtype) for item in held] + [
        pltpu.VMEM(*item)
        for item in (
            ((layers, both, width), low),
            ((layers, both, 3 * dims.third), low),
            ((layers, both, dims.third), low),
            ((layers, HEADS, tokens, tokens), low),
            ((layers, tokens, width), wide),
            ((layers, both, width), low),
            ((layers, both, dims.hidden // 2), low),
            ((layers, both, dims.hidden // 2), low),
            ((layers, tokens, width), wide),
            ((layers, 2, tokens, 128), wide),
            ((tokens, width), wide),
            ((tokens, width), wide),
            ((tokens, width), wide),
            ((2, tokens, width), low),
            ((2 * layers, tokens, width), low),
            ((2, tokens, tokens), wide),
            ((both, width), low),
            ((3, 256, 1024), low),
            ((2, 256, 1024), low),
            ((2, 256, 1024), low),
            ((8, tokens), wide),
            ((8, tokens), wide),
        )
    ]
    if dims.direct:
        rows = dims.vector_rows
        scratch += [
            pltpu.VMEM(item, wide)
            for item in (
                (dims.shards, rows, dims.rows),
                (layers, 8, dims.hidden // 2),
                (dims.shards, rows + layers * heads, dims.rows),
                (dims.shards, rows + layers * heads, dims.rows),
                (dims.reps, rows + 2 * layers * heads, dims.rows),
                (rows, dims.rows),
            )
        ]
    slots = 2 + 2 * dims.bits
    exchange_count = 2 + 8 * layers
    reduce_slots = dims.bits + dims.reps
    scratch = scratch + [
        dma((4 * layers * CUTS,)),
        dma((4 * layers * CUTS, slots)),
        dma((4 * layers * CUTS, slots)),
        dma((exchange_count,)),
        dma((exchange_count,)),
        dma((8 * layers * CUTS, reduce_slots)),
        dma((8 * layers * CUTS, reduce_slots)),
        dma((8 * layers * CUTS,)),
        dma((2, 2)),
        dma((2,)),
        dma((3,)),
        dma((2,)),
    ]
    if dims.direct:
        scratch += [dma((3,)), dma((3,)), dma((32,)), dma((16,))]
    return pl.pallas_call(
        functools.partial(layers_kernel, dims),
        out_shape=outs,
        in_specs=[anywhere] * 2 + [vmem] * (1 + len(vectors)) + [anywhere] * 4,
        out_specs=[vmem] * 3 + [anywhere] + [vmem] * len(summed) + [anywhere] * (len(outs) - 4 - len(summed)),
        scratch_shapes=scratch,
        compiler_params=pltpu.CompilerParams(
            collective_id=0, has_side_effects=True, vmem_limit_bytes=63 * 2**20 + 2**19
        ),
        name="layers",
    )(x, cotangent, segments, *vectors, *weights)


def own_rows(net, value):
    layers, rows, columns = value.shape
    split = value.reshape(layers, 2, rows // 2, columns)
    return lax.dynamic_index_in_dim(split, net.core, 1, keepdims=False)


def gathered_vectors(net, dims, packed):
    lengths = dims.lengths
    packed = net.in_order(packed, net.over_core(packed), net.core)
    packed = net.rows_in_order(net.gather_chips(packed, list(range(net.bits))))

    def whole(layer, member):
        start = sum(lengths[:member])
        return packed[:, layer, start : start + lengths[member]].astype(wide)

    def of_core(layer, member):
        split = whole(layer, member).reshape(net.high, 2, -1)
        return lax.dynamic_index_in_dim(split, net.core, 1, keepdims=False).reshape(-1)

    def wide_row(row):
        return jnp.pad(row, (0, dims.hidden // 2 - row.shape[0]))

    def rows(layer):
        bias_q = of_core(layer, 0)
        bias_qkv = jnp.concatenate([bias_q, jnp.zeros_like(bias_q), of_core(layer, 1)])
        singles = [whole(layer, member).reshape(-1) for member in (2, 4, 5, 6, 7, 8)]
        return [bias_qkv, singles[0], of_core(layer, 3)] + singles[1:]

    return jnp.stack(
        [jnp.stack([wide_row(row) for row in rows(layer)]) for layer in range(dims.layers)]
    )


def summed_vectors(net, dims, vectors, tops):
    layers, lengths, rows = dims.layers, dims.lengths, dims.rows
    half_width, half_hidden = dims.third, dims.hidden // 2
    here = (half_width, half_width, dims.width, half_hidden) + (dims.width,) * 5

    def placed(value, member):
        if member in (0, 1, 3):
            value = value.reshape(net.high, 1, net.step, lengths[member], rows)
            zero = jnp.zeros_like(value)
            first = net.core == 0
            return jnp.concatenate(
                [jnp.where(first, value, zero), jnp.where(first, zero, value)], axis=1
            )
        return value.reshape(net.high, 2, net.step, lengths[member], rows)

    terms = jnp.stack(
        [
            jnp.concatenate(
                [placed(vectors[layer, row, :size], row) for row, size in enumerate(here)], axis=3
            )
            for layer in range(layers)
        ],
        axis=3,
    )
    theirs = lax.dynamic_index_in_dim(terms, 1 - net.core, 1, keepdims=False)
    ours = lax.dynamic_index_in_dim(terms, net.core, 1, keepdims=False)
    terms = ours + net.over_core(theirs)
    terms = terms.reshape((net.pairs,) + terms.shape[2:])
    terms = net.sum_reps(net.scatter_chips(terms, list(range(net.bits))))

    local = tops[:, :, 0]
    local = net.in_order(local, net.over_core(local), net.core)
    local = local.reshape(2, layers, net.high, -1).transpose(1, 2, 0, 3).reshape(layers, HEADS)
    for bit in range(net.bits):
        local = jnp.maximum(local, net.over_bit(local, bit))
    step = 1
    while step < net.reps:
        swap = [(i, i ^ step) for i in range(net.reps)]
        local = jnp.maximum(local, lax.ppermute(local, "rep", swap))
        step *= 2
    return terms, local


def shards(
    inputs,
    cotangent,
    segments,
    w_qkv,
    w_out,
    w_up,
    w_down,
    bias_query,
    bias_value,
    bias_out,
    bias_up,
    bias_down,
    norm1_gain,
    norm1_bias,
    norm2_gain,
    norm2_bias,
    tau,
    *,
    shard_count,
    rep_count,
):
    layer_count = w_qkv.shape[0]
    width = w_qkv.shape[2] // 3
    rows_here = bias_query.shape[1]
    head_dim = width // HEADS
    net = Net(shard_count, rep_count, max(1, head_dim // rows_here))

    vectors = (
        bias_query,
        bias_value,
        bias_out,
        bias_up,
        bias_down,
        norm1_gain,
        norm1_bias,
        norm2_gain,
        norm2_bias,
    )
    lengths = [vector.shape[1] // rows_here for vector in vectors]
    tokens = inputs.shape[0]
    dims = Dims(shard_count, rep_count, net.step, layer_count, tokens, width, w_up.shape[2])
    if dims.direct:
        vector_in = vectors
        matrices = (w_qkv, w_out, w_up, w_down)
    else:
        packed = jnp.concatenate(
            [vector.reshape(layer_count, -1, rows_here) for vector in vectors], axis=1
        )
        vector_in = (gathered_vectors(net, dims, packed),)
        matrices = (by_half(w_qkv, net, 3), w_out, by_half(w_up, net, 1), w_down)
    results = run_layers(dims, inputs, cotangent, segments, vector_in, matrices)
    output, tops, vector_terms, input_grad = results[:4]
    done, swapped = results[-6:-2], results[-2:]

    if dims.direct:
        vector_grads, peak = results[4:6]
        vector_grads = vector_grads.reshape(layer_count, -1, rows_here)
        peak = peak[:, :, 0].reshape(2, layer_count, net.high, -1)
        peak = peak.transpose(1, 2, 0, 3).reshape(layer_count, HEADS)
        full = swapped[0], done[1], swapped[1], done[3]
    else:
        vector_grads, peak = summed_vectors(net, dims, vector_terms, tops)
        paired = [whole_columns(own_rows(net, done[k]), swapped[k // 2], net, 3 - k) for k in (0, 2)]
        full = paired[0], done[1], paired[1], done[3]
    large = tuple(value.astype(wide) for value in full)
    ends = [sum(lengths[: member + 1]) for member in range(len(lengths))]
    vector_grads = [
        vector_grads[:, end - length : end].reshape(layer_count, -1)
        for end, length in zip(ends, lengths)
    ]
    factor = jnp.sqrt(tau / jnp.maximum(peak, tau))
    column_scale = jnp.repeat(factor, head_dim, axis=1)
    both_scale = jnp.concatenate([column_scale, column_scale], axis=1)
    clipped_qk = w_qkv[:, :, : 2 * width].astype(wide) * both_scale[:, None, :]
    start = lax.axis_index("shard") * rows_here
    scale_here = lax.dynamic_slice_in_dim(column_scale, start, rows_here, 1)
    clipped_bias_query = bias_query.astype(wide) * scale_here
    return (output, input_grad) + large + tuple(vector_grads) + (clipped_qk, clipped_bias_query)


def solution(mesh):
    tokens = P(("rep", "shard"), None)
    matrix = P(None, "shard", None)
    vector = P(None, "shard")
    in_specs = (tokens, tokens, tokens) + (matrix,) * 4 + (vector,) * 9 + (P(),)
    out_specs = (tokens, tokens) + (matrix,) * 4 + (vector,) * 9 + (matrix, vector)

    def local(*arrays):
        return shards(*arrays, shard_count=mesh.shape["shard"], rep_count=mesh.shape["rep"])

    return jax.shard_map(local, mesh=mesh, in_specs=in_specs, out_specs=out_specs, check_vma=False)
```
